32 devices in a mesh: dp: 8 (over y, x, core), fsdp: 4 (over z).
Axes of the slice: x: 2, y: 2, z: 4, core: 2. Of those that a mesh axis runs over, the one named last changes fastest.
Arguments:
- tokens: bfloat16 [12288, 2048], P(('dp', 'fsdp')), may hold values from -6 to 6
- cotangent: bfloat16 [12288, 2048], P(('dp', 'fsdp')), may hold values from -6 to 6
- seq_table: int32 [32, 4], P(('dp', 'fsdp')), may hold values from 0 to 384, as said below
- w_qkv: float32 [2048, 2560], P(('dp', 'fsdp')), may hold values from -0.125 to 0.125
- m_qkv: float32 [2048, 2560], P(('dp', 'fsdp')), may hold values from -64 to 64
- v_qkv: float32 [2048, 2560], P(('dp', 'fsdp')), may hold values from 12.288 to 49.152
- w_out: float32 [2048, 2048], P(('dp', 'fsdp')), may hold values from -0.5 to 0.5
- m_out: float32 [2048, 2048], P(('dp', 'fsdp')), may hold values from -20 to 20
- v_out: float32 [2048, 2048], P(('dp', 'fsdp')), may hold values from 1.10592 to 4.42368
- w_gate_up: float32 [2048, 11264], P(('dp', 'fsdp')), may hold values from -0.125 to 0.125
- m_gate_up: float32 [2048, 11264], P(('dp', 'fsdp')), may hold values from -20 to 20
- v_gate_up: float32 [2048, 11264], P(('dp', 'fsdp')), may hold values from 1.10592 to 4.42368
- w_down: float32 [5632, 2048], P(('dp', 'fsdp')), may hold values from -0.078125 to 0.078125
- m_down: float32 [5632, 2048], P(('dp', 'fsdp')), may hold values from -32 to 32
- v_down: float32 [5632, 2048], P(('dp', 'fsdp')), may hold values from 3.072 to 12.288
- norm_gains: float32 [2, 2048], P(None, ('dp', 'fsdp')), may hold values from 0.5 to 1.5
- m_gains: float32 [2, 2048], P(None, ('dp', 'fsdp')), may hold values from -64 to 64
- v_gains: float32 [2, 2048], P(None, ('dp', 'fsdp')), may hold values from 12.288 to 49.152
Outputs:
- output: bfloat16 [12288, 2048], P(('dp', 'fsdp'))
- input_grad: bfloat16 [12288, 2048], P(('dp', 'fsdp'))
- m_qkv_new: float32 [2048, 2560], P(('dp', 'fsdp'))
- v_qkv_new: float32 [2048, 2560], P(('dp', 'fsdp'))
- w_qkv_new: float32 [2048, 2560], P(('dp', 'fsdp'))
- m_out_new: float32 [2048, 2048], P(('dp', 'fsdp'))
- v_out_new: float32 [2048, 2048], P(('dp', 'fsdp'))
- w_out_new: float32 [2048, 2048], P(('dp', 'fsdp'))
- m_gate_up_new: float32 [2048, 11264], P(('dp', 'fsdp'))
- v_gate_up_new: float32 [2048, 11264], P(('dp', 'fsdp'))
- w_gate_up_new: float32 [2048, 11264], P(('dp', 'fsdp'))
- m_down_new: float32 [5632, 2048], P(('dp', 'fsdp'))
- v_down_new: float32 [5632, 2048], P(('dp', 'fsdp'))
- w_down_new: float32 [5632, 2048], P(('dp', 'fsdp'))
- m_gains_new: float32 [2, 2048], P(None, ('dp', 'fsdp'))
- v_gains_new: float32 [2, 2048], P(None, ('dp', 'fsdp'))
- gains_new: float32 [2, 2048], P(None, ('dp', 'fsdp'))
The draws below stay inside these ranges and needn't reach their ends.
Inputs may be any that keep to these rules, and one draw needn't show every extreme that they name: `seq_table`: each row's lengths sum to between 192 and 384; some row holds one sequence of 384 rows and zeros elsewhere.
All inputs are finite; a program needn't handle non-finite values.
Results may differ from the reference program's by a relative error of at most 0.014.
The reference program's roundings to bfloat16 on the way count: a program that leaves them out, or rounds other values in their place, can miss the bound.
Values may be sent and summed in bfloat16 or wider, within the bound.
No kernel may reach another device: no remote copies, remote signals or barrier semaphores. Data moves between devices by JAX's collectives and lax.ppermute only.
A program may use at most 384 MiB of HBM per device.

```python
import math
import jax
import jax.numpy as jnp
from jax import lax

D = 2048
FF = 5632
HEADS = 32
KV_HEADS = 4
HEAD_DIM = 64
CAP = 384
SLOTS = 4
STEP = 10
HOLDERS = 32
TOTAL = 12288
QKV_W = 2560


def draw_seq_table(key, part):
    key = jax.random.fold_in(key, 7)
    keys = jax.random.split(key, 4)
    shares = jax.random.randint(keys[0], (HOLDERS, SLOTS), 1, 5)
    active = jax.random.randint(keys[1], (HOLDERS, 1), 1, SLOTS + 1)
    used = (jnp.arange(SLOTS, dtype=jnp.int32)[None, :] < active).astype(jnp.int32)
    totals = jax.random.randint(keys[2], (HOLDERS, 1), CAP // 2, CAP + 1)
    weighted = shares * used
    lengths = totals * weighted // jnp.sum(weighted, axis=1, keepdims=True)
    lengths = lengths.at[:, 0].add(totals[:, 0] - jnp.sum(lengths, axis=1))
    chosen = jax.random.randint(keys[3], (), 0, HOLDERS)
    single = jnp.zeros((SLOTS,), jnp.int32).at[0].set(CAP)
    lengths = jnp.where((jnp.arange(HOLDERS, dtype=jnp.int32) == chosen)[:, None], single[None, :], lengths)
    return lengths.astype(jnp.int32)


def spiked(drawn, rng, source, target, parts, factor):
    def block_of(axis_at):
        return (jnp.arange(drawn.shape[axis_at]) // (drawn.shape[axis_at] // parts)).reshape((-1,) + (1,) * (drawn.ndim - 1 - axis_at))

    first = jax.random.permutation(rng, parts)[block_of(target)]
    second = (block_of(target) + parts // 2) % parts
    return jnp.where((block_of(source) == first) | (block_of(source) == second), factor * drawn, drawn)


def block_levels(key, shape, cuts, low, largest):
    gain, own = 1.0, jax.random.fold_in(key, 6)
    for dim, shards_of in cuts:
        heights = jnp.exp(jax.random.uniform(jax.random.fold_in(own, dim), (shards_of,), jnp.float32, low / len(cuts), largest / len(cuts)))
        gain = gain * jnp.repeat(heights, shape[dim] // shards_of).reshape([-1 if axis == dim else 1 for axis in range(len(shape))])
    return gain


def bell_draw(stream_key, dims, deviation, most, cuts=(), held_as=jnp.bfloat16):
    drawn = jax.random.normal(stream_key, dims, jnp.float32) * deviation
    if len(cuts) > 0:
        drawn = block_levels(stream_key, dims, cuts, -0.22, 0.18) * drawn
    return jnp.clip(drawn, min=-most, max=most).astype(held_as)


def bell_draw_with(key, shape, deviation, most, cuts, heavy, kind=jnp.bfloat16):
    array = deviation * jax.random.normal(key, shape, jnp.float32)
    if cuts:
        array = array * block_levels(key, shape, cuts, -0.22, 0.18)
    return jnp.clip(spiked(array, jax.random.fold_in(key, 3), *heavy), -most, most).astype(kind)


def setup_inputs(seed: int = 0) -> dict:
    splits = jax.random.split(jax.random.key(seed), 19)
    tokens = bell_draw_with(splits[0], (TOTAL, D), 1.0, 6.0, ((0, 32),), (0, 1, 32, 2.75))
    cotangent = bell_draw(splits[1], (TOTAL, D), 1.0, 6.0, ((0, 32),))
    seq_table = draw_seq_table(jax.random.fold_in(splits[18], 71), 0)
    w_qkv = bell_draw(splits[3], (D, QKV_W), D ** -0.5, 0.125, ((0, 32),), jnp.float32)
    m_qkv = bell_draw(splits[4], (D, QKV_W), (0.11 * (CAP * HOLDERS) ** 0.5), 64.0, ((0, 32),), jnp.float32)
    v_qkv = jnp.clip(jnp.exp(math.log(49.152) - 1.3862944 * jax.random.uniform(splits[5], (D, QKV_W), jnp.float32) ** block_levels(splits[5], (D, QKV_W), ((0, 32),), -0.2, 0.2)), 12.288, 49.152)
    w_out = bell_draw(splits[6], (D, D), (D // 16) ** -0.5, 0.5, ((0, 32),), jnp.float32)
    m_out = bell_draw(splits[7], (D, D), (0.033 * (CAP * HOLDERS) ** 0.5), 20.0, ((0, 32),), jnp.float32)
    v_out = jnp.clip(jnp.exp(math.log(4.42368) - 1.3862944 * jax.random.uniform(splits[8], (D, D), jnp.float32) ** block_levels(splits[8], (D, D), ((0, 32),), -0.2, 0.2)), 1.10592, 4.42368)
    w_gate_up = bell_draw(splits[9], (D, 2 * FF), D ** -0.5, 0.125, ((0, 32),), jnp.float32)
    m_gate_up = bell_draw(splits[10], (D, 2 * FF), (0.033 * (CAP * HOLDERS) ** 0.5), 20.0, ((0, 32),), jnp.float32)
    v_gate_up = jnp.clip(jnp.exp(math.log(4.42368) - 1.3862944 * jax.random.uniform(splits[11], (D, 2 * FF), jnp.float32) ** block_levels(splits[11], (D, 2 * FF), ((0, 32),), -0.2, 0.2)), 1.10592, 4.42368)
    w_down = bell_draw(splits[12], (FF, D), FF ** -0.5, 0.078125, ((0, 32),), jnp.float32)
    m_down = bell_draw(splits[13], (FF, D), (0.055 * (CAP * HOLDERS) ** 0.5), 32.0, ((0, 32),), jnp.float32)
    v_down = jnp.clip(jnp.exp(math.log(12.288) - 1.3862944 * jax.random.uniform(splits[14], (FF, D), jnp.float32) ** block_levels(splits[14], (FF, D), ((0, 32),), -0.2, 0.2)), 3.072, 12.288)
    norm_gains = jnp.clip(1.0 + 0.1 * jax.random.normal(splits[15], (2, D), jnp.float32), 0.5, 1.5)
    m_gains = bell_draw(splits[16], (2, D), (0.11 * (CAP * HOLDERS) ** 0.5), 64.0, ((1, 32),), jnp.float32)
    v_gains = jnp.clip(jnp.exp(math.log(49.152) - 1.3862944 * jax.random.uniform(splits[17], (2, D), jnp.float32) ** block_levels(splits[17], (2, D), ((1, 32),), -0.2, 0.2)), 12.288, 49.152)
    return dict(tokens=tokens, cotangent=cotangent, seq_table=seq_table, w_qkv=w_qkv, m_qkv=m_qkv, v_qkv=v_qkv, w_out=w_out, m_out=m_out, v_out=v_out, w_gate_up=w_gate_up, m_gate_up=m_gate_up, v_gate_up=v_gate_up, w_down=w_down, m_down=m_down, v_down=v_down, norm_gains=norm_gains, m_gains=m_gains, v_gains=v_gains)


EPS_NORM = 1e-05
BETA_ONE = 0.9
BETA_TWO = 0.999
EPS_ADAM = 1e-08
RATE_MATRIX = 0.02
RATE_GAIN = 0.2
DECAY_MATRIX = 0.1
THETA = 10000.0
HIGHEST_PRECISION = lax.Precision.HIGHEST

@jax.custom_vjp
def low(v):
    return lax.optimization_barrier(v.astype(jnp.bfloat16)).astype(jnp.float32)

@jax.custom_vjp
def low_back(v):
    return v

def low_keep(v):
    return (low(v), None)

def low_pass(kept, grad):
    return (grad,)

def back_keep(v):
    return (v, None)

def back_low(kept, grad):
    return (low(grad),)
low.defvjp(low_keep, low_pass)
low_back.defvjp(back_keep, back_low)

def layout(lengths, count):
    seq_ends = jnp.cumsum(lengths).astype(jnp.int32)
    row_ids = jnp.arange(count, dtype=jnp.int32)
    passed = row_ids[:, None] >= seq_ends[None, :]
    segment = lax.optimization_barrier(jnp.sum(passed.astype(jnp.int32), axis=1))
    start = lax.optimization_barrier(jnp.max(jnp.where(passed, seq_ends[None, :], 0), axis=1))
    return (segment, row_ids - start, row_ids < seq_ends[-1])

def angles(position):
    frequency = THETA ** (-(jnp.arange(HEAD_DIM // 2, dtype=jnp.float32) * 2.0 / HEAD_DIM))
    phases = position.astype(jnp.float32)[:, None] * frequency[None, :]
    return (jnp.cos(phases)[:, None, :], jnp.sin(phases)[:, None, :])

def rotary(vectors, cosine, sine_part):
    half_dim = HEAD_DIM // 2
    lower_half = vectors[..., :half_dim]
    upper_half = vectors[..., half_dim:]
    return jnp.concatenate([lower_half * cosine - upper_half * sine_part, upper_half * cosine + lower_half * sine_part], axis=-1)

def rms_scale(values, gain_row):
    return values * lax.rsqrt(lax.optimization_barrier(jnp.mean(values * values, axis=-1, keepdims=True)) + EPS_NORM) * gain_row

def block(inputs, segment, position, w_qkv, w_out, w_gate_up, w_down, gains):
    kv_width = KV_HEADS * HEAD_DIM
    group_size = HEADS // KV_HEADS
    normed_one = low(rms_scale(inputs, gains[0]))
    projected = low_back(jnp.dot(normed_one, w_qkv, precision=HIGHEST_PRECISION))
    cosine, sine_part = angles(position)
    queries = low(rotary(projected[:, :D].reshape(CAP, HEADS, HEAD_DIM), cosine, sine_part))
    key_rows = low(rotary(projected[:, D:D + kv_width].reshape(CAP, KV_HEADS, HEAD_DIM), cosine, sine_part))
    value_rows = low(projected[:, D + kv_width:].reshape(CAP, KV_HEADS, HEAD_DIM))
    queries = queries.reshape(CAP, KV_HEADS, group_size, HEAD_DIM)
    scores = jnp.einsum('qhgd,khd->hgqk', queries, key_rows, precision=HIGHEST_PRECISION) * HEAD_DIM ** (-0.5)
    scores = low_back(scores)
    row_ids = jnp.arange(CAP)
    allowed = (segment[:, None] == segment[None, :]) & (row_ids[None, :] <= row_ids[:, None])
    scores = jnp.where(allowed, scores, -1e+30)
    attention = low(jax.nn.softmax(scores, axis=-1))
    attended = jnp.einsum('hgqk,khd->qhgd', attention, value_rows, precision=HIGHEST_PRECISION).reshape(CAP, D)
    attended = low(low_back(attended))
    middle = inputs + low_back(jnp.dot(attended, w_out, precision=HIGHEST_PRECISION))
    normed_two = low(rms_scale(middle, gains[1]))
    gate_up = low_back(jnp.dot(normed_two, w_gate_up, precision=HIGHEST_PRECISION))
    hidden = low(jax.nn.silu(gate_up[:, :FF]) * gate_up[:, FF:])
    return middle + low_back(jnp.dot(hidden, w_down, precision=HIGHEST_PRECISION))

def adam_step(weight, first_moment, second_moment, gradient, step_rate, weight_decay):
    first_new = BETA_ONE * first_moment + (1.0 - BETA_ONE) * gradient
    second_new = BETA_TWO * second_moment + (1.0 - BETA_TWO) * gradient * gradient
    first_hat = first_new / (1.0 - BETA_ONE ** STEP)
    second_hat = second_new / (1.0 - BETA_TWO ** STEP)
    updated = weight - step_rate * (first_hat / (jnp.sqrt(second_hat) + EPS_ADAM) + weight_decay * weight)
    return (first_new, second_new, updated)

def reference(tokens, cotangent, seq_table, w_qkv, m_qkv, v_qkv, w_out, m_out, v_out, w_gate_up, m_gate_up, v_gate_up, w_down, m_down, v_down, norm_gains, m_gains, v_gains):
    blocks = seq_table.shape[0]
    segment, position, live_rows = jax.vmap(lambda row: layout(row, CAP))(seq_table)
    inputs = tokens.astype(jnp.float32).reshape(blocks, CAP, D)
    back_rows = (cotangent.astype(jnp.float32) * live_rows.reshape(-1)[:, None].astype(jnp.float32)).reshape(blocks, CAP, D)
    masters = (w_qkv, w_out, w_gate_up, w_down, norm_gains)

    def forward(inputs, *weights):
        rounded = [low(weight) for weight in weights]
        one_block = jax.checkpoint(lambda item: block(item[0], item[1], item[2], *rounded))
        return lax.map(one_block, (inputs, segment, position))
    result, pullback = jax.vjp(forward, inputs, *masters)
    gradients = pullback(back_rows)
    output = result.reshape(-1, D).astype(jnp.bfloat16)
    input_grad = gradients[0].reshape(-1, D).astype(jnp.bfloat16)
    qkv_state = adam_step(w_qkv, m_qkv, v_qkv, gradients[1], RATE_MATRIX, DECAY_MATRIX)
    out_state = adam_step(w_out, m_out, v_out, gradients[2], RATE_MATRIX, DECAY_MATRIX)
    ffn_state = adam_step(w_gate_up, m_gate_up, v_gate_up, gradients[3], RATE_MATRIX, DECAY_MATRIX)
    down_state = adam_step(w_down, m_down, v_down, gradients[4], RATE_MATRIX, DECAY_MATRIX)
    gain_state = adam_step(norm_gains, m_gains, v_gains, gradients[5], RATE_GAIN, 0.0)
    return (output, input_grad, qkv_state[0], qkv_state[1], qkv_state[2], out_state[0], out_state[1], out_state[2], ffn_state[0], ffn_state[1], ffn_state[2], down_state[0], down_state[1], down_state[2], gain_state[0], gain_state[1], gain_state[2])
```

```python
import jax
import jax.numpy as jnp
from jax import lax
from jax.experimental import pallas as pl
from jax.experimental.pallas import tpu as pltpu
from jax.sharding import PartitionSpec as P

D = 2048
FF = 5632
HEADS = 32
KV_HEADS = 4
HEAD_DIM = 64
STEP = 10
QKV_W = (HEADS + 2 * KV_HEADS) * HEAD_DIM
PAD = 128


EPS_NORM = 1e-05
BETA_ONE = 0.9
BETA_TWO = 0.999
EPS_ADAM = 1e-08
RATE_MATRIX = 0.02
RATE_GAIN = 0.2
DECAY_MATRIX = 0.1
THETA = 10000.0

BF16 = jnp.bfloat16
F32 = jnp.float32


def layout(lengths, count):
    seq_ends = jnp.cumsum(lengths)
    row_ids = jnp.arange(count, dtype=jnp.int32)
    passed = row_ids[:, None] >= seq_ends[None, :]
    segment = jnp.sum(passed.astype(jnp.int32), axis=1)
    start = jnp.max(jnp.where(passed, seq_ends[None, :], 0), axis=1)
    return (segment, row_ids - start, row_ids < seq_ends[-1])


def adam_step(weight, first_moment, second_moment, gradient, step_rate, weight_decay):
    first_new = BETA_ONE * first_moment + (1.0 - BETA_ONE) * gradient
    second_new = BETA_TWO * second_moment + (1.0 - BETA_TWO) * gradient * gradient
    first_hat = first_new / (1.0 - BETA_ONE**STEP)
    second_hat = second_new / (1.0 - BETA_TWO**STEP)
    updated = weight - step_rate * (
        first_hat / (jnp.sqrt(second_hat) + EPS_ADAM) + weight_decay * weight
    )
    return (first_new, second_new, updated)


VMEM = pltpu.VMEM
ANY = pl.BlockSpec(memory_space=pl.ANY)
WHOLE = pl.BlockSpec(memory_space=pltpu.VMEM)
SCALAR = pl.BlockSpec(memory_space=pltpu.SMEM)
DMA = pltpu.SemaphoreType.DMA


def run(kernel, name, us, args, in_specs, out_shape, out_specs, scratch=(), after=(), aliases=None, prefetch=0, grid=None):
    count, ordered = len(args), len(after)

    def body(*refs):
        kernel(*refs[:count], *refs[count + ordered :])

    specs = dict(
        in_specs=list(in_specs) + [ANY] * ordered,
        out_specs=out_specs,
        scratch_shapes=list(scratch),
    )
    if grid and not prefetch:
        specs["grid"] = grid
    if prefetch:
        specs = dict(grid_spec=pltpu.PrefetchScalarGridSpec(num_scalar_prefetch=prefetch, grid=grid, **specs))
    return pl.pallas_call(
        body,
        out_shape=out_shape,
        input_output_aliases=aliases or {},
        compiler_params=pltpu.CompilerParams(vmem_limit_bytes=48 << 20),
        cost_estimate=pl.CostEstimate(flops=int(us * COST), bytes_accessed=int(us * 1.0e5), transcendentals=0),
        name=name,
        **specs,
    )(*args, *after)


COST = 0.25e9


def low_like(rows, cols):
    return jax.ShapeDtypeStruct((rows, cols), BF16)


def wide_like(rows, cols):
    return jax.ShapeDtypeStruct((rows, cols), F32)


def behind(x, *deps):
    return run(
        lambda x_ref, o_ref: None,
        "behind",
        0.1,
        (x,),
        [ANY],
        jax.ShapeDtypeStruct(x.shape, x.dtype),
        ANY,
        after=deps,
        aliases={0: 0},
    )


def lowered(x, *deps):
    def kernel(x_ref, o_ref):
        o_ref[...] = x_ref[...].astype(BF16)

    return run(kernel, "lowered", 1, (x,), [WHOLE], low_like(*x.shape), WHOLE, after=deps)


def half_of(x, which, *deps):
    rows = x.shape[0] // 2

    def kernel(x_ref, o_ref, sem):
        copy = pltpu.make_async_copy(x_ref.at[pl.ds(which * rows, rows), :], o_ref, sem)
        copy.start()
        copy.wait()

    return run(kernel, "half_of", 1, (x,), [ANY], low_like(rows, x.shape[1]), ANY, [DMA], deps)


def joined(low, high, *deps):
    rows = low.shape[0]

    def kernel(low_ref, high_ref, o_ref, sems):
        copies = [
            pltpu.make_async_copy(ref, o_ref.at[pl.ds(i * rows, rows), :], sems.at[i])
            for i, ref in enumerate((low_ref, high_ref))
        ]
        for copy in copies:
            copy.start()
        for copy in copies:
            copy.wait()

    return run(kernel, "joined", 1, (low, high), [ANY] * 2, low_like(2 * rows, low.shape[1]), ANY, [DMA((2,))], deps)


def tiles(width, step=256):
    return [(at, min(step, width - at)) for at in range(0, width, step)]


NT = (((1,), (1,)), ((), ()))
TN = (((0,), (0,)), ((), ()))


def dot(a, b, dims=(((1,), (0,)), ((), ()))):
    return lax.dot_general(a, b, dims, preferred_element_type=F32)


def fetch(block_refs, held, sems, width):
    copies = [
        pltpu.make_async_copy(ref.at[:, pl.ds(0, width)], held.at[k], sems.at[k]) for k, ref in enumerate(block_refs)
    ]
    for copy in copies:
        copy.start()
    return copies


def row_scale(values):
    return lax.rsqrt(jnp.mean(values * values, axis=-1, keepdims=True) + EPS_NORM)


def project(dp, tokens, blocks):
    rows, model = tokens.shape
    depth, cols = blocks[0].shape
    count = len(blocks)
    wide = cols - 128

    def kernel(dp_ref, x_ref, *refs):
        block_refs, (p_ref, a_ref, g_ref, held, sems) = refs[:count], refs[count:]
        copies = fetch(block_refs, held, sems, cols)
        scale = row_scale(x_ref[...].astype(F32))
        first = lax.broadcasted_iota(jnp.int32, (8, 128), 1) < 64
        for k in range(count):
            copies[k].wait()
            base = (dp_ref[0] ^ k) * depth
            for t in range(depth // 128):
                pair = [
                    jnp.broadcast_to(held[k, 64 * z : 64 * z + 16, wide:].astype(F32)[:1], (8, 128))
                    for z in (2 * t, 2 * t + 1)
                ]
                turned = [pltpu.roll(row, 64, 1) for row in pair]
                at = pl.ds(pl.multiple_of(base + 128 * t, 128), 128)
                g_ref[:8, at] = jnp.where(first, pair[0], turned[1])
                g_ref[8:, at] = jnp.where(first, turned[0], pair[1])
            at = pl.ds(pl.multiple_of(base, depth), depth)
            normed = (x_ref[:, at].astype(F32) * scale * g_ref[:1, at]).astype(BF16)
            a_ref[:, at] = normed
            for c, w in tiles(wide, 512):
                term = dot(normed, held[k, :, c : c + w])
                if k == 0:
                    p_ref[:, c : c + w] = term
                else:
                    p_ref[:, c : c + w] += term

    return run(
        kernel, "project", 11, (dp, tokens, *blocks), [SCALAR, WHOLE] + [ANY] * count,
        (wide_like(rows, wide), low_like(rows, model), wide_like(16, model)), (WHOLE,) * 3,
        [VMEM((count, depth, cols), BF16), DMA((count,))],
    )


def out_norm(dp, attended, blocks, tokens, gains, deps):
    rows, model = tokens.shape
    depth = blocks[0].shape[0]
    count = len(blocks)

    def kernel(dp_ref, o_ref, x_ref, g_ref, *refs):
        block_refs, (m_ref, a_ref, held, sems) = refs[:count], refs[count:]
        copies = fetch(block_refs, held, sems, model)
        for k in range(count):
            copies[k].wait()
            at = pl.ds(pl.multiple_of((dp_ref[0] ^ k) * depth, depth), depth)
            part = o_ref[:, at]
            for c, w in tiles(model, 512):
                term = dot(part, held[k, :, c : c + w])
                if k == 0:
                    m_ref[:, c : c + w] = x_ref[:, c : c + w].astype(F32) + term
                else:
                    m_ref[:, c : c + w] += term
        scale = row_scale(m_ref[...])
        core = dp_ref[0] & 1
        for j in range(count):
            here = slice(depth * j, depth * (j + 1))
            normed = (m_ref[:, here] * scale * g_ref[8:9, here]).astype(BF16)
            to = ((core ^ (j & 1)) * (count // 2) + j // 2) * depth
            a_ref[:, pl.ds(pl.multiple_of(to, depth), depth)] = normed

    return run(
        kernel, "out_norm", 11, (dp, attended, tokens, gains, *blocks), [SCALAR] + [WHOLE] * 3 + [ANY] * count,
        (wide_like(rows, model), low_like(rows, model)), (WHOLE,) * 2,
        [VMEM((count, depth, model), BF16), DMA((count,))], deps,
    )


def norm_back(values, scale, gain, grads, gain_grad_ref, sums):
    model = gain_grad_ref.shape[1]
    inner = 0.0
    for c, w in tiles(model):
        normed, grad = values(c, w) * scale, grads(c, w)
        gain_grad_ref[:, c : c + w] = jnp.broadcast_to(jnp.sum(grad * normed, axis=0, keepdims=True), (8, w))
        inner = inner + jnp.sum(grad * gain(c, w) * normed, axis=-1, keepdims=True)
    inner = inner / model
    for c, w in tiles(model):
        normed = values(c, w) * scale
        sums(c, w, scale * (grads(c, w) * gain(c, w) - normed * inner))


def middle_back(dp, terms, middle, cotangent, live, gains, deps):
    rows, model = middle.shape
    depth = model // 8
    count = len(terms)

    def kernel(dp_ref, m_ref, c_ref, l_ref, g_ref, *refs):
        term_refs, (wide_ref, low_ref, gain_ref, held) = refs[:count], refs[count:]
        core = dp_ref[0] & 1
        for j in range(8):
            at = pl.multiple_of(((core ^ (j & 1)) * 4 + j // 2) * depth, depth)
            held[:, depth * j : depth * (j + 1)] = sum(ref[:, pl.ds(at, depth)].astype(F32) for ref in term_refs)
        scale = row_scale(m_ref[...])
        alive = l_ref[:, :1]

        def keep(c, w, grad):
            total = c_ref[:, c : c + w].astype(F32) * alive + grad
            wide_ref[:, c : c + w] = total
            low_ref[:, c : c + w] = total.astype(BF16)

        norm_back(
            lambda c, w: m_ref[:, c : c + w], scale, lambda c, w: g_ref[8:9, c : c + w],
            lambda c, w: held[:, c : c + w], gain_ref, keep,
        )

    return run(
        kernel, "middle_back", 6, (dp, middle, cotangent, live, gains, *terms), [SCALAR] + [WHOLE] * (4 + count),
        (wide_like(rows, model), low_like(rows, model), wide_like(8, model)), (WHOLE,) * 3,
        [VMEM((rows, model), F32)], deps,
    )


def attended_grad(dp, branch, blocks, deps):
    rows, model = branch.shape
    depth = blocks[0].shape[0]
    count = len(blocks)

    def kernel(dp_ref, y_ref, *refs):
        block_refs, (out_ref, held, sems) = refs[:count], refs[count:]
        copies = fetch(block_refs, held, sems, model)
        for k in range(count):
            copies[k].wait()
            at = pl.ds(pl.multiple_of((dp_ref[0] ^ k) * depth, depth), depth)
            out_ref[:, at] = dot(y_ref[...], held[k], NT).astype(BF16)

    return run(
        kernel, "attended_grad", 11, (dp, branch, *blocks), [SCALAR, WHOLE] + [ANY] * count,
        low_like(rows, model), WHOLE, [VMEM((count, depth, model), BF16), DMA((count,))], deps,
    )


def input_back(dp, grad, blocks, tokens, gains, residual, deps):
    rows, model = tokens.shape
    depth, wide = blocks[0].shape[0], grad.shape[1]
    count = len(blocks)

    def kernel(dp_ref, y_ref, x_ref, g_ref, r_ref, *refs):
        block_refs, (out_ref, gain_ref, held, total, sems) = refs[:count], refs[count:]
        copies = fetch(block_refs, held, sems, wide)
        for k in range(count):
            copies[k].wait()
            at = pl.ds(pl.multiple_of((dp_ref[0] ^ k) * depth, depth), depth)
            total[:, at] = dot(y_ref[...], held[k], NT)
        scale = row_scale(x_ref[...].astype(F32))

        def keep(c, w, back):
            out_ref[:, c : c + w] = (r_ref[:, c : c + w] + back).astype(BF16)

        norm_back(
            lambda c, w: x_ref[:, c : c + w].astype(F32), scale, lambda c, w: g_ref[:1, c : c + w],
            lambda c, w: total[:, c : c + w], gain_ref, keep,
        )

    return run(
        kernel, "input_back", 18, (dp, grad, tokens, gains, residual, *blocks), [SCALAR] + [WHOLE] * 4 + [ANY] * count,
        (low_like(rows, model), wide_like(8, model)), (WHOLE,) * 2,
        [VMEM((count, depth, wide), BF16), VMEM((rows, model), F32), DMA((count,))], deps,
    )


def blocks_outer(dp, x, y, deps):
    rows, cols = y.shape
    depth = x.shape[1] // 8

    def kernel(dp_ref, x_ref, y_ref, odd_ref, even_ref):
        step = pl.program_id(0)
        term = dot(x_ref[...], y_ref[...], TN).astype(BF16)[None]

        @pl.when(step < 4)
        def _():
            odd_ref[...] = term

        @pl.when(step >= 4)
        def _():
            even_ref[...] = term

    block = lambda i, dp_ref: dp_ref[0] ^ (jnp.where(i % 4 == 0, 6, jnp.where(i % 4 == 3, 0, 2 * (i % 4))) + 1 - i // 4)
    return run(
        kernel, "blocks_outer", 10, (dp, x, y),
        [
            pl.BlockSpec((rows, depth), lambda i, dp_ref: (0, block(i, dp_ref))),
            pl.BlockSpec((rows, cols), lambda i, dp_ref: (0, 0)),
        ],
        (jax.ShapeDtypeStruct((4, depth, cols), BF16),) * 2,
        (
            pl.BlockSpec((1, depth, cols), lambda i, dp_ref: (jnp.minimum(i, 3), 0, 0)),
            pl.BlockSpec((1, depth, cols), lambda i, dp_ref: (jnp.maximum(i - 4, 0), 0, 0)),
        ),
        after=deps, prefetch=1, grid=(8,),
    )


def first_sums(even, other, deps):
    _, depth, cols = even.shape
    half = depth // 2

    def kernel(even_ref, other_ref, low_ref, high_ref, *refs):
        add = lambda i, at: (even_ref[i, at].astype(F32) + other_ref[i, at].astype(F32)).astype(BF16)
        low_ref[...] = add(0, slice(0, half))
        high_ref[...] = add(0, slice(half, depth))
        for i, ref in enumerate(refs):
            ref[...] = add(i + 1, slice(0, depth))

    return run(
        kernel, "first_sums", 5, (even, other), [WHOLE] * 2,
        (low_like(half, cols),) * 2 + (low_like(depth, cols),) * 3, (WHOLE,) * 5, after=deps,
    )


def second_sums(x_block, y_block, low, high, deps):
    half, cols = low.shape

    def kernel(x_ref, y_ref, low_ref, high_ref, x_out, y_out):
        add = lambda a, b: (a.astype(F32) + b.astype(F32)).astype(BF16)
        x_out[:half], x_out[half:] = x_ref[:half], add(x_ref[half:], high_ref[...])
        y_out[:half], y_out[half:] = add(y_ref[:half], low_ref[...]), y_ref[half:]

    return run(
        kernel, "second_sums", 2, (x_block, y_block, low, high), [WHOLE] * 4, (low_like(2 * half, cols),) * 2,
        (WHOLE,) * 2, after=deps,
    )


def folded(keep, pieces, deps):
    rows = pieces[0].shape[0]

    def kernel(keep_ref, *refs):
        for i, ref in enumerate(refs[:-1]):
            here = slice(rows * i, rows * (i + 1))
            refs[-1][here] = (keep_ref[here].astype(F32) + ref[...].astype(F32)).astype(BF16)

    count = len(pieces)
    return run(
        kernel, "folded", 7 if count > 1 else 3, (keep, *pieces), [WHOLE] * (1 + count), low_like(*keep.shape), WHOLE, after=deps
    )


def gate_rows(a2, own, other, deps):
    count = len(a2)
    rows, model = a2[0].shape
    half, both = own.shape
    width = both // 2
    parts = tiles(width)

    def kernel(own_hbm, other_hbm, *refs):
        a_hbms, (gu_ref, hid_ref, held, a_ref, sems, a_sems) = refs[:count], refs[count:]
        copies = []
        for i, (at, w) in enumerate(parts):
            for j, (ref, col) in enumerate(
                ((own_hbm, at), (other_hbm, at), (own_hbm, width + at), (other_hbm, width + at))
            ):
                to = held.at[pl.ds((j % 2) * half, half), pl.ds(col, w)]
                copies.append(pltpu.make_async_copy(ref.at[:, pl.ds(col, w)], to, sems.at[4 * i + j]))
        rows_in = [pltpu.make_async_copy(a_hbms[b], a_ref.at[b], a_sems.at[b]) for b in range(count)]

        @pl.when(pl.program_id(0) == 0)
        def _():
            rows_in[0].start()
            for copy in copies + rows_in[1:]:
                copy.start()
            for copy in rows_in:
                copy.wait()

        part = a_ref[pl.program_id(0)]
        for i, (at, w) in enumerate(parts):

            @pl.when(pl.program_id(0) == 0)
            def _():
                for copy in copies[4 * i : 4 * i + 4]:
                    copy.wait()

            gate = dot(part, held[:, at : at + w])
            upper = dot(part, held[:, width + at : width + at + w])
            gu_ref[:, at : at + w] = gate
            gu_ref[:, width + at : width + at + w] = upper
            hid_ref[:, at : at + w] = (gate * jax.nn.sigmoid(gate) * upper).astype(BF16)

    return run(
        kernel, "gate_rows", 2 + 7 * count, (own, other, *a2), [ANY] * (2 + count),
        (wide_like(count * rows, both), low_like(count * rows, width)),
        (pl.BlockSpec((rows, both), lambda i: (i, 0)), pl.BlockSpec((rows, width), lambda i: (i, 0))),
        [VMEM((model, both), BF16), VMEM((count, rows, model), BF16), DMA((4 * len(parts),)), DMA((count,))],
        deps, grid=(count,),
    )


def gate_back(core, gate_up, at_rows, eb, down_own, down_other, own, other, split, deps):
    rows, model = eb[0].shape
    both = gate_up[0].shape[1]
    width = both // 2
    half = down_own.shape[0]
    depth = own.shape[0]
    shares = [rows // 2] * 2 + [rows] if split else [rows] * 2

    def kernel(core_ref, *refs):
        gu_hbms, e_hbms, (down_hbms, gu_w_hbms) = refs[:2], refs[2:4], (refs[4:6], refs[6:8])
        dgu_ref, back_refs, (down_ref, held, gu_ref, e_ref, sems) = refs[8], refs[9:-5], refs[-5:]
        step = pl.program_id(0)
        first, second = [], []
        for i in range(2):
            first.append(pltpu.make_async_copy(e_hbms[i], e_ref.at[i], sems.at[i]))
            to = down_ref.at[pl.ds(pl.multiple_of((core_ref[0] ^ i) * half, 64), half), :]
            first.append(pltpu.make_async_copy(down_hbms[i], to, sems.at[2 + i]))
            first.append(
                pltpu.make_async_copy(gu_hbms[i].at[pl.ds(at_rows[i], rows), :], gu_ref.at[i], sems.at[4 + i])
            )
            second.append(pltpu.make_async_copy(gu_w_hbms[i], held.at[pl.ds(i * depth, depth), :], sems.at[6 + i]))

        @pl.when(step == 0)
        def _():
            for copy in first + second:
                copy.start()
            for copy in first:
                copy.wait()

        part = e_ref[step]
        for at, w in tiles(width):
            back = dot(part, down_ref[at : at + w, :], NT)
            gate, upper = gu_ref[step, :, at : at + w], gu_ref[step, :, width + at : width + at + w]
            sigma = jax.nn.sigmoid(gate)
            dgu_ref[:, at : at + w] = (back * upper * sigma * (1.0 + gate * (1.0 - sigma))).astype(BF16)
            dgu_ref[:, width + at : width + at + w] = (back * gate * sigma).astype(BF16)

        @pl.when(step == 0)
        def _():
            for copy in second:
                copy.wait()

        for i in range(2):

            @pl.when(step == i)
            def _():
                for at, w in tiles(model):
                    part_back = dot(dgu_ref[...], held[at : at + w, :], NT).astype(BF16)
                    if split and i == 0:
                        back_refs[0][:, at : at + w] = part_back[: rows // 2]
                        back_refs[1][:, at : at + w] = part_back[rows // 2 :]
                    else:
                        back_refs[i + split][:, at : at + w] = part_back

    return run(
        kernel, "gate_back", 22, (core, *gate_up, *eb, down_own, down_other, own, other), [SCALAR] + [ANY] * 8,
        (low_like(2 * rows, both),) + tuple(low_like(share, model) for share in shares),
        (pl.BlockSpec((rows, both), lambda i: (i, 0)),)
        + tuple(pl.BlockSpec((share, model), lambda i: (0, 0)) for share in shares),
        [
            VMEM((width, model), BF16), VMEM((2 * depth, both), BF16), VMEM((2, rows, both), F32),
            VMEM((2, rows, model), BF16), DMA((8,)),
        ],
        deps, grid=(2,),
    )


def down_rows(core, hidden, rows, own, other, deps):
    width = hidden[0].shape[1]
    half, model = own.shape
    count = len(hidden)
    blocks = [(i, at) for i, h in enumerate(hidden) for at in range(0, h.shape[0], rows)]

    def kernel(core_ref, own_hbm, other_hbm, *refs):
        hid_refs, out_refs, (held, sems) = refs[:count], refs[count : count + len(blocks)], refs[count + len(blocks) :]
        copies = []
        for i, ref in enumerate((own_hbm, other_hbm)):
            to = held.at[pl.ds(pl.multiple_of((core_ref[0] ^ i) * half, 64), half), :]
            copies.append(pltpu.make_async_copy(ref, to, sems.at[i]))
            copies[-1].start()
        for copy in copies:
            copy.wait()
        for (i, at_row), out_ref in zip(blocks, out_refs):
            for at, w in tiles(model):
                out_ref[:, at : at + w] = dot(hid_refs[i][at_row : at_row + rows], held[:, at : at + w]).astype(BF16)

    return run(
        kernel, "down_rows", 13, (core, own, other, *hidden), [SCALAR, ANY, ANY] + [WHOLE] * count,
        (low_like(rows, model),) * len(blocks), (WHOLE,) * len(blocks),
        [VMEM((width, model), BF16), DMA((2,))], deps,
    )


def outer_sum(starts, xs, ys, pieces, deps):
    height, cols = xs[0].shape[1], ys[0].shape[1]
    rows = sum(x.shape[0] for x in xs)
    half = height // 2
    count, share = len(xs), half // pieces

    def kernel(starts_ref, *refs):
        x_refs, y_refs = refs[:count], refs[count : count + len(ys)]
        keep_ref, piece_refs, (turned, tile) = refs[count + len(ys)], refs[count + len(ys) + 1 : -2], refs[-2:]

        @pl.when(pl.program_id(0) == 0)
        def _():
            base = 0
            for ref in x_refs:
                for at in range(0, height, 128):
                    turned[at : at + 128, base : base + ref.shape[0]] = ref[:, at : at + 128].T
                base += ref.shape[0]

        base = 0
        for ref in y_refs:
            tile[base : base + ref.shape[0], :] = ref[...]
            base += ref.shape[0]
        at = pl.multiple_of(starts_ref[0], 64)
        keep_ref[...] = dot(turned[pl.ds(at, half), :], tile[...]).astype(BF16)
        for i, ref in enumerate(piece_refs):
            at = pl.multiple_of(starts_ref[1] + i * share, 64)
            ref[...] = dot(turned[pl.ds(at, share), :], tile[...]).astype(BF16)

    fixed = lambda i, s: (0, 0)
    column = lambda i, s: (0, i)
    return run(
        kernel, "outer_sum", 25 if cols > D else 14, (starts, *xs, *ys),
        [pl.BlockSpec(x.shape, fixed) for x in xs] + [pl.BlockSpec((y.shape[0], 256), column) for y in ys],
        (low_like(half, cols),) + (low_like(share, cols),) * pieces,
        (pl.BlockSpec((half, 256), column),) + (pl.BlockSpec((share, 256), column),) * pieces,
        [VMEM((height, rows), BF16), VMEM((rows, 256), BF16)],
        deps, prefetch=1, grid=(cols // 256,),
    )


def turn(x, cosine, sine):
    lane = lax.broadcasted_iota(jnp.int32, cosine.shape, 1)
    lower = (lane & (HEAD_DIM - 1)) < HEAD_DIM // 2
    out = []
    for j in range(x.shape[1] // 128):
        tile = x[:, 128 * j : 128 * (j + 1)]
        other = jnp.where(lower, pltpu.roll(tile, 96, 1), pltpu.roll(tile, 32, 1))
        out.append(tile * cosine + other * sine)
    return out


def both_halves(tile, which):
    lane = lax.broadcasted_iota(jnp.int32, tile.shape, 1)
    other = pltpu.roll(tile, HEAD_DIM, 1)
    low, high = (tile, other) if which == 0 else (other, tile)
    zero = jnp.zeros_like(tile)
    return jnp.where(lane < HEAD_DIM, low, zero), jnp.where(lane >= HEAD_DIM, high, zero)


PAIRS = HEADS // KV_HEADS // 2
STEP_ROWS = 128


def masked_scores(q, k, seg_q, seg_k, first):
    scores = lax.dot_general(q, k, (((1,), (1,)), ((), ())), preferred_element_type=F32) * HEAD_DIM ** (-0.5)
    pairs, keys = q.shape[0] // STEP_ROWS, k.shape[0]
    rows = lax.broadcasted_iota(jnp.int32, (STEP_ROWS, keys), 0) + first
    cols = lax.broadcasted_iota(jnp.int32, (STEP_ROWS, keys), 1)
    allowed = (seg_q == seg_k) & (cols <= rows)
    scores = jnp.where(allowed[None], scores.reshape(pairs, STEP_ROWS, keys), -1e30)
    raised = jnp.exp(scores - jnp.max(scores, axis=-1, keepdims=True))
    return (raised / jnp.sum(raised, axis=-1, keepdims=True)).reshape(pairs * STEP_ROWS, keys)


def attend(projected, cosine, sine, segment):
    rows = projected.shape[0]
    kv = KV_HEADS * HEAD_DIM

    def kernel(p_ref, cos_ref, sin_ref, segq_ref, segk_ref, q_ref, k_ref, v_ref, o_ref):
        cosine, sine = cos_ref[...], sin_ref[...]
        for j, tile in enumerate(turn(p_ref[:, :D], cosine, sine)):
            q_ref[:, 128 * j : 128 * (j + 1)] = tile.astype(BF16)
        for j, tile in enumerate(turn(p_ref[:, D : D + kv], cosine, sine)):
            k_ref[:, 128 * j : 128 * (j + 1)] = tile.astype(BF16)
        v_ref[...] = p_ref[:, D + kv : D + 2 * kv].astype(BF16)
        for g in range(KV_HEADS):
            tile = slice(128 * (g // 2), 128 * (g // 2 + 1))
            k_low, k_high = both_halves(k_ref[:, tile].astype(F32), g % 2)
            v_low, v_high = both_halves(v_ref[:, tile].astype(F32), g % 2)
            k_low, k_high, v_low, v_high = (x.astype(BF16) for x in (k_low, k_high, v_low, v_high))
            for first in range(0, rows, STEP_ROWS):
                keys = first + STEP_ROWS
                at = lambda j: slice(128 * (g * PAIRS + j), 128 * (g * PAIRS + j + 1))
                q = jnp.concatenate([q_ref[first:keys, at(j)] for j in range(PAIRS)], axis=0)
                seg_q, seg_k = segq_ref[first:keys, :1], segk_ref[:1, :keys]
                low = masked_scores(q, k_low[:keys], seg_q, seg_k, first).astype(BF16)
                high = masked_scores(q, k_high[:keys], seg_q, seg_k, first).astype(BF16)
                out = jnp.dot(low, v_low[:keys], preferred_element_type=F32)
                out = out + jnp.dot(high, v_high[:keys], preferred_element_type=F32)
                for j in range(PAIRS):
                    o_ref[first:keys, at(j)] = out[STEP_ROWS * j : STEP_ROWS * (j + 1)].astype(BF16)

    return run(
        kernel, "attend", 15,
        (projected, cosine, sine, jnp.broadcast_to(segment[:, None], (rows, 128)), jnp.broadcast_to(segment[None], (8, rows))),
        [WHOLE] * 5, (low_like(rows, D), low_like(rows, kv), low_like(rows, kv), low_like(rows, D)), (WHOLE,) * 4,
    )


def attend_back(queries, key_rows, value_rows, attended_back, cosine, sine, segment, deps):
    rows = queries.shape[0]
    kv = KV_HEADS * HEAD_DIM
    factor = HEAD_DIM ** (-0.5)

    def kernel(q_ref, k_ref, v_ref, b_ref, cos_ref, sin_ref, segq_ref, segk_ref, dp_ref, dk_ref, dv_ref):
        cosine, sine = cos_ref[...], -sin_ref[...]
        lane = lax.broadcasted_iota(jnp.int32, (STEP_ROWS, 128), 1)
        contract = lambda a, b: lax.dot_general(a, b, (((0,), (0,)), ((), ())), preferred_element_type=F32)
        for g in range(KV_HEADS):
            tile = slice(128 * (g // 2), 128 * (g // 2 + 1))
            k_low, k_high = both_halves(k_ref[:, tile].astype(F32), g % 2)
            v_low, v_high = both_halves(v_ref[:, tile].astype(F32), g % 2)
            k_low, k_high, v_low, v_high = (x.astype(BF16) for x in (k_low, k_high, v_low, v_high))
            dk_ref[...] = jnp.zeros_like(dk_ref)
            dv_ref[...] = jnp.zeros_like(dv_ref)
            for first in range(0, rows, STEP_ROWS):
                keys = first + STEP_ROWS
                at = lambda j: slice(128 * (g * PAIRS + j), 128 * (g * PAIRS + j + 1))
                q = jnp.concatenate([q_ref[first:keys, at(j)] for j in range(PAIRS)], axis=0)
                b = jnp.concatenate([b_ref[first:keys, at(j)] for j in range(PAIRS)], axis=0)
                seg_q, seg_k = segq_ref[first:keys, :1], segk_ref[:1, :keys]
                dq, dk, dv = None, [], []
                for k_half, v_half in ((k_low, v_low), (k_high, v_high)):
                    probs = masked_scores(q, k_half[:keys], seg_q, seg_k, first)
                    back = lax.dot_general(b, v_half[:keys], (((1,), (1,)), ((), ())), preferred_element_type=F32)
                    inner = jnp.sum(back * probs, axis=-1, keepdims=True)
                    ds = (probs * (back - inner)).astype(BF16)
                    dv.append(contract(probs.astype(BF16), b))
                    dk.append(contract(ds, q))
                    term = jnp.dot(ds, k_half[:keys], preferred_element_type=F32)
                    dq = term if dq is None else dq + term
                low = lax.broadcasted_iota(jnp.int32, (keys, 128), 1) < HEAD_DIM
                dk_ref[:keys] += jnp.where(low, dk[0], dk[1])
                dv_ref[:keys] += jnp.where(low, dv[0], dv[1])
                for j in range(PAIRS):
                    (turned,) = turn(
                        dq[STEP_ROWS * j : STEP_ROWS * (j + 1)] * factor, cosine[first:keys], sine[first:keys]
                    )
                    dp_ref[first:keys, at(j)] = turned.astype(BF16)
            total_k = dk_ref[...] + pltpu.roll(dk_ref[...], HEAD_DIM, 1)
            total_v = dv_ref[...] + pltpu.roll(dv_ref[...], HEAD_DIM, 1)
            (total_k,) = turn(total_k * factor, cosine, sine)
            mine = lax.broadcasted_iota(jnp.int32, (rows, 128), 1) // HEAD_DIM == g % 2
            for base, total in ((D, total_k), (D + kv, total_v)):
                here = slice(base + 128 * (g // 2), base + 128 * (g // 2 + 1))
                if g % 2 == 0:
                    dp_ref[:, here] = total.astype(BF16)
                else:
                    dp_ref[:, here] = jnp.where(mine, total, dp_ref[:, here].astype(F32)).astype(BF16)

    return run(
        kernel, "attend_back", 24,
        (
            queries, key_rows, value_rows, attended_back, cosine, sine,
            jnp.broadcast_to(segment[:, None], (rows, 128)), jnp.broadcast_to(segment[None], (8, rows)),
        ),
        [WHOLE] * 8, low_like(rows, QKV_W), WHOLE, [VMEM((rows, 128), F32)] * 2, deps,
    )


def turning(position):
    frequency = THETA ** (-(jnp.arange(HEAD_DIM // 2, dtype=F32) * 2.0 / HEAD_DIM))
    phases = position.astype(F32)[:, None] * frequency[None, :]
    cosine, sine = jnp.cos(phases), jnp.sin(phases)
    return jnp.concatenate([cosine] * 4, axis=1), jnp.concatenate([-sine, sine] * 2, axis=1)


def rotary(vectors, cosine, sine_part):
    half_dim = HEAD_DIM // 2
    lower_half = vectors[..., :half_dim]
    upper_half = vectors[..., half_dim:]
    return jnp.concatenate(
        [
            lower_half * cosine - upper_half * sine_part,
            upper_half * cosine + lower_half * sine_part,
        ],
        axis=-1,
    )


def any_mesh(
    tokens, cotangent, seq_table, w_qkv, m_qkv, v_qkv, w_out, m_out, v_out, w_gate_up, m_gate_up, v_gate_up,
    w_down, m_down, v_down, norm_gains, m_gains, v_gains,
):
    everyone = ("dp", "fsdp")
    nd = lax.axis_size("dp")
    rows_here = tokens.shape[0]
    kv_width = KV_HEADS * HEAD_DIM
    group_size = HEADS // KV_HEADS
    factor = HEAD_DIM ** (-0.5)
    width = FF // nd
    d_rows = w_gate_up.shape[0]
    einsum = lambda how, a, b: jnp.einsum(how, a, b, preferred_element_type=F32)
    scatter = lambda x, axes, dim: lax.psum_scatter(x.astype(BF16), axes, scatter_dimension=dim, tiled=True)

    segment, position, live_rows = layout(seq_table[0], rows_here)
    row_ids = jnp.arange(rows_here)
    allowed = (segment[:, None] == segment[None, :]) & (row_ids[None, :] <= row_ids[:, None])
    frequency = THETA ** (-(jnp.arange(HEAD_DIM // 2, dtype=F32) * 2.0 / HEAD_DIM))
    phases = position.astype(F32)[:, None] * frequency[None, :]
    cosine, sine = jnp.cos(phases)[:, None, :], jnp.sin(phases)[:, None, :]

    qkv_full = lax.all_gather(w_qkv.astype(BF16), everyone, axis=0, tiled=True)
    out_full = lax.all_gather(w_out.astype(BF16), everyone, axis=0, tiled=True)
    gains_full = lax.all_gather(norm_gains.astype(BF16), everyone, axis=1, tiled=True).astype(F32)
    pieces = w_gate_up.astype(BF16).reshape(d_rows, 2, nd, width).transpose(2, 0, 1, 3).reshape(nd, d_rows, 2 * width)
    gate_up_here = lax.all_to_all(pieces, "dp", 0, 0, tiled=True)
    gate_up_here = lax.all_gather(gate_up_here, "fsdp", axis=1, tiled=True).reshape(D, 2 * width)
    down_here = lax.all_gather(w_down.astype(BF16), "fsdp", axis=0, tiled=True)

    inputs = tokens.astype(F32)
    scale_one = lax.rsqrt(jnp.mean(inputs * inputs, axis=-1, keepdims=True) + EPS_NORM)
    normed_one = inputs * scale_one
    low_one = (normed_one * gains_full[0]).astype(BF16)
    projected = einsum("td,de->te", low_one, qkv_full)
    queries = rotary(projected[:, :D].reshape(rows_here, HEADS, HEAD_DIM), cosine, sine)
    queries = queries.astype(BF16).reshape(rows_here, KV_HEADS, group_size, HEAD_DIM)
    key_rows = rotary(projected[:, D : D + kv_width].reshape(rows_here, KV_HEADS, HEAD_DIM), cosine, sine).astype(BF16)
    value_rows = projected[:, D + kv_width :].reshape(rows_here, KV_HEADS, HEAD_DIM).astype(BF16)
    scores = jnp.where(allowed, einsum("qhgd,khd->hgqk", queries, key_rows) * factor, -1e30)
    raised = jnp.exp(scores - jnp.max(scores, axis=-1, keepdims=True))
    attention = raised / jnp.sum(raised, axis=-1, keepdims=True)
    attention_low = attention.astype(BF16)
    attended = einsum("hgqk,khd->qhgd", attention_low, value_rows).reshape(rows_here, D).astype(BF16)
    middle = inputs + einsum("td,de->te", attended, out_full)
    scale_two = lax.rsqrt(jnp.mean(middle * middle, axis=-1, keepdims=True) + EPS_NORM)
    normed_two = middle * scale_two
    low_two = lax.all_gather((normed_two * gains_full[1]).astype(BF16), "dp", axis=0, tiled=True)

    back_rows = cotangent.astype(F32) * live_rows[:, None].astype(F32)
    down_back = lax.all_gather(back_rows.astype(BF16), "dp", axis=0, tiled=True)
    gate_up = einsum("td,df->tf", low_two, gate_up_here)
    gate, upper = gate_up[:, :width], gate_up[:, width:]
    sigma = jax.nn.sigmoid(gate)
    hidden = (gate * sigma * upper).astype(BF16)
    output = (middle + scatter(einsum("tf,fd->td", hidden, down_here), "dp", 0).astype(F32)).astype(BF16)
    hidden_back = einsum("td,fd->tf", down_back, down_here)
    gate_back = hidden_back * upper * sigma * (1.0 + gate * (1.0 - sigma))
    gate_up_back = jnp.concatenate([gate_back, hidden_back * gate * sigma], axis=1).astype(BF16)
    normed_two_back = scatter(einsum("tf,df->td", gate_up_back, gate_up_here), "dp", 0).astype(F32)
    down_shard = scatter(einsum("tf,td->fd", hidden, down_back), "fsdp", 0).astype(F32)
    gate_up_grad = einsum("td,tf->df", low_two, gate_up_back).reshape(nd, D // nd, 2 * width)
    gate_up_grad = lax.all_to_all(scatter(gate_up_grad, "fsdp", 1), "dp", 0, 0, tiled=True)
    gate_up_shard = gate_up_grad.reshape(nd, d_rows, 2, width).transpose(1, 2, 0, 3).reshape(d_rows, 2 * FF).astype(F32)

    def norm_grad(normed, scale, gain, grad):
        inner = grad * gain
        grad_in = scale * (inner - normed * jnp.mean(inner * normed, axis=-1, keepdims=True))
        return grad_in, jnp.sum(grad * normed, axis=0)

    middle_grad, gain_two_grad = norm_grad(normed_two, scale_two, gains_full[1], normed_two_back)
    middle_grad = back_rows + middle_grad
    branch_back = middle_grad.astype(BF16)
    out_shard = scatter(scatter(einsum("tr,tf->rf", attended, branch_back), "dp", 0), "fsdp", 0).astype(F32)
    attended_back = einsum("te,de->td", branch_back, out_full).astype(BF16)
    attended_back = attended_back.reshape(rows_here, KV_HEADS, group_size, HEAD_DIM)
    prob_back = einsum("qhgd,khd->hgqk", attended_back, value_rows)
    value_back = einsum("hgqk,qhgd->khd", attention_low, attended_back)
    score_back = attention * (prob_back - jnp.sum(prob_back * attention, axis=-1, keepdims=True))
    score_back = score_back.astype(BF16)
    query_back = einsum("hgqk,khd->qhgd", score_back, key_rows) * factor
    key_back = einsum("hgqk,qhgd->khd", score_back, queries) * factor
    query_back = rotary(query_back.reshape(rows_here, HEADS, HEAD_DIM), cosine, -sine).reshape(rows_here, D)
    key_back = rotary(key_back, cosine, -sine).reshape(rows_here, kv_width)
    projected_back = jnp.concatenate([query_back, key_back, value_back.reshape(rows_here, kv_width)], axis=1).astype(BF16)
    qkv_shard = scatter(scatter(einsum("tr,tf->rf", low_one, projected_back), "dp", 0), "fsdp", 0).astype(F32)
    normed_one_back = einsum("te,de->td", projected_back, qkv_full)
    input_norm_back, gain_one_grad = norm_grad(normed_one, scale_one, gains_full[0], normed_one_back)
    input_grad = (middle_grad + input_norm_back).astype(BF16)
    gain_grads = jnp.stack([gain_one_grad, gain_two_grad], axis=1)
    gain_shard = lax.psum_scatter(gain_grads, everyone, scatter_dimension=0, tiled=True).T

    return (
        output,
        input_grad,
        *adam_step(w_qkv, m_qkv, v_qkv, qkv_shard, RATE_MATRIX, DECAY_MATRIX),
        *adam_step(w_out, m_out, v_out, out_shard, RATE_MATRIX, DECAY_MATRIX),
        *adam_step(w_gate_up, m_gate_up, v_gate_up, gate_up_shard, RATE_MATRIX, DECAY_MATRIX),
        *adam_step(w_down, m_down, v_down, down_shard, RATE_MATRIX, DECAY_MATRIX),
        *adam_step(norm_gains, m_gains, v_gains, gain_shard, RATE_GAIN, 0.0),
    )


def swap(x, k):
    return lax.ppermute(x, "dp", [(d, d ^ k) for d in range(8)])


def gather_plane(own, *deps):
    b = {0: own}
    b[2] = swap(own, 2)
    b[4] = swap(own, 4)
    b[1] = swap(own, 1)
    low = half_of(b[4], 0, *deps)
    high = half_of(b[2], 1, *deps)
    b[6] = joined(swap(low, 2), swap(high, 4))
    for k in (2, 4, 6):
        b[k + 1] = swap(b[k], 1)
    return [b[k] for k in range(8)]


def total(terms):
    return sum(term.astype(F32) for term in terms)


def cube(
    tokens, cotangent, seq_table, w_qkv, m_qkv, v_qkv, w_out, m_out, v_out, w_gate_up, m_gate_up, v_gate_up,
    w_down, m_down, v_down, norm_gains, m_gains, v_gains,
):
    nf = lax.axis_size("fsdp")
    dp_index = lax.axis_index("dp")
    dp = dp_index[None]
    core, chip = dp & 1, dp_index >> 1
    rows_here = tokens.shape[0]
    d_rows = w_qkv.shape[0]
    width = FF // 4

    gain_pad = jnp.pad(norm_gains.astype(BF16).reshape(1, 2 * d_rows), ((0, d_rows - 1), (0, 128 - 2 * d_rows)))
    qkv_low = jnp.concatenate([w_qkv.astype(BF16), gain_pad], axis=1)
    qkv_own = lax.all_gather(qkv_low, "fsdp", axis=0, tiled=True)

    gu_low = lowered(w_gate_up, qkv_low)
    gu_cols = jnp.zeros((4, d_rows, 2 * width), BF16)
    for k in range(4):
        there = chip ^ k
        piece = jnp.concatenate(
            [lax.dynamic_slice(gu_low, (0, (h * 4 + there) * width), (d_rows, width)) for h in range(2)], axis=1
        )
        if k:
            piece = swap(piece, 2 * k)
        gu_cols = lax.dynamic_update_slice(gu_cols, piece[None], (there, 0, 0))

    segment, position, live_rows = layout(seq_table[0], rows_here)
    cosine, sine = turning(position)
    live = jnp.broadcast_to(live_rows[:, None].astype(F32), (rows_here, 128))
    eb = (cotangent.astype(F32) * live_rows[:, None].astype(F32)).astype(BF16)
    eb_x_high = swap(half_of(eb, 1, qkv_low), 2)
    eb_y_low = swap(half_of(eb, 0, qkv_low), 4)

    out_own = lax.all_gather(lowered(w_out, gu_cols, eb_x_high, eb_y_low), "fsdp", axis=0, tiled=True)
    gu_own = lax.all_gather(behind(gu_cols, qkv_own), "fsdp", axis=1, tiled=True).reshape(D // 2, 2 * width)

    qkv_blocks = gather_plane(qkv_own)
    down_own = lax.all_gather(lowered(w_down, qkv_blocks[2], qkv_blocks[4]), "fsdp", axis=0, tiled=True)
    projected, low_one, gains = project(dp, tokens, qkv_blocks)
    queries, key_rows, value_rows, attended = attend(projected, cosine, sine, segment)
    out_blocks = gather_plane(behind(out_own, qkv_blocks[6]), attended)
    eb_x = joined(swap(half_of(eb, 0, attended), 2), eb_x_high)
    eb_y = joined(eb_y_low, swap(half_of(eb, 1, attended), 4))
    middle, a2 = out_norm(dp, attended, out_blocks, tokens, gains, (eb_x, eb_y))

    a2_x, a2_y = swap(a2, 2), swap(a2, 4)
    gu_own = behind(gu_own, a2)
    gu_other = swap(gu_own, 1)
    a2_low, a2_high = swap(half_of(a2_y, 0), 2), swap(half_of(a2_x, 1), 4)
    eb_low, eb_high = swap(half_of(eb_y, 0, a2_x), 2), swap(half_of(eb_x, 1, a2_y), 4)
    gate_up_a, hidden_a = gate_rows((a2, a2_x, a2_y), gu_own, gu_other, ())
    a2_d = joined(a2_low, a2_high, hidden_a)
    gate_up_b, hidden_b = gate_rows((a2_d,), gu_own, gu_other, (hidden_a,))
    eb_d = joined(eb_low, eb_high, hidden_b)
    hidden = (hidden_a, hidden_b)
    half_ff = width // 2
    keep, send = outer_sum(jnp.concatenate([core, 1 - core]) * half_ff, hidden, (eb, eb_x, eb_y, eb_d), 1, ())
    down_own = behind(down_own, keep)
    down_other = swap(down_own, 1)
    down_grad = folded(keep, (swap(send, 1),), ())
    down_shard = lax.psum_scatter(down_grad, "fsdp", scatter_dimension=0, tiled=True)
    down_state = adam_step(w_down, m_down, v_down, down_shard.astype(F32), RATE_MATRIX, DECAY_MATRIX)

    weights = (down_own, down_other, gu_own, gu_other)
    back_gu_a, back_low, back_high, back_y = gate_back(
        core, (gate_up_b, gate_up_a), (0, 2 * rows_here), (eb_d, eb_y), *weights, True, (down_grad,)
    )
    back_low, back_high = swap(back_low, 2), swap(back_high, 4)
    back_gu_b, back_x, back_own = gate_back(
        core, (gate_up_a, gate_up_a), (rows_here, 0), (eb_x, eb), *weights, False, (back_y,)
    )
    back_x, back_y = second_sums(back_x, back_y, back_low, back_high, ())
    sent_x, sent_y = swap(back_x, 2), swap(back_y, 4)
    keep, send = outer_sum(
        jnp.array([0, D // 2], jnp.int32), (a2_d, a2_y, a2_x, a2), (back_gu_a, back_gu_b), 1, (back_x,)
    )
    send = swap(send, 1)
    out_own_rows, out_x, out_y, out_d = down_rows(core, hidden, rows_here, down_own, down_other, (keep,))

    wide_back, branch_back, gain_two_grad = middle_back(
        dp, (back_own, sent_x, sent_y), middle, cotangent, live, gains, (out_x, down_state[2])
    )
    out_x, out_y = swap(behind(out_x, branch_back), 2), swap(behind(out_y, branch_back), 4)
    odd, even = blocks_outer(dp, attended, branch_back, ())
    odd = swap(odd, 1)
    gu_grad = folded(keep, (send,), (even,)).reshape(4, D // 8, 2 * width)
    gu_grad_z = lax.psum_scatter(gu_grad, "fsdp", scatter_dimension=1, tiled=True)
    attended_back = attended_grad(dp, branch_back, out_blocks, (gu_grad,))
    low, high, sum_x, sum_y, out_terms = first_sums(even, odd, (attended_back,))
    low, high = swap(low, 2), swap(high, 4)
    projected_back = attend_back(queries, key_rows, value_rows, attended_back, cosine, sine, segment, (sum_x,))
    sum_x, sum_y = second_sums(sum_x, sum_y, low, high, (projected_back, out_x, out_y))
    out_terms = (out_terms, swap(sum_x, 2), swap(sum_y, 4))
    odd, even = blocks_outer(dp, low_one, projected_back, (sum_x,))
    odd = swap(odd, 1)
    low, high, sum_x, sum_y, qkv_terms = first_sums(even, odd, ())
    low, high = swap(low, 2), swap(high, 4)
    input_grad, gain_one_grad = input_back(dp, projected_back, qkv_blocks, tokens, gains, wide_back, (sum_x,))
    gain_grads = jnp.stack([gain_one_grad[0], gain_two_grad[0]])
    gain_grads = gain_grads + swap(gain_grads, 1)
    sum_x, sum_y = second_sums(sum_x, sum_y, low, high, (input_grad, *out_terms[1:]))
    qkv_terms = (qkv_terms, swap(sum_x, 2), swap(sum_y, 4))
    out_mine = total((behind(out_terms[0], sum_x),) + out_terms[1:]).astype(BF16)
    out_shard = lax.psum_scatter(out_mine, "fsdp", scatter_dimension=0, tiled=True).astype(F32)

    gain_grads = gain_grads + swap(gain_grads, 2) + swap(gain_grads, 4) + swap(gain_grads, 6)
    gain_mine = lax.dynamic_slice(gain_grads, (0, dp_index * (D // 8)), (2, D // 8)).reshape(2, nf, d_rows)
    gain_mine = gain_mine.transpose(1, 0, 2).reshape(nf, 1, 2 * d_rows).astype(BF16)
    gain_mine = jnp.pad(gain_mine, ((0, 0), (0, d_rows - 1), (0, 128 - 2 * d_rows))).reshape(D // 8, 128)
    qkv_mine = jnp.concatenate([total(qkv_terms).astype(BF16), gain_mine], axis=1)
    qkv_mine = behind(qkv_mine, gu_grad_z)
    qkv_shard = lax.psum_scatter(qkv_mine, "fsdp", scatter_dimension=0, tiled=True).astype(F32)
    gain_shard = qkv_shard[0, QKV_W : QKV_W + 2 * d_rows].reshape(2, d_rows)
    out_d = swap(behind(out_d, qkv_mine), 6)
    output = (middle + total((out_own_rows, out_x, out_y, out_d))).astype(BF16)

    gate_up_shard = jnp.zeros((d_rows, 2 * FF), BF16)
    for k in range(4):
        there = chip ^ k
        piece = lax.dynamic_slice(gu_grad_z, (there, 0, 0), (1, d_rows, 2 * width))[0]
        if k:
            piece = swap(piece, 2 * k)
        for h in range(2):
            gate_up_shard = lax.dynamic_update_slice(
                gate_up_shard, piece[:, h * width : (h + 1) * width], (0, (h * 4 + there) * width)
            )

    gate_up_state = adam_step(
        w_gate_up, m_gate_up, v_gate_up, gate_up_shard.astype(F32), RATE_MATRIX, DECAY_MATRIX
    )

    return (
        output,
        input_grad,
        *adam_step(w_qkv, m_qkv, v_qkv, qkv_shard[:, :QKV_W], RATE_MATRIX, DECAY_MATRIX),
        *adam_step(w_out, m_out, v_out, out_shard, RATE_MATRIX, DECAY_MATRIX),
        *gate_up_state,
        *down_state,
        *adam_step(norm_gains, m_gains, v_gains, gain_shard, RATE_GAIN, 0.0),
    )


def solution(mesh):
    rows = P(("dp", "fsdp"), None)
    cols = P(None, ("dp", "fsdp"))
    in_specs = (rows,) * 15 + (cols,) * 3
    out_specs = (rows,) * 14 + (cols,) * 3
    body = cube if (mesh.shape["dp"], mesh.shape["fsdp"]) == (8, 4) else any_mesh
    return jax.shard_map(body, mesh=mesh, in_specs=in_specs, out_specs=out_specs, check_vma=False)
```

```python
import jax
import jax.numpy as jnp
from jax import lax
from jax.experimental import pallas as pl
from jax.experimental.pallas import tpu as pltpu
from jax.sharding import PartitionSpec as P

D = 2048
FF = 5632
HEADS = 32
KV_HEADS = 4
HEAD_DIM = 64
STEP = 10
QKV_W = (HEADS + 2 * KV_HEADS) * HEAD_DIM
PAD = 128


EPS_NORM = 1e-05
BETA_ONE = 0.9
BETA_TWO = 0.999
EPS_ADAM = 1e-08
RATE_MATRIX = 0.02
RATE_GAIN = 0.2
DECAY_MATRIX = 0.1
THETA = 10000.0

BF16 = jnp.bfloat16
F32 = jnp.float32


def layout(lengths, count):
    seq_ends = jnp.cumsum(lengths)
    row_ids = jnp.arange(count, dtype=jnp.int32)
    passed = row_ids[:, None] >= seq_ends[None, :]
    segment = jnp.sum(passed.astype(jnp.int32), axis=1)
    start = jnp.max(jnp.where(passed, seq_ends[None, :], 0), axis=1)
    return (segment, row_ids - start, row_ids < seq_ends[-1])


def adam_step(weight, first_moment, second_moment, gradient, step_rate, weight_decay):
    first_new = BETA_ONE * first_moment + (1.0 - BETA_ONE) * gradient
    second_new = BETA_TWO * second_moment + (1.0 - BETA_TWO) * gradient * gradient
    first_hat = first_new / (1.0 - BETA_ONE**STEP)
    second_hat = second_new / (1.0 - BETA_TWO**STEP)
    updated = weight - step_rate * (
        first_hat / (jnp.sqrt(second_hat) + EPS_ADAM) + weight_decay * weight
    )
    return (first_new, second_new, updated)


VMEM = pltpu.VMEM
ANY = pl.BlockSpec(memory_space=pl.ANY)
WHOLE = pl.BlockSpec(memory_space=pltpu.VMEM)
SCALAR = pl.BlockSpec(memory_space=pltpu.SMEM)
DMA = pltpu.SemaphoreType.DMA
HBM = pl.BlockSpec(memory_space=pltpu.HBM)


def run(
    kernel, name, us, args, in_specs, out_shape, out_specs, scratch=(), after=(), aliases=None, prefetch=0, grid=None, vmem=52
):
    count, ordered = len(args), len(after)

    def body(*refs):
        kernel(*refs[:count], *refs[count + ordered :])

    specs = dict(
        in_specs=list(in_specs) + [ANY] * ordered,
        out_specs=out_specs,
        scratch_shapes=list(scratch),
    )
    if grid and not prefetch:
        specs["grid"] = grid
    if prefetch:
        specs = dict(grid_spec=pltpu.PrefetchScalarGridSpec(num_scalar_prefetch=prefetch, grid=grid, **specs))
    return pl.pallas_call(
        body,
        out_shape=out_shape,
        input_output_aliases=aliases or {},
        compiler_params=pltpu.CompilerParams(vmem_limit_bytes=vmem << 20),
        cost_estimate=pl.CostEstimate(flops=int(us * COST), bytes_accessed=int(us * 1.0e5), transcendentals=0),
        name=name,
        **specs,
    )(*args, *after)


COST = 0.1e9


def low_like(rows, cols):
    return jax.ShapeDtypeStruct((rows, cols), BF16)


def wide_like(rows, cols):
    return jax.ShapeDtypeStruct((rows, cols), F32)


def behind(x, *deps, vmem=52):
    return run(
        lambda x_ref, o_ref: None,
        "behind",
        0.1,
        (x,),
        [HBM],
        jax.ShapeDtypeStruct(x.shape, x.dtype),
        HBM,
        after=deps,
        aliases={0: 0},
        vmem=vmem,
    )


def lowered(x, *deps):
    def kernel(x_ref, o_ref):
        o_ref[...] = x_ref[...].astype(BF16)

    return run(kernel, "lowered", 1, (x,), [WHOLE], low_like(*x.shape), WHOLE, after=deps)


def half_of(x, which, *deps):
    rows = x.shape[0] // 2

    def kernel(x_ref, o_ref, sem):
        copy = pltpu.make_async_copy(x_ref.at[pl.ds(which * rows, rows), :], o_ref, sem)
        copy.start()
        copy.wait()

    return run(kernel, "half_of", 1, (x,), [ANY], low_like(rows, x.shape[1]), WHOLE, [DMA], deps)


def halves(first, second, *deps):
    rows = first.shape[0] // 2

    def kernel(first_ref, second_ref, upper_ref, lower_ref, sems):
        copies = [
            pltpu.make_async_copy(ref.at[pl.ds(i * rows, rows), :], out_ref, sems.at[i])
            for i, (ref, out_ref) in enumerate(((first_ref, upper_ref), (second_ref, lower_ref)))
        ]
        for copy in copies:
            copy.start()
        for copy in copies:
            copy.wait()

    return run(
        kernel, "halves", 1, (first, second), [ANY] * 2, (low_like(rows, first.shape[1]),) * 2, (WHOLE,) * 2,
        [DMA((2,))], deps,
    )


def stacked(slots, pieces, *deps):
    count = len(pieces)

    def kernel(slots_ref, *refs):
        copies = [
            pltpu.make_async_copy(ref, refs[count].at[slots_ref[i]], refs[count + 1].at[i])
            for i, ref in enumerate(refs[:count])
        ]
        for copy in copies:
            copy.start()
        for copy in copies:
            copy.wait()

    return run(
        kernel, "stacked", 1, (slots, *pieces), [SCALAR] + [ANY] * count,
        jax.ShapeDtypeStruct((count, *pieces[0].shape), BF16), WHOLE, [DMA((count,))], deps,
    )


def tiles(width, step=256):
    return [(at, min(step, width - at)) for at in range(0, width, step)]


NT = (((1,), (1,)), ((), ()))
TN = (((0,), (0,)), ((), ()))


def dot(a, b, dims=(((1,), (0,)), ((), ()))):
    return lax.dot_general(a, b, dims, preferred_element_type=F32)


def flat(blocks):
    pieces, places = [], []
    for i, block in enumerate(blocks):
        row = 0
        for piece in block if isinstance(block, tuple) else (block,):
            pieces.append(piece)
            places.append((i, row))
            row += piece.shape[0]
    return pieces, places


def fetch(piece_refs, places, held, sems, width):
    copies = {}
    for j, (ref, (i, row)) in enumerate(zip(piece_refs, places)):
        to = held.at[i, pl.ds(row, ref.shape[0]), :]
        copies.setdefault(i, []).append(pltpu.make_async_copy(ref.at[:, pl.ds(0, width)], to, sems.at[j]))
        copies[i][-1].start()
    return copies


def wait(copies):
    for copy in copies:
        copy.wait()


def row_scale(values):
    return lax.rsqrt(jnp.mean(values * values, axis=-1, keepdims=True) + EPS_NORM)


def project_blocks(dp, ks, x_ref, scale, held, copies, a_ref, g_ref, add):
    _, depth, cols = held.shape
    wide = cols - 128
    first = lax.broadcasted_iota(jnp.int32, (8, 128), 1) < 64
    for i, k in enumerate(ks):
        wait(copies[i])
        base = (dp ^ k) * depth
        for t in range(depth // 128):
            pair = [
                jnp.broadcast_to(held[i, 64 * z : 64 * z + 16, wide:].astype(F32)[:1], (8, 128))
                for z in (2 * t, 2 * t + 1)
            ]
            turned = [pltpu.roll(row, 64, 1) for row in pair]
            at = pl.ds(pl.multiple_of(base + 128 * t, 128), 128)
            g_ref[:8, at] = jnp.where(first, pair[0], turned[1])
            g_ref[8:, at] = jnp.where(first, turned[0], pair[1])
        at = pl.ds(pl.multiple_of(base, depth), depth)
        normed = (x_ref[:, at].astype(F32) * scale * g_ref[:1, at]).astype(BF16)
        a_ref[:, at] = normed
        for c, w in tiles(wide, 512):
            add(i, c, w, dot(normed, held[i, :, c : c + w]))


def project(dp, ks, tokens, blocks, before):
    rows, model = tokens.shape
    pieces, places = flat(blocks)
    depth, cols = model // 8, pieces[0].shape[1]
    count, ahead = len(pieces), len(before)
    wide = cols - 128

    def kernel(dp_ref, x_ref, *refs):
        before_refs, block_refs = refs[:ahead], refs[ahead : ahead + count]
        p_ref, a_ref, g_ref, held, sems = refs[ahead + count :]
        copies = fetch(block_refs, places, held, sems, cols)
        if ahead:
            a_ref[...] = before_refs[1][...]
            g_ref[...] = before_refs[2][...]
        else:
            a_ref[...] = jnp.zeros_like(a_ref)
            g_ref[...] = jnp.zeros_like(g_ref)

        def add(i, c, w, term):
            if i:
                p_ref[:, c : c + w] += term
            elif ahead:
                p_ref[:, c : c + w] = before_refs[0][:, c : c + w] + term
            else:
                p_ref[:, c : c + w] = term

        project_blocks(dp_ref[0], ks, x_ref, row_scale(x_ref[...].astype(F32)), held, copies, a_ref, g_ref, add)

    return run(
        kernel, "project", 5 if ahead else 9, (dp, tokens, *before, *pieces), [SCALAR] + [WHOLE] * (1 + ahead) + [ANY] * count,
        (wide_like(rows, wide), low_like(rows, model), wide_like(16, model)), (WHOLE,) * 3,
        [VMEM((len(blocks), depth, cols), BF16), DMA((count,))],
    )


def out_part(dp, ks, attended, blocks, base, deps):
    rows, model = base.shape
    pieces, places = flat(blocks)
    depth, count = model // 8, len(pieces)

    def kernel(dp_ref, o_ref, x_ref, *refs):
        block_refs, (m_ref, held, sems) = refs[:count], refs[count:]
        copies = fetch(block_refs, places, held, sems, model)
        add_blocks(dp_ref[0], ks, o_ref, x_ref, held, copies, m_ref)

    return run(
        kernel, "out_part", 8, (dp, attended, base, *pieces), [SCALAR] + [WHOLE] * 2 + [ANY] * count,
        wide_like(rows, model), WHOLE, [VMEM((len(blocks), depth, model), BF16), DMA((count,))], deps,
    )


def add_blocks(dp, ks, o_ref, x_ref, held, copies, m_ref):
    _, depth, model = held.shape
    for i, k in enumerate(ks):
        wait(copies[i])
        at = pl.ds(pl.multiple_of((dp ^ k) * depth, depth), depth)
        part = o_ref[:, at]
        for c, w in tiles(model, 512):
            term = dot(part, held[i, :, c : c + w])
            if i == 0:
                m_ref[:, c : c + w] = x_ref[:, c : c + w].astype(F32) + term
            else:
                m_ref[:, c : c + w] += term


def out_norm(dp, ks, attended, blocks, base, gains, deps):
    rows, model = base.shape
    pieces, places = flat(blocks)
    depth, count = model // 8, len(pieces)

    def kernel(dp_ref, o_ref, x_ref, g_ref, *refs):
        block_refs, (m_ref, a_ref, held, sems) = refs[:count], refs[count:]
        copies = fetch(block_refs, places, held, sems, model)
        add_blocks(dp_ref[0], ks, o_ref, x_ref, held, copies, m_ref)
        scale = row_scale(m_ref[...])
        for c, w in tiles(model):
            a_ref[:, c : c + w] = (m_ref[:, c : c + w] * scale * g_ref[8:9, c : c + w]).astype(BF16)

    return run(
        kernel, "out_norm", 6, (dp, attended, base, gains, *pieces), [SCALAR] + [WHOLE] * 3 + [ANY] * count,
        (wide_like(rows, model), low_like(rows, model)), (WHOLE,) * 2,
        [VMEM((len(blocks), depth, model), BF16), DMA((count,))], deps,
    )


def norm_back(values, scale, gain, grads, gain_grad_ref, sums):
    model = gain_grad_ref.shape[1]
    inner = 0.0
    for c, w in tiles(model):
        normed, grad = values(c, w) * scale, grads(c, w)
        gain_grad_ref[:, c : c + w] = jnp.broadcast_to(jnp.sum(grad * normed, axis=0, keepdims=True), (8, w))
        inner = inner + jnp.sum(grad * gain(c, w) * normed, axis=-1, keepdims=True)
    inner = inner / model
    for c, w in tiles(model):
        normed = values(c, w) * scale
        sums(c, w, scale * (grads(c, w) * gain(c, w) - normed * inner))


def middle_back(terms, middle, cotangent, live, gains, deps):
    rows, model = middle.shape
    count = len(terms)

    def kernel(m_ref, c_ref, l_ref, g_ref, *refs):
        term_refs, (wide_ref, low_ref, gain_ref, held) = refs[:count], refs[count:]
        for c, w in tiles(model):
            held[:, c : c + w] = sum(ref[:, c : c + w].astype(F32) for ref in term_refs)
        scale = row_scale(m_ref[...])
        alive = l_ref[:, :1]

        def keep(c, w, grad):
            total = c_ref[:, c : c + w].astype(F32) * alive + grad
            wide_ref[:, c : c + w] = total
            low_ref[:, c : c + w] = total.astype(BF16)

        norm_back(
            lambda c, w: m_ref[:, c : c + w], scale, lambda c, w: g_ref[8:9, c : c + w],
            lambda c, w: held[:, c : c + w], gain_ref, keep,
        )

    return run(
        kernel, "middle_back", 6, (middle, cotangent, live, gains, *terms), [WHOLE] * (4 + count),
        (wide_like(rows, model), low_like(rows, model), wide_like(8, model)), (WHOLE,) * 3,
        [VMEM((rows, model), F32)], deps,
    )


def attended_grad(dp, branch, blocks, deps):
    rows, model = branch.shape
    pieces, places = flat(blocks)
    depth, count = model // 8, len(pieces)

    def kernel(dp_ref, y_ref, *refs):
        block_refs, (out_ref, held, sems) = refs[:count], refs[count:]
        copies = fetch(block_refs, places, held, sems, model)
        for k in range(len(blocks)):
            wait(copies[k])
            at = pl.ds(pl.multiple_of((dp_ref[0] ^ k) * depth, depth), depth)
            out_ref[:, at] = dot(y_ref[...], held[k], NT).astype(BF16)

    return run(
        kernel, "attended_grad", 11, (dp, branch, *pieces), [SCALAR, WHOLE] + [ANY] * count,
        low_like(rows, model), WHOLE, [VMEM((len(blocks), depth, model), BF16), DMA((count,))], deps,
    )


def input_back(dp, grad, blocks, tokens, gains, residual, deps):
    rows, model = tokens.shape
    pieces, places = flat(blocks)
    depth, wide, count = model // 8, grad.shape[1], len(pieces)

    def kernel(dp_ref, y_ref, x_ref, g_ref, r_ref, *refs):
        block_refs, (out_ref, gain_ref, held, total, sems) = refs[:count], refs[count:]
        copies = fetch(block_refs, places, held, sems, wide)
        for k in range(len(blocks)):
            wait(copies[k])
            at = pl.ds(pl.multiple_of((dp_ref[0] ^ k) * depth, depth), depth)
            total[:, at] = dot(y_ref[...], held[k], NT)
        scale = row_scale(x_ref[...].astype(F32))

        def keep(c, w, back):
            out_ref[:, c : c + w] = (r_ref[:, c : c + w] + back).astype(BF16)

        norm_back(
            lambda c, w: x_ref[:, c : c + w].astype(F32), scale, lambda c, w: g_ref[:1, c : c + w],
            lambda c, w: total[:, c : c + w], gain_ref, keep,
        )

    return run(
        kernel, "input_back", 18, (dp, grad, tokens, gains, residual, *pieces), [SCALAR] + [WHOLE] * 4 + [ANY] * count,
        (low_like(rows, model), wide_like(8, model)), (WHOLE,) * 2,
        [VMEM((len(blocks), depth, wide), BF16), VMEM((rows, model), F32), DMA((count,))], deps,
    )


def blocks_outer(dp, x, y, deps):
    rows, cols = y.shape
    depth = x.shape[1] // 8

    def kernel(dp_ref, x_ref, y_ref, *out_refs):
        step = pl.program_id(0)
        term = dot(x_ref[...], y_ref[...], TN).astype(BF16)[None]
        for ref, low, high in zip(out_refs, (0, 2, 4), (2, 4, 8)):

            @pl.when((step >= low) & (step < high))
            def _():
                ref[...] = term

    block = lambda i, dp_ref: dp_ref[0] ^ (jnp.where(i % 4 == 0, 6, jnp.where(i % 4 == 3, 0, 2 * (i % 4))) + 1 - i // 4)
    return run(
        kernel, "blocks_outer", 10, (dp, x, y),
        [
            pl.BlockSpec((rows, depth), lambda i, dp_ref: (0, block(i, dp_ref))),
            pl.BlockSpec((rows, cols), lambda i, dp_ref: (0, 0)),
        ],
        tuple(jax.ShapeDtypeStruct((n, depth, cols), BF16) for n in (2, 2, 4)),
        tuple(
            pl.BlockSpec((1, depth, cols), lambda i, dp_ref, low=low, n=n: (jnp.clip(i - low, 0, n - 1), 0, 0))
            for low, n in ((0, 2), (2, 2), (4, 4))
        ),
        after=deps, prefetch=1, grid=(8,),
    )


def first_sums(even, others, deps):
    _, depth, cols = even.shape
    half = depth // 2

    def kernel(even_ref, first_ref, second_ref, low_ref, high_ref, *refs):
        other = lambda i, at: (first_ref if i < 2 else second_ref)[i % 2, at].astype(F32)
        add = lambda i, at: (even_ref[i, at].astype(F32) + other(i, at)).astype(BF16)
        low_ref[...] = add(0, slice(0, half))
        high_ref[...] = add(0, slice(half, depth))
        for i, ref in enumerate(refs):
            ref[...] = add(i + 1, slice(0, depth))

    return run(
        kernel, "first_sums", 5, (even, *others), [WHOLE] * 3,
        (low_like(half, cols),) * 2 + (low_like(depth, cols),) * 3, (WHOLE,) * 5, after=deps,
    )


def second_sums(x_block, y_block, low, high, deps):
    half, cols = low.shape

    def kernel(x_ref, y_ref, low_ref, high_ref, x_out, y_out):
        add = lambda a, b: (a.astype(F32) + b.astype(F32)).astype(BF16)
        x_out[:half], x_out[half:] = x_ref[:half], add(x_ref[half:], high_ref[...])
        y_out[:half], y_out[half:] = add(y_ref[:half], low_ref[...]), y_ref[half:]

    return run(
        kernel, "second_sums", 2, (x_block, y_block, low, high), [WHOLE] * 4, (low_like(2 * half, cols),) * 2,
        (WHOLE,) * 2, after=deps,
    )


def folded(keep, others, parts, deps):
    rows, cols = keep.shape
    share, count = cols // parts, len(others)

    def kernel(keep_ref, *refs):
        row = 0
        for other_ref in refs[:count]:
            down = slice(row, row + other_ref.shape[0])
            row += other_ref.shape[0]
            for i, ref in enumerate(refs[count:]):
                here = slice(share * i, share * (i + 1))
                ref[down] = (keep_ref[down, here].astype(F32) + other_ref[:, here].astype(F32)).astype(BF16)

    return run(
        kernel, "folded", 2 if parts > 1 else 1, (keep, *others), [WHOLE] * (1 + count), (low_like(rows, share),) * parts,
        (WHOLE,) * parts, after=deps,
    )


def gate_rows(a2, weight, deps):
    pieces, _ = flat(a2)
    count = len(pieces)
    rows = sum(piece.shape[0] for piece in pieces)
    model, both = weight.shape
    width = both // 2
    parts = tiles(width)

    def kernel(w_hbm, *refs):
        a_hbms, (gu_hbm, hid_ref, held, a_ref, stage, sems, a_sems, out_sems) = refs[:count], refs[count:]
        row, rows_in, arriving = 0, [], []
        for i, ref in enumerate(a_hbms):
            rows_in.append(pltpu.make_async_copy(ref, a_ref.at[pl.ds(row, ref.shape[0]), :], a_sems.at[i]))
            row += ref.shape[0]
        for i, (at, w) in enumerate(parts):
            arriving.append([])
            for h, col in enumerate((at, width + at)):
                here = (slice(None), pl.ds(col, w))
                arriving[-1].append(pltpu.make_async_copy(w_hbm.at[here], held.at[here], sems.at[2 * i + h]))
        for copy in rows_in + sum(arriving, []):
            copy.start()
        wait(rows_in)
        leaving = []
        for i, (at, w) in enumerate(parts):
            wait(arriving[i])
            slot = i % 2
            if i > 1:
                wait(leaving[i - 2])
            gate = dot(a_ref[...], held[:, at : at + w])
            stage[slot, 0, :, :w] = gate
            upper = dot(a_ref[...], held[:, width + at : width + at + w])
            stage[slot, 1, :, :w] = upper
            hid_ref[:, at : at + w] = (gate * jax.nn.sigmoid(gate) * upper).astype(BF16)
            leaving.append(
                [
                    pltpu.make_async_copy(
                        stage.at[slot, h, :, pl.ds(0, w)], gu_hbm.at[:, pl.ds(h * width + at, w)], out_sems.at[slot, h]
                    )
                    for h in range(2)
                ]
            )
            for copy in leaving[-1]:
                copy.start()
        for copies in leaving[-2:]:
            wait(copies)

    return run(
        kernel, "gate_rows", 2 + 7 * rows // 384, (weight, *pieces), [ANY] * (1 + count),
        (wide_like(rows, both), low_like(rows, width)), (ANY, WHOLE),
        [
            VMEM((model, both), BF16), VMEM((rows, model), BF16), VMEM((2, 2, rows, 256), F32),
            DMA((2 * len(parts),)), DMA((count,)), DMA((2, 2)),
        ],
        deps,
    )


def gate_back(gate_up, at_rows, eb, down, weight, split, deps):
    pieces, _ = flat(eb)
    count = len(pieces)
    rows = sum(piece.shape[0] for piece in pieces) // 2
    model, both = weight.shape
    width = both // 2
    shares = [rows // 2] * 2 + [rows] if split else [rows] * 2

    def kernel(*refs):
        gu_hbms, (down_hbm, w_hbm), e_hbms = refs[:2], refs[2:4], refs[4 : 4 + count]
        dgu_ref, back_refs, (down_ref, held, gu_ref, e_ref, sems) = refs[4 + count], refs[5 + count : -5], refs[-5:]
        first, row = [pltpu.make_async_copy(down_hbm, down_ref, sems.at[0])], 0
        for j, ref in enumerate(e_hbms):
            first.append(pltpu.make_async_copy(ref, e_ref.at[pl.ds(row, ref.shape[0]), :], sems.at[4 + j]))
            row += ref.shape[0]
        for i in range(2):
            to = gu_ref.at[pl.ds(rows * i, rows), :]
            first.append(pltpu.make_async_copy(gu_hbms[i].at[pl.ds(at_rows[i], rows), :], to, sems.at[2 + i]))
        second = [pltpu.make_async_copy(w_hbm, held, sems.at[1])]
        for copy in first + second:
            copy.start()
        wait(first)
        for at, w in tiles(width):
            back = dot(e_ref[...], down_ref[at : at + w, :], NT)
            gate, upper = gu_ref[:, at : at + w], gu_ref[:, width + at : width + at + w]
            sigma = jax.nn.sigmoid(gate)
            dgu_ref[:, at : at + w] = (back * upper * sigma * (1.0 + gate * (1.0 - sigma))).astype(BF16)
            dgu_ref[:, width + at : width + at + w] = (back * gate * sigma).astype(BF16)
        wait(second)
        for at, w in tiles(model):
            part = dot(dgu_ref[...], held[at : at + w, :], NT).astype(BF16)
            row = 0
            for share, ref in zip(shares, back_refs):
                ref[:, at : at + w] = part[row : row + share]
                row += share

    return run(
        kernel, "gate_back", 22, (*gate_up, down, weight, *pieces), [ANY] * (4 + count),
        (low_like(2 * rows, both),) + tuple(low_like(share, model) for share in shares), (WHOLE,) * (1 + len(shares)),
        [
            VMEM((width, model), BF16), VMEM((model, both), BF16), VMEM((2 * rows, both), F32),
            VMEM((2 * rows, model), BF16), DMA((4 + count,)),
        ],
        deps,
    )


def down_rows(hidden, rows, down, deps):
    width, model = down.shape
    count = len(hidden)
    blocks = [(i, at) for i, h in enumerate(hidden) for at in range(0, h.shape[0], rows)]

    def kernel(down_ref, *refs):
        hid_refs, out_refs = refs[:count], refs[count:]
        for (i, at_row), out_ref in zip(blocks, out_refs):
            for at, w in tiles(model):
                out_ref[:, at : at + w] = dot(hid_refs[i][at_row : at_row + rows], down_ref[:, at : at + w]).astype(BF16)

    return run(
        kernel, "down_rows", 13, (down, *hidden), [WHOLE] * (1 + count),
        (low_like(rows, model),) * len(blocks), (WHOLE,) * len(blocks), after=deps,
    )


def outer_sum(starts, sizes, xs, ys, deps):
    xs, ys = flat(xs)[0], flat(ys)[0]
    height, cols = xs[0].shape[1], ys[0].shape[1]
    rows = sum(x.shape[0] for x in xs)
    half = height // 2
    count, pieces = len(xs), len(sizes)

    def kernel(starts_ref, *refs):
        x_refs, y_refs = refs[:count], refs[count : count + len(ys)]
        keep_ref, piece_refs, (turned, tile) = refs[count + len(ys)], refs[count + len(ys) + 1 : -2], refs[-2:]

        @pl.when(pl.program_id(0) == 0)
        def _():
            base = 0
            for ref in x_refs:
                for at in range(0, height, 128):
                    turned[at : at + 128, base : base + ref.shape[0]] = ref[:, at : at + 128].T
                base += ref.shape[0]

        base = 0
        for ref in y_refs:
            tile[base : base + ref.shape[0], :] = ref[...]
            base += ref.shape[0]
        row, into = 0, []
        for size in sizes:
            into.append(keep_ref.at[pl.ds(row, size), :])
            row += size
        for i, ref in enumerate((*into, *piece_refs)):
            at = pl.multiple_of(starts_ref[i], 16)
            ref[...] = dot(turned[pl.ds(at, sizes[i % pieces]), :], tile[...]).astype(BF16)

    fixed = lambda i, s: (0, 0)
    column = lambda i, s: (0, i)
    return run(
        kernel, "outer_sum", 8 if cols > D else 5, (starts, *xs, *ys),
        [pl.BlockSpec(x.shape, fixed) for x in xs] + [pl.BlockSpec((y.shape[0], 256), column) for y in ys],
        (low_like(half, cols),) + tuple(low_like(size, cols) for size in sizes),
        (pl.BlockSpec((half, 256), column),) + tuple(pl.BlockSpec((size, 256), column) for size in sizes),
        [VMEM((height, rows), BF16), VMEM((rows, 256), BF16)],
        deps, prefetch=1, grid=(cols // 256,), vmem=60,
    )


def adam_attention(grads, weight, first_moment, second_moment, gains, first_gains, second_gains):
    rows, wide = weight.shape
    share = gains.shape[1]

    def kernel(g_ref, w_ref, m_ref, v_ref, gain_ref, gain_m_ref, gain_v_ref, *out_refs):
        for c, w in tiles(wide, 512):
            here = (slice(None), slice(c, c + w))
            state = adam_step(w_ref[here], m_ref[here], v_ref[here], g_ref[here].astype(F32), RATE_MATRIX, DECAY_MATRIX)
            for ref, value in zip(out_refs[:3], state):
                ref[here] = value
        row = g_ref[:16, wide:].astype(F32)
        grad = jnp.concatenate([row[:1], pltpu.roll(row, share, 1)[:1]], axis=0)[:, :share]
        state = adam_step(gain_ref[...], gain_m_ref[...], gain_v_ref[...], grad, RATE_GAIN, 0.0)
        for ref, value in zip(out_refs[3:], state):
            ref[...] = value

    state = (wide_like(rows, wide),) * 3 + (wide_like(2, share),) * 3
    return run(
        kernel, "adam_attention", 3,
        (grads, weight, first_moment, second_moment, gains, first_gains, second_gains), [WHOLE] * 7, state, (WHOLE,) * 6,
    )


def turn(x, cosine, sine):
    lane = lax.broadcasted_iota(jnp.int32, cosine.shape, 1)
    lower = (lane & (HEAD_DIM - 1)) < HEAD_DIM // 2
    out = []
    for j in range(x.shape[1] // 128):
        tile = x[:, 128 * j : 128 * (j + 1)]
        other = jnp.where(lower, pltpu.roll(tile, 96, 1), pltpu.roll(tile, 32, 1))
        out.append(tile * cosine + other * sine)
    return out


def both_halves(tile, which):
    lane = lax.broadcasted_iota(jnp.int32, tile.shape, 1)
    other = pltpu.roll(tile, HEAD_DIM, 1)
    low, high = (tile, other) if which == 0 else (other, tile)
    zero = jnp.zeros_like(tile)
    return jnp.where(lane < HEAD_DIM, low, zero), jnp.where(lane >= HEAD_DIM, high, zero)


PAIRS = HEADS // KV_HEADS // 2
STEP_ROWS = 128


def masked_scores(q, k, seg_q, seg_k, first):
    scores = lax.dot_general(q, k, (((1,), (1,)), ((), ())), preferred_element_type=F32) * HEAD_DIM ** (-0.5)
    pairs, keys = q.shape[0] // STEP_ROWS, k.shape[0]
    rows = lax.broadcasted_iota(jnp.int32, (STEP_ROWS, keys), 0) + first
    cols = lax.broadcasted_iota(jnp.int32, (STEP_ROWS, keys), 1)
    allowed = (seg_q == seg_k) & (cols <= rows)
    scores = jnp.where(allowed[None], scores.reshape(pairs, STEP_ROWS, keys), -1e30)
    raised = jnp.exp(scores - jnp.max(scores, axis=-1, keepdims=True))
    return (raised / jnp.sum(raised, axis=-1, keepdims=True)).reshape(pairs * STEP_ROWS, keys)


def attend(projected, cosine, sine, segment):
    rows = projected.shape[0]
    kv = KV_HEADS * HEAD_DIM

    def kernel(p_ref, cos_ref, sin_ref, segq_ref, segk_ref, q_ref, k_ref, v_ref, o_ref):
        cosine, sine = cos_ref[...], sin_ref[...]
        for j, tile in enumerate(turn(p_ref[:, :D], cosine, sine)):
            q_ref[:, 128 * j : 128 * (j + 1)] = tile.astype(BF16)
        for j, tile in enumerate(turn(p_ref[:, D : D + kv], cosine, sine)):
            k_ref[:, 128 * j : 128 * (j + 1)] = tile.astype(BF16)
        v_ref[...] = p_ref[:, D + kv : D + 2 * kv].astype(BF16)
        for g in range(KV_HEADS):
            tile = slice(128 * (g // 2), 128 * (g // 2 + 1))
            k_low, k_high = both_halves(k_ref[:, tile].astype(F32), g % 2)
            v_low, v_high = both_halves(v_ref[:, tile].astype(F32), g % 2)
            k_low, k_high, v_low, v_high = (x.astype(BF16) for x in (k_low, k_high, v_low, v_high))
            for first in range(0, rows, STEP_ROWS):
                keys = first + STEP_ROWS
                at = lambda j: slice(128 * (g * PAIRS + j), 128 * (g * PAIRS + j + 1))
                q = jnp.concatenate([q_ref[first:keys, at(j)] for j in range(PAIRS)], axis=0)
                seg_q, seg_k = segq_ref[first:keys, :1], segk_ref[:1, :keys]
                low = masked_scores(q, k_low[:keys], seg_q, seg_k, first).astype(BF16)
                high = masked_scores(q, k_high[:keys], seg_q, seg_k, first).astype(BF16)
                out = jnp.dot(low, v_low[:keys], preferred_element_type=F32)
                out = out + jnp.dot(high, v_high[:keys], preferred_element_type=F32)
                for j in range(PAIRS):
                    o_ref[first:keys, at(j)] = out[STEP_ROWS * j : STEP_ROWS * (j + 1)].astype(BF16)

    return run(
        kernel, "attend", 15,
        (projected, cosine, sine, jnp.broadcast_to(segment[:, None], (rows, 128)), jnp.broadcast_to(segment[None], (8, rows))),
        [WHOLE] * 5, (low_like(rows, D), low_like(rows, kv), low_like(rows, kv), low_like(rows, D)), (WHOLE,) * 4,
    )


def attend_back(queries, key_rows, value_rows, attended_back, cosine, sine, segment, deps):
    rows = queries.shape[0]
    kv = KV_HEADS * HEAD_DIM
    factor = HEAD_DIM ** (-0.5)

    def kernel(q_ref, k_ref, v_ref, b_ref, cos_ref, sin_ref, segq_ref, segk_ref, dp_ref, dk_ref, dv_ref):
        cosine, sine = cos_ref[...], -sin_ref[...]
        lane = lax.broadcasted_iota(jnp.int32, (STEP_ROWS, 128), 1)
        contract = lambda a, b: lax.dot_general(a, b, (((0,), (0,)), ((), ())), preferred_element_type=F32)
        for g in range(KV_HEADS):
            tile = slice(128 * (g // 2), 128 * (g // 2 + 1))
            k_low, k_high = both_halves(k_ref[:, tile].astype(F32), g % 2)
            v_low, v_high = both_halves(v_ref[:, tile].astype(F32), g % 2)
            k_low, k_high, v_low, v_high = (x.astype(BF16) for x in (k_low, k_high, v_low, v_high))
            dk_ref[...] = jnp.zeros_like(dk_ref)
            dv_ref[...] = jnp.zeros_like(dv_ref)
            for first in range(0, rows, STEP_ROWS):
                keys = first + STEP_ROWS
                at = lambda j: slice(128 * (g * PAIRS + j), 128 * (g * PAIRS + j + 1))
                q = jnp.concatenate([q_ref[first:keys, at(j)] for j in range(PAIRS)], axis=0)
                b = jnp.concatenate([b_ref[first:keys, at(j)] for j in range(PAIRS)], axis=0)
                seg_q, seg_k = segq_ref[first:keys, :1], segk_ref[:1, :keys]
                dq, dk, dv = None, [], []
                for k_half, v_half in ((k_low, v_low), (k_high, v_high)):
                    probs = masked_scores(q, k_half[:keys], seg_q, seg_k, first)
                    back = lax.dot_general(b, v_half[:keys], (((1,), (1,)), ((), ())), preferred_element_type=F32)
                    inner = jnp.sum(back * probs, axis=-1, keepdims=True)
                    ds = (probs * (back - inner)).astype(BF16)
                    dv.append(contract(probs.astype(BF16), b))
                    dk.append(contract(ds, q))
                    term = jnp.dot(ds, k_half[:keys], preferred_element_type=F32)
                    dq = term if dq is None else dq + term
                low = lax.broadcasted_iota(jnp.int32, (keys, 128), 1) < HEAD_DIM
                dk_ref[:keys] += jnp.where(low, dk[0], dk[1])
                dv_ref[:keys] += jnp.where(low, dv[0], dv[1])
                for j in range(PAIRS):
                    (turned,) = turn(
                        dq[STEP_ROWS * j : STEP_ROWS * (j + 1)] * factor, cosine[first:keys], sine[first:keys]
                    )
                    dp_ref[first:keys, at(j)] = turned.astype(BF16)
            total_k = dk_ref[...] + pltpu.roll(dk_ref[...], HEAD_DIM, 1)
            total_v = dv_ref[...] + pltpu.roll(dv_ref[...], HEAD_DIM, 1)
            (total_k,) = turn(total_k * factor, cosine, sine)
            mine = lax.broadcasted_iota(jnp.int32, (rows, 128), 1) // HEAD_DIM == g % 2
            for base, total in ((D, total_k), (D + kv, total_v)):
                here = slice(base + 128 * (g // 2), base + 128 * (g // 2 + 1))
                if g % 2 == 0:
                    dp_ref[:, here] = total.astype(BF16)
                else:
                    dp_ref[:, here] = jnp.where(mine, total, dp_ref[:, here].astype(F32)).astype(BF16)

    return run(
        kernel, "attend_back", 24,
        (
            queries, key_rows, value_rows, attended_back, cosine, sine,
            jnp.broadcast_to(segment[:, None], (rows, 128)), jnp.broadcast_to(segment[None], (8, rows)),
        ),
        [WHOLE] * 8, low_like(rows, QKV_W), WHOLE, [VMEM((rows, 128), F32)] * 2, deps,
    )


def turning(position):
    frequency = THETA ** (-(jnp.arange(HEAD_DIM // 2, dtype=F32) * 2.0 / HEAD_DIM))
    phases = position.astype(F32)[:, None] * frequency[None, :]
    cosine, sine = jnp.cos(phases), jnp.sin(phases)
    return jnp.concatenate([cosine] * 4, axis=1), jnp.concatenate([-sine, sine] * 2, axis=1)


def rotary(vectors, cosine, sine_part):
    half_dim = HEAD_DIM // 2
    lower_half = vectors[..., :half_dim]
    upper_half = vectors[..., half_dim:]
    return jnp.concatenate(
        [
            lower_half * cosine - upper_half * sine_part,
            upper_half * cosine + lower_half * sine_part,
        ],
        axis=-1,
    )


def any_mesh(
    tokens, cotangent, seq_table, w_qkv, m_qkv, v_qkv, w_out, m_out, v_out, w_gate_up, m_gate_up, v_gate_up,
    w_down, m_down, v_down, norm_gains, m_gains, v_gains,
):
    everyone = ("dp", "fsdp")
    nd = lax.axis_size("dp")
    rows_here = tokens.shape[0]
    kv_width = KV_HEADS * HEAD_DIM
    group_size = HEADS // KV_HEADS
    factor = HEAD_DIM ** (-0.5)
    width = FF // nd
    d_rows = w_gate_up.shape[0]
    einsum = lambda how, a, b: jnp.einsum(how, a, b, preferred_element_type=F32)
    scatter = lambda x, axes, dim: lax.psum_scatter(x.astype(BF16), axes, scatter_dimension=dim, tiled=True)

    segment, position, live_rows = layout(seq_table[0], rows_here)
    row_ids = jnp.arange(rows_here)
    allowed = (segment[:, None] == segment[None, :]) & (row_ids[None, :] <= row_ids[:, None])
    frequency = THETA ** (-(jnp.arange(HEAD_DIM // 2, dtype=F32) * 2.0 / HEAD_DIM))
    phases = position.astype(F32)[:, None] * frequency[None, :]
    cosine, sine = jnp.cos(phases)[:, None, :], jnp.sin(phases)[:, None, :]

    qkv_full = lax.all_gather(w_qkv.astype(BF16), everyone, axis=0, tiled=True)
    out_full = lax.all_gather(w_out.astype(BF16), everyone, axis=0, tiled=True)
    gains_full = lax.all_gather(norm_gains.astype(BF16), everyone, axis=1, tiled=True).astype(F32)
    pieces = w_gate_up.astype(BF16).reshape(d_rows, 2, nd, width).transpose(2, 0, 1, 3).reshape(nd, d_rows, 2 * width)
    gate_up_here = lax.all_to_all(pieces, "dp", 0, 0, tiled=True)
    gate_up_here = lax.all_gather(gate_up_here, "fsdp", axis=1, tiled=True).reshape(D, 2 * width)
    down_here = lax.all_gather(w_down.astype(BF16), "fsdp", axis=0, tiled=True)

    inputs = tokens.astype(F32)
    scale_one = lax.rsqrt(jnp.mean(inputs * inputs, axis=-1, keepdims=True) + EPS_NORM)
    normed_one = inputs * scale_one
    low_one = (normed_one * gains_full[0]).astype(BF16)
    projected = einsum("td,de->te", low_one, qkv_full)
    queries = rotary(projected[:, :D].reshape(rows_here, HEADS, HEAD_DIM), cosine, sine)
    queries = queries.astype(BF16).reshape(rows_here, KV_HEADS, group_size, HEAD_DIM)
    key_rows = rotary(projected[:, D : D + kv_width].reshape(rows_here, KV_HEADS, HEAD_DIM), cosine, sine).astype(BF16)
    value_rows = projected[:, D + kv_width :].reshape(rows_here, KV_HEADS, HEAD_DIM).astype(BF16)
    scores = jnp.where(allowed, einsum("qhgd,khd->hgqk", queries, key_rows) * factor, -1e30)
    raised = jnp.exp(scores - jnp.max(scores, axis=-1, keepdims=True))
    attention = raised / jnp.sum(raised, axis=-1, keepdims=True)
    attention_low = attention.astype(BF16)
    attended = einsum("hgqk,khd->qhgd", attention_low, value_rows).reshape(rows_here, D).astype(BF16)
    middle = inputs + einsum("td,de->te", attended, out_full)
    scale_two = lax.rsqrt(jnp.mean(middle * middle, axis=-1, keepdims=True) + EPS_NORM)
    normed_two = middle * scale_two
    low_two = lax.all_gather((normed_two * gains_full[1]).astype(BF16), "dp", axis=0, tiled=True)

    back_rows = cotangent.astype(F32) * live_rows[:, None].astype(F32)
    down_back = lax.all_gather(back_rows.astype(BF16), "dp", axis=0, tiled=True)
    gate_up = einsum("td,df->tf", low_two, gate_up_here)
    gate, upper = gate_up[:, :width], gate_up[:, width:]
    sigma = jax.nn.sigmoid(gate)
    hidden = (gate * sigma * upper).astype(BF16)
    output = (middle + scatter(einsum("tf,fd->td", hidden, down_here), "dp", 0).astype(F32)).astype(BF16)
    hidden_back = einsum("td,fd->tf", down_back, down_here)
    gate_back = hidden_back * upper * sigma * (1.0 + gate * (1.0 - sigma))
    gate_up_back = jnp.concatenate([gate_back, hidden_back * gate * sigma], axis=1).astype(BF16)
    normed_two_back = scatter(einsum("tf,df->td", gate_up_back, gate_up_here), "dp", 0).astype(F32)
    down_shard = scatter(einsum("tf,td->fd", hidden, down_back), "fsdp", 0).astype(F32)
    gate_up_grad = einsum("td,tf->df", low_two, gate_up_back).reshape(nd, D // nd, 2 * width)
    gate_up_grad = lax.all_to_all(scatter(gate_up_grad, "fsdp", 1), "dp", 0, 0, tiled=True)
    gate_up_shard = gate_up_grad.reshape(nd, d_rows, 2, width).transpose(1, 2, 0, 3).reshape(d_rows, 2 * FF).astype(F32)

    def norm_grad(normed, scale, gain, grad):
        inner = grad * gain
        grad_in = scale * (inner - normed * jnp.mean(inner * normed, axis=-1, keepdims=True))
        return grad_in, jnp.sum(grad * normed, axis=0)

    middle_grad, gain_two_grad = norm_grad(normed_two, scale_two, gains_full[1], normed_two_back)
    middle_grad = back_rows + middle_grad
    branch_back = middle_grad.astype(BF16)
    out_shard = scatter(scatter(einsum("tr,tf->rf", attended, branch_back), "dp", 0), "fsdp", 0).astype(F32)
    attended_back = einsum("te,de->td", branch_back, out_full).astype(BF16)
    attended_back = attended_back.reshape(rows_here, KV_HEADS, group_size, HEAD_DIM)
    prob_back = einsum("qhgd,khd->hgqk", attended_back, value_rows)
    value_back = einsum("hgqk,qhgd->khd", attention_low, attended_back)
    score_back = attention * (prob_back - jnp.sum(prob_back * attention, axis=-1, keepdims=True))
    score_back = score_back.astype(BF16)
    query_back = einsum("hgqk,khd->qhgd", score_back, key_rows) * factor
    key_back = einsum("hgqk,qhgd->khd", score_back, queries) * factor
    query_back = rotary(query_back.reshape(rows_here, HEADS, HEAD_DIM), cosine, -sine).reshape(rows_here, D)
    key_back = rotary(key_back, cosine, -sine).reshape(rows_here, kv_width)
    projected_back = jnp.concatenate([query_back, key_back, value_back.reshape(rows_here, kv_width)], axis=1).astype(BF16)
    qkv_shard = scatter(scatter(einsum("tr,tf->rf", low_one, projected_back), "dp", 0), "fsdp", 0).astype(F32)
    normed_one_back = einsum("te,de->td", projected_back, qkv_full)
    input_norm_back, gain_one_grad = norm_grad(normed_one, scale_one, gains_full[0], normed_one_back)
    input_grad = (middle_grad + input_norm_back).astype(BF16)
    gain_grads = jnp.stack([gain_one_grad, gain_two_grad], axis=1)
    gain_shard = lax.psum_scatter(gain_grads, everyone, scatter_dimension=0, tiled=True).T

    return (
        output,
        input_grad,
        *adam_step(w_qkv, m_qkv, v_qkv, qkv_shard, RATE_MATRIX, DECAY_MATRIX),
        *adam_step(w_out, m_out, v_out, out_shard, RATE_MATRIX, DECAY_MATRIX),
        *adam_step(w_gate_up, m_gate_up, v_gate_up, gate_up_shard, RATE_MATRIX, DECAY_MATRIX),
        *adam_step(w_down, m_down, v_down, down_shard, RATE_MATRIX, DECAY_MATRIX),
        *adam_step(norm_gains, m_gains, v_gains, gain_shard, RATE_GAIN, 0.0),
    )


PLANE = ("tp", "core")


def swap(x, k):
    return lax.ppermute(x, PLANE, [(d, d ^ k) for d in range(8)])


NEAR, FAR = (0, 1, 2, 4, 3, 5), (6, 7)


def gather_plane(own, deps, with_near):
    b = {0: own}
    b[2] = swap(own, 2)
    b[4] = swap(own, 4)
    b[1] = swap(own, 1)
    if deps:
        b[2], b[4] = behind(b[2], *deps), behind(b[4], *deps)
    low, high = halves(b[4], b[2])
    low, high = swap(low, 2), swap(high, 4)
    for k in (2, 4):
        b[k + 1] = swap(b[k], 1)
    near = with_near([b[k] for k in NEAR])
    first = jax.tree.leaves(near)[0]
    b[6] = (behind(low, first), behind(high, first))
    b[7] = (swap(b[6][0], 1), swap(b[6][1], 1))
    return [b[k] for k in range(8)], near


def total(terms):
    return sum(term.astype(F32) for term in terms)


def cube(
    tokens, cotangent, seq_table, w_qkv, m_qkv, v_qkv, w_out, m_out, v_out, w_gate_up, m_gate_up, v_gate_up,
    w_down, m_down, v_down, norm_gains, m_gains, v_gains,
):
    nf = lax.axis_size("fsdp")
    dp_index = lax.axis_index(PLANE)
    dp = dp_index[None]
    core, chip = dp & 1, dp_index >> 1
    rows_here = tokens.shape[0]
    d_rows = w_qkv.shape[0]
    width = FF // 4

    gain_pad = jnp.pad(norm_gains.astype(BF16).reshape(1, 2 * d_rows), ((0, d_rows - 1), (0, 128 - 2 * d_rows)))
    qkv_low = jnp.concatenate([w_qkv.astype(BF16), gain_pad], axis=1)
    qkv_own = lax.all_gather(qkv_low, "fsdp", axis=0, tiled=True)

    segment, position, live_rows = layout(seq_table[0], rows_here)
    cosine, sine = turning(position)
    live = jnp.broadcast_to(live_rows[:, None].astype(F32), (rows_here, 128))
    eb = (cotangent.astype(F32) * live_rows[:, None].astype(F32)).astype(BF16)
    gu_low = lowered(w_gate_up, qkv_low)
    pieces = []
    for k in range(4):
        there = chip ^ k
        piece = jnp.concatenate(
            [lax.dynamic_slice(gu_low, (0, (h * 4 + there) * width), (d_rows, width)) for h in range(2)], axis=1
        )
        pieces.append(swap(piece, 2 * k) if k else piece)
    chips = jnp.stack([chip ^ k for k in range(4)])

    out_own = lax.all_gather(lowered(w_out, *pieces[1:]), "fsdp", axis=0, tiled=True)
    gate_up_here = lax.all_gather(stacked(chips, pieces, qkv_own), ("core", "fsdp"), axis=1, tiled=True)
    gate_up_here = gate_up_here.reshape(D, 2 * width)

    qkv_blocks, near = gather_plane(qkv_own, (), lambda blocks: project(dp, NEAR, tokens, blocks, ()))
    down_here = lax.all_gather(lowered(w_down, qkv_blocks[2], qkv_blocks[4]), ("core", "fsdp"), axis=0, tiled=True)
    projected, low_one, gains = project(dp, FAR, tokens, qkv_blocks[6:], near)
    queries, key_rows, value_rows, attended = attend(projected, cosine, sine, segment)
    out_blocks, near = gather_plane(
        behind(out_own, *qkv_blocks[6]), (attended,),
        lambda blocks: out_part(dp, NEAR, attended, blocks, tokens, ()),
    )
    middle, a2 = out_norm(dp, FAR, attended, out_blocks[6:], near, gains, ())

    a2_x, a2_y = swap(a2, 2), swap(a2, 4)
    a2_low, a2_high = halves(a2_y, a2_x)
    cut = (a2_low, a2_high)
    a2_low, a2_high = swap(a2_low, 2), swap(a2_high, 4)
    gate_up_a, hidden_a = gate_rows((a2, a2_x, a2_y), gate_up_here, cut)
    eb = behind(eb, hidden_a, a2_low, a2_high)
    eb_x, eb_y = swap(eb, 2), swap(eb, 4)
    a2_d = (a2_low, a2_high)
    gate_up_b, hidden_b = gate_rows((a2_d,), gate_up_here, (hidden_a,))
    hidden = (hidden_a, hidden_b)
    half_ff = width // 2
    thirds = (240, 240, 224)
    thirds_at = jnp.concatenate([c * half_ff + at for c in (core, 1 - core) for at in (0, 240, 480)])
    out_own_rows, out_x, out_y, out_d = down_rows(hidden, rows_here, down_here, (hidden_b,))
    eb_low, eb_high = halves(eb_y, eb_x, out_own_rows)
    eb_low, eb_high = swap(eb_low, 2), swap(eb_high, 4)
    eb_d = (eb_low, eb_high)
    weights = (down_here, gate_up_here)
    back_gu_a, back_x, back_own = gate_back(
        (gate_up_a, gate_up_a), (rows_here, 0), (eb_x, eb), *weights, False, (out_own_rows,)
    )
    out_x, out_y = swap(behind(out_x, back_x), 2), swap(behind(out_y, back_x), 4)
    back_gu_b, back_low, back_high, back_y = gate_back(
        (gate_up_b, gate_up_a), (0, 2 * rows_here), (eb_d, eb_y), *weights, True, (back_x,)
    )
    back_low, back_high = swap(back_low, 2), swap(back_high, 4)
    keep, *send = outer_sum(
        thirds_at, thirds, hidden, (eb, eb_x, eb_y, eb_d), (back_y,)
    )
    back_x, back_y = second_sums(back_x, back_y, back_low, back_high, (keep, out_x, out_y))
    send = [swap(behind(piece, back_x), 1) for piece in send]
    (down_grad,) = folded(keep, send, 1, ())
    down_shard = lax.psum_scatter(down_grad, "fsdp", scatter_dimension=0, tiled=True)
    sent_x, sent_y = swap(back_x, 2), swap(back_y, 4)
    chunks_at = jnp.concatenate([2 * t + c for c in (core, 1 - core) for t in range(4)]) * (D // 8)
    keep, *send = outer_sum(chunks_at, (D // 8,) * 4, (a2_x, a2, a2_d, a2_y), (back_gu_a, back_gu_b), (down_grad,))
    wide_back, branch_back, gain_two_grad = middle_back(
        (back_own, sent_x, sent_y), middle, cotangent, live, gains, (keep,)
    )
    send = [swap(behind(piece, sent_x, sent_y, vmem=62), 1) for piece in send]
    gu_grads = folded(keep, send, 2, (branch_back,))
    gu_grads = [grad.reshape(4, D // 8, width) for grad in gu_grads]
    gate_grad, up_grad = (lax.psum_scatter(grad, "fsdp", scatter_dimension=1, tiled=True) for grad in gu_grads)

    out_d = swap(behind(out_d, branch_back), 6)
    *odd, even = blocks_outer(dp, attended, branch_back, (gu_grads[0],))
    odd = [swap(part, 1) for part in odd]
    attended_back = attended_grad(dp, branch_back, out_blocks, (even,))
    low, high, sum_x, sum_y, out_terms = first_sums(even, odd, (attended_back,))
    low, high = swap(low, 2), swap(high, 4)
    projected_back = attend_back(queries, key_rows, value_rows, attended_back, cosine, sine, segment, (sum_x,))
    *odd, even = blocks_outer(dp, low_one, projected_back, (out_d, low, high))
    odd = [swap(part, 1) for part in odd]
    sum_x, sum_y = second_sums(sum_x, sum_y, low, high, (even,))
    out_terms = (out_terms, swap(sum_x, 2), swap(sum_y, 4))
    low, high, sum_x, sum_y, qkv_terms = first_sums(even, odd, (sum_x,))
    low, high = swap(low, 2), swap(high, 4)
    input_grad, gain_one_grad = input_back(dp, projected_back, qkv_blocks, tokens, gains, wide_back, (sum_x,))
    gain_grads = jnp.stack([gain_one_grad[0], gain_two_grad[0]])
    gain_grads = gain_grads + swap(gain_grads, 1)
    sum_x, sum_y = second_sums(sum_x, sum_y, low, high, (input_grad,))
    qkv_terms = (qkv_terms, swap(sum_x, 2), swap(sum_y, 4))
    out_mine = total((behind(out_terms[0], sum_x),) + out_terms[1:]).astype(BF16)
    out_mine = behind(out_mine, up_grad, gate_grad, down_shard)
    out_shard = lax.psum_scatter(out_mine, "fsdp", scatter_dimension=0, tiled=True).astype(F32)

    gain_grads = behind(gain_grads, sum_x)
    down_state = adam_step(
        w_down, m_down, v_down, behind(down_shard, sum_x).astype(F32), RATE_MATRIX, DECAY_MATRIX
    )
    gain_grads = gain_grads + swap(gain_grads, 2) + swap(gain_grads, 4) + swap(gain_grads, 6)
    gain_mine = lax.dynamic_slice(gain_grads, (0, dp_index * (D // 8)), (2, D // 8)).reshape(2, nf, d_rows)
    gain_mine = gain_mine.transpose(1, 0, 2).reshape(nf, 1, 2 * d_rows).astype(BF16)
    gain_mine = jnp.pad(gain_mine, ((0, 0), (0, d_rows - 1), (0, 128 - 2 * d_rows))).reshape(D // 8, 128)
    qkv_mine = jnp.concatenate([total(qkv_terms).astype(BF16), gain_mine], axis=1)
    qkv_grads = lax.psum_scatter(qkv_mine, "fsdp", scatter_dimension=0, tiled=True)
    attention_state = adam_attention(qkv_grads, w_qkv, m_qkv, v_qkv, norm_gains, m_gains, v_gains)
    output = (middle + total((behind(out_own_rows, sum_x), out_x, out_y, out_d))).astype(BF16)

    gate_grad, up_grad = (behind(grad, *qkv_terms[1:]) for grad in (gate_grad, up_grad))
    gate_up_shard = jnp.zeros((d_rows, 2 * FF), BF16)
    for k in range(4):
        there = chip ^ k
        piece = jnp.concatenate(
            [lax.dynamic_slice(grad, (there, 0, 0), (1, d_rows, width))[0] for grad in (gate_grad, up_grad)], axis=1
        )
        if k:
            piece = swap(piece, 2 * k)
        for h in range(2):
            gate_up_shard = lax.dynamic_update_slice(
                gate_up_shard, piece[:, h * width : (h + 1) * width], (0, (h * 4 + there) * width)
            )

    gate_up_state = adam_step(
        w_gate_up, m_gate_up, v_gate_up, gate_up_shard.astype(F32), RATE_MATRIX, DECAY_MATRIX
    )

    return (
        output,
        input_grad,
        *attention_state[:3],
        *adam_step(w_out, m_out, v_out, out_shard, RATE_MATRIX, DECAY_MATRIX),
        *gate_up_state,
        *down_state,
        *attention_state[3:],
    )


def solution(mesh):
    body, axes = any_mesh, ("dp", "fsdp")
    if (mesh.shape["dp"], mesh.shape["fsdp"]) == (8, 4):
        body, axes = cube, ("tp", "core", "fsdp")
        mesh = jax.sharding.Mesh(mesh.devices.reshape(4, 2, 4), axes)
    rows, cols = P(axes, None), P(None, axes)
    in_specs = (rows,) * 15 + (cols,) * 3
    out_specs = (rows,) * 14 + (cols,) * 3
    return jax.shard_map(body, mesh=mesh, in_specs=in_specs, out_specs=out_specs, check_vma=False)
```

```python
import jax
import jax.numpy as jnp
from jax import lax
from jax.experimental import pallas as pl
from jax.experimental.pallas import tpu as pltpu
from jax.sharding import PartitionSpec as P

D = 2048
FF = 5632
HEADS = 32
KV_HEADS = 4
HEAD_DIM = 64
STEP = 10
QKV_W = (HEADS + 2 * KV_HEADS) * HEAD_DIM
PAD = 128


EPS_NORM = 1e-05
BETA_ONE = 0.9
BETA_TWO = 0.999
EPS_ADAM = 1e-08
RATE_MATRIX = 0.02
RATE_GAIN = 0.2
DECAY_MATRIX = 0.1
THETA = 10000.0

BF16 = jnp.bfloat16
F32 = jnp.float32


def layout(lengths, count):
    seq_ends = jnp.cumsum(lengths)
    row_ids = jnp.arange(count, dtype=jnp.int32)
    passed = row_ids[:, None] >= seq_ends[None, :]
    segment = jnp.sum(passed.astype(jnp.int32), axis=1)
    start = jnp.max(jnp.where(passed, seq_ends[None, :], 0), axis=1)
    return (segment, row_ids - start, row_ids < seq_ends[-1])


def adam_step(weight, first_moment, second_moment, gradient, step_rate, weight_decay):
    first_new = BETA_ONE * first_moment + (1.0 - BETA_ONE) * gradient
    second_new = BETA_TWO * second_moment + (1.0 - BETA_TWO) * gradient * gradient
    first_hat = first_new / (1.0 - BETA_ONE**STEP)
    second_hat = second_new / (1.0 - BETA_TWO**STEP)
    updated = weight - step_rate * (
        first_hat / (jnp.sqrt(second_hat) + EPS_ADAM) + weight_decay * weight
    )
    return (first_new, second_new, updated)


VMEM = pltpu.VMEM
ANY = pl.BlockSpec(memory_space=pl.ANY)
WHOLE = pl.BlockSpec(memory_space=pltpu.VMEM)
SCALAR = pl.BlockSpec(memory_space=pltpu.SMEM)
DMA = pltpu.SemaphoreType.DMA
HBM = pl.BlockSpec(memory_space=pltpu.HBM)


def run(
    kernel, name, us, args, in_specs, out_shape, out_specs, scratch=(), after=(), aliases=None, prefetch=0, grid=None, vmem=52
):
    count, ordered = len(args), len(after)

    def body(*refs):
        kernel(*refs[:count], *refs[count + ordered :])

    specs = dict(
        in_specs=list(in_specs) + [ANY] * ordered,
        out_specs=out_specs,
        scratch_shapes=list(scratch),
    )
    if grid and not prefetch:
        specs["grid"] = grid
    if prefetch:
        specs = dict(grid_spec=pltpu.PrefetchScalarGridSpec(num_scalar_prefetch=prefetch, grid=grid, **specs))
    return pl.pallas_call(
        body,
        out_shape=out_shape,
        input_output_aliases=aliases or {},
        compiler_params=pltpu.CompilerParams(vmem_limit_bytes=vmem << 20),
        cost_estimate=pl.CostEstimate(flops=int(us * COST), bytes_accessed=int(us * 1.0e5), transcendentals=0),
        name=name,
        **specs,
    )(*args, *after)


COST = 0.1e9


def low_like(rows, cols):
    return jax.ShapeDtypeStruct((rows, cols), BF16)


def wide_like(rows, cols):
    return jax.ShapeDtypeStruct((rows, cols), F32)


def behind(x, *deps, vmem=52):
    return run(
        lambda x_ref, o_ref: None,
        "behind",
        0.1,
        (x,),
        [HBM],
        jax.ShapeDtypeStruct(x.shape, x.dtype),
        HBM,
        after=deps,
        aliases={0: 0},
        vmem=vmem,
    )


def lowered(x, *deps):
    def kernel(x_ref, o_ref):
        o_ref[...] = x_ref[...].astype(BF16)

    return run(kernel, "lowered", 1, (x,), [WHOLE], low_like(*x.shape), WHOLE, after=deps)


def half_of(x, which, *deps):
    rows = x.shape[0] // 2

    def kernel(x_ref, o_ref, sem):
        copy = pltpu.make_async_copy(x_ref.at[pl.ds(which * rows, rows), :], o_ref, sem)
        copy.start()
        copy.wait()

    return run(kernel, "half_of", 1, (x,), [ANY], low_like(rows, x.shape[1]), WHOLE, [DMA], deps)


def halves(first, second, *deps):
    rows = first.shape[0] // 2

    def kernel(first_ref, second_ref, upper_ref, lower_ref, sems):
        copies = [
            pltpu.make_async_copy(ref.at[pl.ds(i * rows, rows), :], out_ref, sems.at[i])
            for i, (ref, out_ref) in enumerate(((first_ref, upper_ref), (second_ref, lower_ref)))
        ]
        for copy in copies:
            copy.start()
        for copy in copies:
            copy.wait()

    return run(
        kernel, "halves", 1, (first, second), [ANY] * 2, (low_like(rows, first.shape[1]),) * 2, (WHOLE,) * 2,
        [DMA((2,))], deps,
    )


def stacked(slots, pieces, *deps):
    count = len(pieces)

    def kernel(slots_ref, *refs):
        copies = [
            pltpu.make_async_copy(ref, refs[count].at[slots_ref[i]], refs[count + 1].at[i])
            for i, ref in enumerate(refs[:count])
        ]
        for copy in copies:
            copy.start()
        for copy in copies:
            copy.wait()

    return run(
        kernel, "stacked", 1, (slots, *pieces), [SCALAR] + [ANY] * count,
        jax.ShapeDtypeStruct((count, *pieces[0].shape), BF16), WHOLE, [DMA((count,))], deps,
    )


def tiles(width, step=256):
    return [(at, min(step, width - at)) for at in range(0, width, step)]


NT = (((1,), (1,)), ((), ()))
TN = (((0,), (0,)), ((), ()))


def dot(a, b, dims=(((1,), (0,)), ((), ()))):
    return lax.dot_general(a, b, dims, preferred_element_type=F32)


def flat(blocks):
    pieces, places = [], []
    for i, block in enumerate(blocks):
        row = 0
        for piece in block if isinstance(block, tuple) else (block,):
            pieces.append(piece)
            places.append((i, row))
            row += piece.shape[0]
    return pieces, places


def fetch(piece_refs, places, held, sems, width):
    copies = {}
    for j, (ref, (i, row)) in enumerate(zip(piece_refs, places)):
        to = held.at[i, pl.ds(row, ref.shape[0]), :]
        copies.setdefault(i, []).append(pltpu.make_async_copy(ref.at[:, pl.ds(0, width)], to, sems.at[j]))
        copies[i][-1].start()
    return copies


def wait(copies):
    for copy in copies:
        copy.wait()


def row_scale(values):
    return lax.rsqrt(jnp.mean(values * values, axis=-1, keepdims=True) + EPS_NORM)


def project_blocks(dp, ks, x_ref, scale, held, copies, a_ref, g_ref, add):
    _, depth, cols = held.shape
    wide = cols - 128
    first = lax.broadcasted_iota(jnp.int32, (8, 128), 1) < 64
    for i, k in enumerate(ks):
        wait(copies[i])
        base = (dp ^ k) * depth
        for t in range(depth // 128):
            pair = [
                jnp.broadcast_to(held[i, 64 * z : 64 * z + 16, wide:].astype(F32)[:1], (8, 128))
                for z in (2 * t, 2 * t + 1)
            ]
            turned = [pltpu.roll(row, 64, 1) for row in pair]
            at = pl.ds(pl.multiple_of(base + 128 * t, 128), 128)
            g_ref[:8, at] = jnp.where(first, pair[0], turned[1])
            g_ref[8:, at] = jnp.where(first, turned[0], pair[1])
        at = pl.ds(pl.multiple_of(base, depth), depth)
        normed = (x_ref[:, at].astype(F32) * scale * g_ref[:1, at]).astype(BF16)
        a_ref[:, at] = normed
        for c, w in tiles(wide, 512):
            add(i, c, w, dot(normed, held[i, :, c : c + w]))


def project(dp, ks, tokens, blocks, before):
    rows, model = tokens.shape
    pieces, places = flat(blocks)
    depth, cols = model // 8, pieces[0].shape[1]
    count, ahead = len(pieces), len(before)
    wide = cols - 128

    def kernel(dp_ref, x_ref, *refs):
        before_refs, block_refs = refs[:ahead], refs[ahead : ahead + count]
        p_ref, a_ref, g_ref, held, sems = refs[ahead + count :]
        copies = fetch(block_refs, places, held, sems, cols)
        if ahead:
            a_ref[...] = before_refs[1][...]
            g_ref[...] = before_refs[2][...]
        else:
            a_ref[...] = jnp.zeros_like(a_ref)
            g_ref[...] = jnp.zeros_like(g_ref)

        def add(i, c, w, term):
            if i:
                p_ref[:, c : c + w] += term
            elif ahead:
                p_ref[:, c : c + w] = before_refs[0][:, c : c + w] + term
            else:
                p_ref[:, c : c + w] = term

        project_blocks(dp_ref[0], ks, x_ref, row_scale(x_ref[...].astype(F32)), held, copies, a_ref, g_ref, add)

    return run(
        kernel, "project", 5 if ahead else 9, (dp, tokens, *before, *pieces), [SCALAR] + [WHOLE] * (1 + ahead) + [ANY] * count,
        (wide_like(rows, wide), low_like(rows, model), wide_like(16, model)), (WHOLE,) * 3,
        [VMEM((len(blocks), depth, cols), BF16), DMA((count,))],
    )


def out_part(dp, ks, attended, blocks, base, deps):
    rows, model = base.shape
    pieces, places = flat(blocks)
    depth, count = model // 8, len(pieces)

    def kernel(dp_ref, o_ref, x_ref, *refs):
        block_refs, (m_ref, held, sems) = refs[:count], refs[count:]
        copies = fetch(block_refs, places, held, sems, model)
        add_blocks(dp_ref[0], ks, o_ref, x_ref, held, copies, m_ref)

    return run(
        kernel, "out_part", 8, (dp, attended, base, *pieces), [SCALAR] + [WHOLE] * 2 + [ANY] * count,
        wide_like(rows, model), WHOLE, [VMEM((len(blocks), depth, model), BF16), DMA((count,))], deps,
    )


def add_blocks(dp, ks, o_ref, x_ref, held, copies, m_ref):
    _, depth, model = held.shape
    for i, k in enumerate(ks):
        wait(copies[i])
        at = pl.ds(pl.multiple_of((dp ^ k) * depth, depth), depth)
        part = o_ref[:, at]
        for c, w in tiles(model, 512):
            term = dot(part, held[i, :, c : c + w])
            if i == 0:
                m_ref[:, c : c + w] = x_ref[:, c : c + w].astype(F32) + term
            else:
                m_ref[:, c : c + w] += term


def out_norm(dp, ks, attended, blocks, base, gains, deps):
    rows, model = base.shape
    pieces, places = flat(blocks)
    depth, count = model // 8, len(pieces)

    def kernel(dp_ref, o_ref, x_ref, g_ref, *refs):
        block_refs, (m_ref, a_ref, held, sems) = refs[:count], refs[count:]
        copies = fetch(block_refs, places, held, sems, model)
        add_blocks(dp_ref[0], ks, o_ref, x_ref, held, copies, m_ref)
        scale = row_scale(m_ref[...])
        for c, w in tiles(model):
            a_ref[:, c : c + w] = (m_ref[:, c : c + w] * scale * g_ref[8:9, c : c + w]).astype(BF16)

    return run(
        kernel, "out_norm", 6, (dp, attended, base, gains, *pieces), [SCALAR] + [WHOLE] * 3 + [ANY] * count,
        (wide_like(rows, model), low_like(rows, model)), (WHOLE,) * 2,
        [VMEM((len(blocks), depth, model), BF16), DMA((count,))], deps,
    )


def norm_back(values, scale, gain, grads, gain_grad_ref, sums):
    model = gain_grad_ref.shape[1]
    inner = 0.0
    for c, w in tiles(model):
        normed, grad = values(c, w) * scale, grads(c, w)
        gain_grad_ref[:, c : c + w] = jnp.broadcast_to(jnp.sum(grad * normed, axis=0, keepdims=True), (8, w))
        inner = inner + jnp.sum(grad * gain(c, w) * normed, axis=-1, keepdims=True)
    inner = inner / model
    for c, w in tiles(model):
        normed = values(c, w) * scale
        sums(c, w, scale * (grads(c, w) * gain(c, w) - normed * inner))


def middle_back(terms, middle, cotangent, live, gains, deps):
    rows, model = middle.shape
    count = len(terms)

    def kernel(m_ref, c_ref, l_ref, g_ref, *refs):
        term_refs, (wide_ref, low_ref, gain_ref, held) = refs[:count], refs[count:]
        for c, w in tiles(model):
            held[:, c : c + w] = sum(ref[:, c : c + w].astype(F32) for ref in term_refs)
        scale = row_scale(m_ref[...])
        alive = l_ref[:, :1]

        def keep(c, w, grad):
            total = c_ref[:, c : c + w].astype(F32) * alive + grad
            wide_ref[:, c : c + w] = total
            low_ref[:, c : c + w] = total.astype(BF16)

        norm_back(
            lambda c, w: m_ref[:, c : c + w], scale, lambda c, w: g_ref[8:9, c : c + w],
            lambda c, w: held[:, c : c + w], gain_ref, keep,
        )

    return run(
        kernel, "middle_back", 6, (middle, cotangent, live, gains, *terms), [WHOLE] * (4 + count),
        (wide_like(rows, model), low_like(rows, model), wide_like(8, model)), (WHOLE,) * 3,
        [VMEM((rows, model), F32)], deps,
    )


def attended_grad(dp, branch, blocks, deps):
    rows, model = branch.shape
    pieces, places = flat(blocks)
    depth, count = model // 8, len(pieces)

    def kernel(dp_ref, y_ref, *refs):
        block_refs, (out_ref, held, sems) = refs[:count], refs[count:]
        copies = fetch(block_refs, places, held, sems, model)
        for k in range(len(blocks)):
            wait(copies[k])
            at = pl.ds(pl.multiple_of((dp_ref[0] ^ k) * depth, depth), depth)
            out_ref[:, at] = dot(y_ref[...], held[k], NT).astype(BF16)

    return run(
        kernel, "attended_grad", 11, (dp, branch, *pieces), [SCALAR, WHOLE] + [ANY] * count,
        low_like(rows, model), WHOLE, [VMEM((len(blocks), depth, model), BF16), DMA((count,))], deps,
    )


def input_back(dp, grad, blocks, tokens, gains, residual, deps):
    rows, model = tokens.shape
    pieces, places = flat(blocks)
    depth, wide, count = model // 8, grad.shape[1], len(pieces)

    def kernel(dp_ref, y_ref, x_ref, g_ref, r_ref, *refs):
        block_refs, (out_ref, gain_ref, held, total, sems) = refs[:count], refs[count:]
        copies = fetch(block_refs, places, held, sems, wide)
        for k in range(len(blocks)):
            wait(copies[k])
            at = pl.ds(pl.multiple_of((dp_ref[0] ^ k) * depth, depth), depth)
            total[:, at] = dot(y_ref[...], held[k], NT)
        scale = row_scale(x_ref[...].astype(F32))

        def keep(c, w, back):
            out_ref[:, c : c + w] = (r_ref[:, c : c + w] + back).astype(BF16)

        norm_back(
            lambda c, w: x_ref[:, c : c + w].astype(F32), scale, lambda c, w: g_ref[:1, c : c + w],
            lambda c, w: total[:, c : c + w], gain_ref, keep,
        )

    return run(
        kernel, "input_back", 18, (dp, grad, tokens, gains, residual, *pieces), [SCALAR] + [WHOLE] * 4 + [ANY] * count,
        (low_like(rows, model), wide_like(8, model)), (WHOLE,) * 2,
        [VMEM((len(blocks), depth, wide), BF16), VMEM((rows, model), F32), DMA((count,))], deps,
    )


def blocks_outer(dp, x, y, deps):
    rows, cols = y.shape
    depth = x.shape[1] // 8

    def kernel(dp_ref, x_ref, y_ref, *out_refs):
        step = pl.program_id(0)
        term = dot(x_ref[...], y_ref[...], TN).astype(BF16)[None]
        for ref, low, high in zip(out_refs, (0, 2, 4), (2, 4, 8)):

            @pl.when((step >= low) & (step < high))
            def _():
                ref[...] = term

    block = lambda i, dp_ref: dp_ref[0] ^ (jnp.where(i % 4 == 0, 6, jnp.where(i % 4 == 3, 0, 2 * (i % 4))) + 1 - i // 4)
    return run(
        kernel, "blocks_outer", 10, (dp, x, y),
        [
            pl.BlockSpec((rows, depth), lambda i, dp_ref: (0, block(i, dp_ref))),
            pl.BlockSpec((rows, cols), lambda i, dp_ref: (0, 0)),
        ],
        tuple(jax.ShapeDtypeStruct((n, depth, cols), BF16) for n in (2, 2, 4)),
        tuple(
            pl.BlockSpec((1, depth, cols), lambda i, dp_ref, low=low, n=n: (jnp.clip(i - low, 0, n - 1), 0, 0))
            for low, n in ((0, 2), (2, 2), (4, 4))
        ),
        after=deps, prefetch=1, grid=(8,),
    )


def first_sums(even, others, deps):
    _, depth, cols = even.shape
    half = depth // 2

    def kernel(even_ref, first_ref, second_ref, low_ref, high_ref, *refs):
        other = lambda i, at: (first_ref if i < 2 else second_ref)[i % 2, at].astype(F32)
        add = lambda i, at: (even_ref[i, at].astype(F32) + other(i, at)).astype(BF16)
        low_ref[...] = add(0, slice(0, half))
        high_ref[...] = add(0, slice(half, depth))
        for i, ref in enumerate(refs):
            ref[...] = add(i + 1, slice(0, depth))

    return run(
        kernel, "first_sums", 5, (even, *others), [WHOLE] * 3,
        (low_like(half, cols),) * 2 + (low_like(depth, cols),) * 3, (WHOLE,) * 5, after=deps,
    )


def second_sums(x_block, y_block, low, high, deps):
    half, cols = low.shape

    def kernel(x_ref, y_ref, low_ref, high_ref, x_out, y_out):
        add = lambda a, b: (a.astype(F32) + b.astype(F32)).astype(BF16)
        x_out[:half], x_out[half:] = x_ref[:half], add(x_ref[half:], high_ref[...])
        y_out[:half], y_out[half:] = add(y_ref[:half], low_ref[...]), y_ref[half:]

    return run(
        kernel, "second_sums", 2, (x_block, y_block, low, high), [WHOLE] * 4, (low_like(2 * half, cols),) * 2,
        (WHOLE,) * 2, after=deps,
    )


def folded(keep, others, parts, deps):
    rows, cols = keep.shape
    share, count = cols // parts, len(others)

    def kernel(keep_ref, *refs):
        row = 0
        for other_ref in refs[:count]:
            down = slice(row, row + other_ref.shape[0])
            row += other_ref.shape[0]
            for i, ref in enumerate(refs[count:]):
                here = slice(share * i, share * (i + 1))
                ref[down] = (keep_ref[down, here].astype(F32) + other_ref[:, here].astype(F32)).astype(BF16)

    return run(
        kernel, "folded", 2 if parts > 1 else 1, (keep, *others), [WHOLE] * (1 + count), (low_like(rows, share),) * parts,
        (WHOLE,) * parts, after=deps,
    )


def gate_rows(a2, weight, deps):
    pieces, _ = flat(a2)
    count = len(pieces)
    rows = sum(piece.shape[0] for piece in pieces)
    model, both = weight.shape
    width = both // 2
    parts = tiles(width)

    def kernel(w_hbm, *refs):
        a_hbms, (gu_hbm, hid_ref, held, a_ref, stage, sems, a_sems, out_sems) = refs[:count], refs[count:]
        row, rows_in, arriving = 0, [], []
        for i, ref in enumerate(a_hbms):
            rows_in.append(pltpu.make_async_copy(ref, a_ref.at[pl.ds(row, ref.shape[0]), :], a_sems.at[i]))
            row += ref.shape[0]
        for i, (at, w) in enumerate(parts):
            arriving.append([])
            for h, col in enumerate((at, width + at)):
                here = (slice(None), pl.ds(col, w))
                arriving[-1].append(pltpu.make_async_copy(w_hbm.at[here], held.at[here], sems.at[2 * i + h]))
        for copy in rows_in + sum(arriving, []):
            copy.start()
        wait(rows_in)
        leaving = []
        for i, (at, w) in enumerate(parts):
            wait(arriving[i])
            slot = i % 2
            if i > 1:
                wait(leaving[i - 2])
            gate = dot(a_ref[...], held[:, at : at + w])
            stage[slot, 0, :, :w] = gate
            upper = dot(a_ref[...], held[:, width + at : width + at + w])
            stage[slot, 1, :, :w] = upper
            hid_ref[:, at : at + w] = (gate * jax.nn.sigmoid(gate) * upper).astype(BF16)
            leaving.append(
                [
                    pltpu.make_async_copy(
                        stage.at[slot, h, :, pl.ds(0, w)], gu_hbm.at[:, pl.ds(h * width + at, w)], out_sems.at[slot, h]
                    )
                    for h in range(2)
                ]
            )
            for copy in leaving[-1]:
                copy.start()
        for copies in leaving[-2:]:
            wait(copies)

    return run(
        kernel, "gate_rows", 2 + 7 * rows // 384, (weight, *pieces), [ANY] * (1 + count),
        (wide_like(rows, both), low_like(rows, width)), (ANY, WHOLE),
        [
            VMEM((model, both), BF16), VMEM((rows, model), BF16), VMEM((2, 2, rows, 256), F32),
            DMA((2 * len(parts),)), DMA((count,)), DMA((2, 2)),
        ],
        deps,
    )


def gate_back(gate_up, at_rows, eb, down, weight, split, deps):
    pieces, _ = flat(eb)
    count = len(pieces)
    rows = sum(piece.shape[0] for piece in pieces) // 2
    model, both = weight.shape
    width = both // 2
    shares = [rows // 2] * 2 + [rows] if split else [rows] * 2

    def kernel(*refs):
        gu_hbms, (down_hbm, w_hbm), e_hbms = refs[:2], refs[2:4], refs[4 : 4 + count]
        dgu_ref, back_refs, (down_ref, held, gu_ref, e_ref, sems) = refs[4 + count], refs[5 + count : -5], refs[-5:]
        first, row = [pltpu.make_async_copy(down_hbm, down_ref, sems.at[0])], 0
        for j, ref in enumerate(e_hbms):
            first.append(pltpu.make_async_copy(ref, e_ref.at[pl.ds(row, ref.shape[0]), :], sems.at[4 + j]))
            row += ref.shape[0]
        for i in range(2):
            to = gu_ref.at[pl.ds(rows * i, rows), :]
            first.append(pltpu.make_async_copy(gu_hbms[i].at[pl.ds(at_rows[i], rows), :], to, sems.at[2 + i]))
        second = [pltpu.make_async_copy(w_hbm, held, sems.at[1])]
        for copy in first + second:
            copy.start()
        wait(first)
        for at, w in tiles(width):
            back = dot(e_ref[...], down_ref[at : at + w, :], NT)
            gate, upper = gu_ref[:, at : at + w], gu_ref[:, width + at : width + at + w]
            sigma = jax.nn.sigmoid(gate)
            dgu_ref[:, at : at + w] = (back * upper * sigma * (1.0 + gate * (1.0 - sigma))).astype(BF16)
            dgu_ref[:, width + at : width + at + w] = (back * gate * sigma).astype(BF16)
        wait(second)
        for at, w in tiles(model):
            part = dot(dgu_ref[...], held[at : at + w, :], NT).astype(BF16)
            row = 0
            for share, ref in zip(shares, back_refs):
                ref[:, at : at + w] = part[row : row + share]
                row += share

    return run(
        kernel, "gate_back", 22, (*gate_up, down, weight, *pieces), [ANY] * (4 + count),
        (low_like(2 * rows, both),) + tuple(low_like(share, model) for share in shares), (WHOLE,) * (1 + len(shares)),
        [
            VMEM((width, model), BF16), VMEM((model, both), BF16), VMEM((2 * rows, both), F32),
            VMEM((2 * rows, model), BF16), DMA((4 + count,)),
        ],
        deps,
    )


def down_rows(hidden, rows, down, deps):
    width, model = down.shape
    count = len(hidden)
    blocks = [(i, at) for i, h in enumerate(hidden) for at in range(0, h.shape[0], rows)]

    def kernel(down_ref, *refs):
        hid_refs, out_refs = refs[:count], refs[count:]
        for (i, at_row), out_ref in zip(blocks, out_refs):
            for at, w in tiles(model):
                out_ref[:, at : at + w] = dot(hid_refs[i][at_row : at_row + rows], down_ref[:, at : at + w]).astype(BF16)

    return run(
        kernel, "down_rows", 13, (down, *hidden), [WHOLE] * (1 + count),
        (low_like(rows, model),) * len(blocks), (WHOLE,) * len(blocks), after=deps,
    )


def outer_sum(starts, sizes, xs, ys, deps):
    xs, ys = flat(xs)[0], flat(ys)[0]
    height, cols = xs[0].shape[1], ys[0].shape[1]
    rows = sum(x.shape[0] for x in xs)
    half = height // 2
    count, pieces = len(xs), len(sizes)

    def kernel(starts_ref, *refs):
        x_refs, y_refs = refs[:count], refs[count : count + len(ys)]
        keep_ref, piece_refs, (turned, tile) = refs[count + len(ys)], refs[count + len(ys) + 1 : -2], refs[-2:]

        @pl.when(pl.program_id(0) == 0)
        def _():
            base = 0
            for ref in x_refs:
                for at in range(0, height, 128):
                    turned[at : at + 128, base : base + ref.shape[0]] = ref[:, at : at + 128].T
                base += ref.shape[0]

        base = 0
        for ref in y_refs:
            tile[base : base + ref.shape[0], :] = ref[...]
            base += ref.shape[0]
        row, into = 0, []
        for size in sizes:
            into.append(keep_ref.at[pl.ds(row, size), :])
            row += size
        for i, ref in enumerate((*into, *piece_refs)):
            at = pl.multiple_of(starts_ref[i], 16)
            ref[...] = dot(turned[pl.ds(at, sizes[i % pieces]), :], tile[...]).astype(BF16)

    fixed = lambda i, s: (0, 0)
    column = lambda i, s: (0, i)
    return run(
        kernel, "outer_sum", 8 if cols > D else 5, (starts, *xs, *ys),
        [pl.BlockSpec(x.shape, fixed) for x in xs] + [pl.BlockSpec((y.shape[0], 256), column) for y in ys],
        (low_like(half, cols),) + tuple(low_like(size, cols) for size in sizes),
        (pl.BlockSpec((half, 256), column),) + tuple(pl.BlockSpec((size, 256), column) for size in sizes),
        [VMEM((height, rows), BF16), VMEM((rows, 256), BF16)],
        deps, prefetch=1, grid=(cols // 256,), vmem=60,
    )


def adam_attention(grads, weight, first_moment, second_moment, gains, first_gains, second_gains):
    rows, wide = weight.shape
    share = gains.shape[1]

    def kernel(g_ref, w_ref, m_ref, v_ref, gain_ref, gain_m_ref, gain_v_ref, *out_refs):
        for c, w in tiles(wide, 512):
            here = (slice(None), slice(c, c + w))
            state = adam_step(w_ref[here], m_ref[here], v_ref[here], g_ref[here].astype(F32), RATE_MATRIX, DECAY_MATRIX)
            for ref, value in zip(out_refs[:3], state):
                ref[here] = value
        row = g_ref[:16, wide:].astype(F32)
        grad = jnp.concatenate([row[:1], pltpu.roll(row, share, 1)[:1]], axis=0)[:, :share]
        state = adam_step(gain_ref[...], gain_m_ref[...], gain_v_ref[...], grad, RATE_GAIN, 0.0)
        for ref, value in zip(out_refs[3:], state):
            ref[...] = value

    state = (wide_like(rows, wide),) * 3 + (wide_like(2, share),) * 3
    return run(
        kernel, "adam_attention", 3,
        (grads, weight, first_moment, second_moment, gains, first_gains, second_gains), [WHOLE] * 7, state, (WHOLE,) * 6,
    )


def turn(x, cosine, sine):
    lane = lax.broadcasted_iota(jnp.int32, cosine.shape, 1)
    lower = (lane & (HEAD_DIM - 1)) < HEAD_DIM // 2
    out = []
    for j in range(x.shape[1] // 128):
        tile = x[:, 128 * j : 128 * (j + 1)]
        other = jnp.where(lower, pltpu.roll(tile, 96, 1), pltpu.roll(tile, 32, 1))
        out.append(tile * cosine + other * sine)
    return out


def both_halves(tile, which):
    lane = lax.broadcasted_iota(jnp.int32, tile.shape, 1)
    other = pltpu.roll(tile, HEAD_DIM, 1)
    low, high = (tile, other) if which == 0 else (other, tile)
    zero = jnp.zeros_like(tile)
    return jnp.where(lane < HEAD_DIM, low, zero), jnp.where(lane >= HEAD_DIM, high, zero)


PAIRS = HEADS // KV_HEADS // 2
STEP_ROWS = 128


def masked_scores(q, k, seg_q, seg_k, first):
    scores = lax.dot_general(q, k, (((1,), (1,)), ((), ())), preferred_element_type=F32) * HEAD_DIM ** (-0.5)
    pairs, keys = q.shape[0] // STEP_ROWS, k.shape[0]
    rows = lax.broadcasted_iota(jnp.int32, (STEP_ROWS, keys), 0) + first
    cols = lax.broadcasted_iota(jnp.int32, (STEP_ROWS, keys), 1)
    allowed = (seg_q == seg_k) & (cols <= rows)
    scores = jnp.where(allowed[None], scores.reshape(pairs, STEP_ROWS, keys), -1e30)
    raised = jnp.exp(scores - jnp.max(scores, axis=-1, keepdims=True))
    return (raised / jnp.sum(raised, axis=-1, keepdims=True)).reshape(pairs * STEP_ROWS, keys)


def attend(projected, cosine, sine, segment):
    rows = projected.shape[0]
    kv = KV_HEADS * HEAD_DIM

    def kernel(p_ref, cos_ref, sin_ref, segq_ref, segk_ref, q_ref, k_ref, v_ref, o_ref):
        cosine, sine = cos_ref[...], sin_ref[...]
        for j, tile in enumerate(turn(p_ref[:, :D], cosine, sine)):
            q_ref[:, 128 * j : 128 * (j + 1)] = tile.astype(BF16)
        for j, tile in enumerate(turn(p_ref[:, D : D + kv], cosine, sine)):
            k_ref[:, 128 * j : 128 * (j + 1)] = tile.astype(BF16)
        v_ref[...] = p_ref[:, D + kv : D + 2 * kv].astype(BF16)
        for g in range(KV_HEADS):
            tile = slice(128 * (g // 2), 128 * (g // 2 + 1))
            k_low, k_high = both_halves(k_ref[:, tile].astype(F32), g % 2)
            v_low, v_high = both_halves(v_ref[:, tile].astype(F32), g % 2)
            k_low, k_high, v_low, v_high = (x.astype(BF16) for x in (k_low, k_high, v_low, v_high))
            for first in range(0, rows, STEP_ROWS):
                keys = first + STEP_ROWS
                at = lambda j: slice(128 * (g * PAIRS + j), 128 * (g * PAIRS + j + 1))
                q = jnp.concatenate([q_ref[first:keys, at(j)] for j in range(PAIRS)], axis=0)
                seg_q, seg_k = segq_ref[first:keys, :1], segk_ref[:1, :keys]
                low = masked_scores(q, k_low[:keys], seg_q, seg_k, first).astype(BF16)
                high = masked_scores(q, k_high[:keys], seg_q, seg_k, first).astype(BF16)
                out = jnp.dot(low, v_low[:keys], preferred_element_type=F32)
                out = out + jnp.dot(high, v_high[:keys], preferred_element_type=F32)
                for j in range(PAIRS):
                    o_ref[first:keys, at(j)] = out[STEP_ROWS * j : STEP_ROWS * (j + 1)].astype(BF16)

    return run(
        kernel, "attend", 15,
        (projected, cosine, sine, jnp.broadcast_to(segment[:, None], (rows, 128)), jnp.broadcast_to(segment[None], (8, rows))),
        [WHOLE] * 5, (low_like(rows, D), low_like(rows, kv), low_like(rows, kv), low_like(rows, D)), (WHOLE,) * 4,
    )


def attend_back(queries, key_rows, value_rows, attended_back, cosine, sine, segment, deps):
    rows = queries.shape[0]
    kv = KV_HEADS * HEAD_DIM
    factor = HEAD_DIM ** (-0.5)

    def kernel(q_ref, k_ref, v_ref, b_ref, cos_ref, sin_ref, segq_ref, segk_ref, dp_ref, dk_ref, dv_ref):
        cosine, sine = cos_ref[...], -sin_ref[...]
        lane = lax.broadcasted_iota(jnp.int32, (STEP_ROWS, 128), 1)
        contract = lambda a, b: lax.dot_general(a, b, (((0,), (0,)), ((), ())), preferred_element_type=F32)
        for g in range(KV_HEADS):
            tile = slice(128 * (g // 2), 128 * (g // 2 + 1))
            k_low, k_high = both_halves(k_ref[:, tile].astype(F32), g % 2)
            v_low, v_high = both_halves(v_ref[:, tile].astype(F32), g % 2)
            k_low, k_high, v_low, v_high = (x.astype(BF16) for x in (k_low, k_high, v_low, v_high))
            dk_ref[...] = jnp.zeros_like(dk_ref)
            dv_ref[...] = jnp.zeros_like(dv_ref)
            for first in range(0, rows, STEP_ROWS):
                keys = first + STEP_ROWS
                at = lambda j: slice(128 * (g * PAIRS + j), 128 * (g * PAIRS + j + 1))
                q = jnp.concatenate([q_ref[first:keys, at(j)] for j in range(PAIRS)], axis=0)
                b = jnp.concatenate([b_ref[first:keys, at(j)] for j in range(PAIRS)], axis=0)
                seg_q, seg_k = segq_ref[first:keys, :1], segk_ref[:1, :keys]
                dq, dk, dv = None, [], []
                for k_half, v_half in ((k_low, v_low), (k_high, v_high)):
                    probs = masked_scores(q, k_half[:keys], seg_q, seg_k, first)
                    back = lax.dot_general(b, v_half[:keys], (((1,), (1,)), ((), ())), preferred_element_type=F32)
                    inner = jnp.sum(back * probs, axis=-1, keepdims=True)
                    ds = (probs * (back - inner)).astype(BF16)
                    dv.append(contract(probs.astype(BF16), b))
                    dk.append(contract(ds, q))
                    term = jnp.dot(ds, k_half[:keys], preferred_element_type=F32)
                    dq = term if dq is None else dq + term
                low = lax.broadcasted_iota(jnp.int32, (keys, 128), 1) < HEAD_DIM
                dk_ref[:keys] += jnp.where(low, dk[0], dk[1])
                dv_ref[:keys] += jnp.where(low, dv[0], dv[1])
                for j in range(PAIRS):
                    (turned,) = turn(
                        dq[STEP_ROWS * j : STEP_ROWS * (j + 1)] * factor, cosine[first:keys], sine[first:keys]
                    )
                    dp_ref[first:keys, at(j)] = turned.astype(BF16)
            total_k = dk_ref[...] + pltpu.roll(dk_ref[...], HEAD_DIM, 1)
            total_v = dv_ref[...] + pltpu.roll(dv_ref[...], HEAD_DIM, 1)
            (total_k,) = turn(total_k * factor, cosine, sine)
            mine = lax.broadcasted_iota(jnp.int32, (rows, 128), 1) // HEAD_DIM == g % 2
            for base, total in ((D, total_k), (D + kv, total_v)):
                here = slice(base + 128 * (g // 2), base + 128 * (g // 2 + 1))
                if g % 2 == 0:
                    dp_ref[:, here] = total.astype(BF16)
                else:
                    dp_ref[:, here] = jnp.where(mine, total, dp_ref[:, here].astype(F32)).astype(BF16)

    return run(
        kernel, "attend_back", 24,
        (
            queries, key_rows, value_rows, attended_back, cosine, sine,
            jnp.broadcast_to(segment[:, None], (rows, 128)), jnp.broadcast_to(segment[None], (8, rows)),
        ),
        [WHOLE] * 8, low_like(rows, QKV_W), WHOLE, [VMEM((rows, 128), F32)] * 2, deps, vmem=28,
    )


def turning(position):
    frequency = THETA ** (-(jnp.arange(HEAD_DIM // 2, dtype=F32) * 2.0 / HEAD_DIM))
    phases = position.astype(F32)[:, None] * frequency[None, :]
    cosine, sine = jnp.cos(phases), jnp.sin(phases)
    return jnp.concatenate([cosine] * 4, axis=1), jnp.concatenate([-sine, sine] * 2, axis=1)


def rotary(vectors, cosine, sine_part):
    half_dim = HEAD_DIM // 2
    lower_half = vectors[..., :half_dim]
    upper_half = vectors[..., half_dim:]
    return jnp.concatenate(
        [
            lower_half * cosine - upper_half * sine_part,
            upper_half * cosine + lower_half * sine_part,
        ],
        axis=-1,
    )


def any_mesh(
    tokens, cotangent, seq_table, w_qkv, m_qkv, v_qkv, w_out, m_out, v_out, w_gate_up, m_gate_up, v_gate_up,
    w_down, m_down, v_down, norm_gains, m_gains, v_gains,
):
    everyone = ("dp", "fsdp")
    nd = lax.axis_size("dp")
    rows_here = tokens.shape[0]
    kv_width = KV_HEADS * HEAD_DIM
    group_size = HEADS // KV_HEADS
    factor = HEAD_DIM ** (-0.5)
    width = FF // nd
    d_rows = w_gate_up.shape[0]
    einsum = lambda how, a, b: jnp.einsum(how, a, b, preferred_element_type=F32)
    scatter = lambda x, axes, dim: lax.psum_scatter(x.astype(BF16), axes, scatter_dimension=dim, tiled=True)

    segment, position, live_rows = layout(seq_table[0], rows_here)
    row_ids = jnp.arange(rows_here)
    allowed = (segment[:, None] == segment[None, :]) & (row_ids[None, :] <= row_ids[:, None])
    frequency = THETA ** (-(jnp.arange(HEAD_DIM // 2, dtype=F32) * 2.0 / HEAD_DIM))
    phases = position.astype(F32)[:, None] * frequency[None, :]
    cosine, sine = jnp.cos(phases)[:, None, :], jnp.sin(phases)[:, None, :]

    qkv_full = lax.all_gather(w_qkv.astype(BF16), everyone, axis=0, tiled=True)
    out_full = lax.all_gather(w_out.astype(BF16), everyone, axis=0, tiled=True)
    gains_full = lax.all_gather(norm_gains.astype(BF16), everyone, axis=1, tiled=True).astype(F32)
    pieces = w_gate_up.astype(BF16).reshape(d_rows, 2, nd, width).transpose(2, 0, 1, 3).reshape(nd, d_rows, 2 * width)
    gate_up_here = lax.all_to_all(pieces, "dp", 0, 0, tiled=True)
    gate_up_here = lax.all_gather(gate_up_here, "fsdp", axis=1, tiled=True).reshape(D, 2 * width)
    down_here = lax.all_gather(w_down.astype(BF16), "fsdp", axis=0, tiled=True)

    inputs = tokens.astype(F32)
    scale_one = lax.rsqrt(jnp.mean(inputs * inputs, axis=-1, keepdims=True) + EPS_NORM)
    normed_one = inputs * scale_one
    low_one = (normed_one * gains_full[0]).astype(BF16)
    projected = einsum("td,de->te", low_one, qkv_full)
    queries = rotary(projected[:, :D].reshape(rows_here, HEADS, HEAD_DIM), cosine, sine)
    queries = queries.astype(BF16).reshape(rows_here, KV_HEADS, group_size, HEAD_DIM)
    key_rows = rotary(projected[:, D : D + kv_width].reshape(rows_here, KV_HEADS, HEAD_DIM), cosine, sine).astype(BF16)
    value_rows = projected[:, D + kv_width :].reshape(rows_here, KV_HEADS, HEAD_DIM).astype(BF16)
    scores = jnp.where(allowed, einsum("qhgd,khd->hgqk", queries, key_rows) * factor, -1e30)
    raised = jnp.exp(scores - jnp.max(scores, axis=-1, keepdims=True))
    attention = raised / jnp.sum(raised, axis=-1, keepdims=True)
    attention_low = attention.astype(BF16)
    attended = einsum("hgqk,khd->qhgd", attention_low, value_rows).reshape(rows_here, D).astype(BF16)
    middle = inputs + einsum("td,de->te", attended, out_full)
    scale_two = lax.rsqrt(jnp.mean(middle * middle, axis=-1, keepdims=True) + EPS_NORM)
    normed_two = middle * scale_two
    low_two = lax.all_gather((normed_two * gains_full[1]).astype(BF16), "dp", axis=0, tiled=True)

    back_rows = cotangent.astype(F32) * live_rows[:, None].astype(F32)
    down_back = lax.all_gather(back_rows.astype(BF16), "dp", axis=0, tiled=True)
    gate_up = einsum("td,df->tf", low_two, gate_up_here)
    gate, upper = gate_up[:, :width], gate_up[:, width:]
    sigma = jax.nn.sigmoid(gate)
    hidden = (gate * sigma * upper).astype(BF16)
    output = (middle + scatter(einsum("tf,fd->td", hidden, down_here), "dp", 0).astype(F32)).astype(BF16)
    hidden_back = einsum("td,fd->tf", down_back, down_here)
    gate_back = hidden_back * upper * sigma * (1.0 + gate * (1.0 - sigma))
    gate_up_back = jnp.concatenate([gate_back, hidden_back * gate * sigma], axis=1).astype(BF16)
    normed_two_back = scatter(einsum("tf,df->td", gate_up_back, gate_up_here), "dp", 0).astype(F32)
    down_shard = scatter(einsum("tf,td->fd", hidden, down_back), "fsdp", 0).astype(F32)
    gate_up_grad = einsum("td,tf->df", low_two, gate_up_back).reshape(nd, D // nd, 2 * width)
    gate_up_grad = lax.all_to_all(scatter(gate_up_grad, "fsdp", 1), "dp", 0, 0, tiled=True)
    gate_up_shard = gate_up_grad.reshape(nd, d_rows, 2, width).transpose(1, 2, 0, 3).reshape(d_rows, 2 * FF).astype(F32)

    def norm_grad(normed, scale, gain, grad):
        inner = grad * gain
        grad_in = scale * (inner - normed * jnp.mean(inner * normed, axis=-1, keepdims=True))
        return grad_in, jnp.sum(grad * normed, axis=0)

    middle_grad, gain_two_grad = norm_grad(normed_two, scale_two, gains_full[1], normed_two_back)
    middle_grad = back_rows + middle_grad
    branch_back = middle_grad.astype(BF16)
    out_shard = scatter(scatter(einsum("tr,tf->rf", attended, branch_back), "dp", 0), "fsdp", 0).astype(F32)
    attended_back = einsum("te,de->td", branch_back, out_full).astype(BF16)
    attended_back = attended_back.reshape(rows_here, KV_HEADS, group_size, HEAD_DIM)
    prob_back = einsum("qhgd,khd->hgqk", attended_back, value_rows)
    value_back = einsum("hgqk,qhgd->khd", attention_low, attended_back)
    score_back = attention * (prob_back - jnp.sum(prob_back * attention, axis=-1, keepdims=True))
    score_back = score_back.astype(BF16)
    query_back = einsum("hgqk,khd->qhgd", score_back, key_rows) * factor
    key_back = einsum("hgqk,qhgd->khd", score_back, queries) * factor
    query_back = rotary(query_back.reshape(rows_here, HEADS, HEAD_DIM), cosine, -sine).reshape(rows_here, D)
    key_back = rotary(key_back, cosine, -sine).reshape(rows_here, kv_width)
    projected_back = jnp.concatenate([query_back, key_back, value_back.reshape(rows_here, kv_width)], axis=1).astype(BF16)
    qkv_shard = scatter(scatter(einsum("tr,tf->rf", low_one, projected_back), "dp", 0), "fsdp", 0).astype(F32)
    normed_one_back = einsum("te,de->td", projected_back, qkv_full)
    input_norm_back, gain_one_grad = norm_grad(normed_one, scale_one, gains_full[0], normed_one_back)
    input_grad = (middle_grad + input_norm_back).astype(BF16)
    gain_grads = jnp.stack([gain_one_grad, gain_two_grad], axis=1)
    gain_shard = lax.psum_scatter(gain_grads, everyone, scatter_dimension=0, tiled=True).T

    return (
        output,
        input_grad,
        *adam_step(w_qkv, m_qkv, v_qkv, qkv_shard, RATE_MATRIX, DECAY_MATRIX),
        *adam_step(w_out, m_out, v_out, out_shard, RATE_MATRIX, DECAY_MATRIX),
        *adam_step(w_gate_up, m_gate_up, v_gate_up, gate_up_shard, RATE_MATRIX, DECAY_MATRIX),
        *adam_step(w_down, m_down, v_down, down_shard, RATE_MATRIX, DECAY_MATRIX),
        *adam_step(norm_gains, m_gains, v_gains, gain_shard, RATE_GAIN, 0.0),
    )


PLANE = ("tp", "core")


def swap(x, k):
    return lax.ppermute(x, PLANE, [(d, d ^ k) for d in range(8)])


NEAR, FAR = (0, 1, 2, 4, 3, 5), (6, 7)


def gather_plane(own, deps, with_near):
    b = {0: own}
    b[2] = swap(own, 2)
    b[4] = swap(own, 4)
    b[1] = swap(own, 1)
    if deps:
        b[2], b[4] = behind(b[2], *deps), behind(b[4], *deps)
    low, high = halves(b[4], b[2])
    low, high = swap(low, 2), swap(high, 4)
    for k in (2, 4):
        b[k + 1] = swap(b[k], 1)
    near = with_near([b[k] for k in NEAR])
    first = jax.tree.leaves(near)[0]
    b[6] = (behind(low, first), behind(high, first))
    b[7] = (swap(b[6][0], 1), swap(b[6][1], 1))
    return [b[k] for k in range(8)], near


def total(terms):
    return sum(term.astype(F32) for term in terms)


def cube(
    tokens, cotangent, seq_table, w_qkv, m_qkv, v_qkv, w_out, m_out, v_out, w_gate_up, m_gate_up, v_gate_up,
    w_down, m_down, v_down, norm_gains, m_gains, v_gains,
):
    nf = lax.axis_size("fsdp")
    dp_index = lax.axis_index(PLANE)
    dp = dp_index[None]
    core, chip = dp & 1, dp_index >> 1
    rows_here = tokens.shape[0]
    d_rows = w_qkv.shape[0]
    width = FF // 4

    gain_pad = jnp.pad(norm_gains.astype(BF16).reshape(1, 2 * d_rows), ((0, d_rows - 1), (0, 128 - 2 * d_rows)))
    qkv_low = jnp.concatenate([w_qkv.astype(BF16), gain_pad], axis=1)
    qkv_own = lax.all_gather(qkv_low, "fsdp", axis=0, tiled=True)

    segment, position, live_rows = layout(seq_table[0], rows_here)
    cosine, sine = turning(position)
    live = jnp.broadcast_to(live_rows[:, None].astype(F32), (rows_here, 128))
    eb = (cotangent.astype(F32) * live_rows[:, None].astype(F32)).astype(BF16)
    gu_low = lowered(w_gate_up, qkv_low)
    pieces = []
    for k in range(4):
        there = chip ^ k
        piece = jnp.concatenate(
            [lax.dynamic_slice(gu_low, (0, (h * 4 + there) * width), (d_rows, width)) for h in range(2)], axis=1
        )
        pieces.append(swap(piece, 2 * k) if k else piece)
    chips = jnp.stack([chip ^ k for k in range(4)])

    out_low = lowered(w_out, *pieces[1:])
    out_own = lax.all_gather(out_low, "fsdp", axis=0, tiled=True)
    gate_up_here = lax.all_gather(stacked(chips, pieces, out_low), ("core", "fsdp"), axis=1, tiled=True)
    gate_up_here = gate_up_here.reshape(D, 2 * width)

    qkv_blocks, near = gather_plane(qkv_own, (), lambda blocks: project(dp, NEAR, tokens, blocks, ()))
    down_here = lax.all_gather(lowered(w_down, qkv_blocks[2], qkv_blocks[4]), ("core", "fsdp"), axis=0, tiled=True)
    projected, low_one, gains = project(dp, FAR, tokens, qkv_blocks[6:], near)
    queries, key_rows, value_rows, attended = attend(projected, cosine, sine, segment)
    out_blocks, near = gather_plane(
        behind(out_own, *qkv_blocks[6]), (attended,),
        lambda blocks: out_part(dp, NEAR, attended, blocks, tokens, ()),
    )
    middle, a2 = out_norm(dp, FAR, attended, out_blocks[6:], near, gains, ())

    a2_x, a2_y = swap(a2, 2), swap(a2, 4)
    a2_low, a2_high = halves(a2_y, a2_x)
    cut = (a2_low, a2_high)
    a2_low, a2_high = swap(a2_low, 2), swap(a2_high, 4)
    gate_up_a, hidden_a = gate_rows((a2, a2_x, a2_y), gate_up_here, cut)
    eb = behind(eb, hidden_a, a2_low, a2_high)
    eb_x, eb_y = swap(eb, 2), swap(eb, 4)
    a2_d = (a2_low, a2_high)
    gate_up_b, hidden_b = gate_rows((a2_d,), gate_up_here, (hidden_a,))
    hidden = (hidden_a, hidden_b)
    half_ff = width // 2
    thirds = (240, 240, 224)
    thirds_at = jnp.concatenate([c * half_ff + at for c in (core, 1 - core) for at in (0, 240, 480)])
    out_own_rows, out_x, out_y, out_d = down_rows(hidden, rows_here, down_here, (hidden_b,))
    eb_low, eb_high = halves(eb_y, eb_x, out_own_rows)
    eb_low, eb_high = swap(eb_low, 2), swap(eb_high, 4)
    eb_d = (eb_low, eb_high)
    weights = (down_here, gate_up_here)
    back_gu_a, back_x, back_own = gate_back(
        (gate_up_a, gate_up_a), (rows_here, 0), (eb_x, eb), *weights, False, (out_own_rows,)
    )
    out_x, out_y = swap(behind(out_x, back_x), 2), swap(behind(out_y, back_x), 4)
    back_gu_b, back_low, back_high, back_y = gate_back(
        (gate_up_b, gate_up_a), (0, 2 * rows_here), (eb_d, eb_y), *weights, True, (back_x,)
    )
    back_low, back_high = swap(back_low, 2), swap(back_high, 4)
    keep, *send = outer_sum(
        thirds_at, thirds, hidden, (eb, eb_x, eb_y, eb_d), (back_y,)
    )
    back_x, back_y = second_sums(back_x, back_y, back_low, back_high, (keep, out_x, out_y))
    send = [swap(behind(piece, back_x), 1) for piece in send]
    (down_grad,) = folded(keep, send, 1, ())
    down_shard = lax.psum_scatter(down_grad, "fsdp", scatter_dimension=0, tiled=True)
    sent_x, sent_y = swap(back_x, 2), swap(back_y, 4)
    chunks_at = jnp.concatenate([2 * t + c for c in (core, 1 - core) for t in range(4)]) * (D // 8)
    keep, *send = outer_sum(chunks_at, (D // 8,) * 4, (a2_x, a2, a2_d, a2_y), (back_gu_a, back_gu_b), (down_grad,))
    wide_back, branch_back, gain_two_grad = middle_back(
        (back_own, sent_x, sent_y), middle, cotangent, live, gains, (keep,)
    )
    send = [swap(behind(piece, sent_x, sent_y, vmem=62), 1) for piece in send]
    gu_grads = folded(keep, send, 2, (branch_back,))
    gu_grads = [grad.reshape(4, D // 8, width) for grad in gu_grads]
    gate_grad, up_grad = (lax.psum_scatter(grad, "fsdp", scatter_dimension=1, tiled=True) for grad in gu_grads)

    out_d = swap(behind(out_d, branch_back), 6)
    *odd, even = blocks_outer(dp, attended, branch_back, (gu_grads[0],))
    odd = [swap(part, 1) for part in odd]
    attended_back = attended_grad(dp, branch_back, out_blocks, (even,))
    low, high, sum_x, sum_y, out_terms = first_sums(even, odd, (attended_back,))
    low, high = swap(low, 2), swap(high, 4)
    projected_back = attend_back(queries, key_rows, value_rows, attended_back, cosine, sine, segment, (sum_x,))
    sum_x, sum_y = second_sums(sum_x, sum_y, low, high, (projected_back,))
    out_terms = (out_terms, swap(sum_x, 2), swap(sum_y, 4))
    *odd, even = blocks_outer(dp, low_one, projected_back, (out_d, sum_x))
    odd = [swap(part, 1) for part in odd]
    low, high, sum_x, sum_y, qkv_terms = first_sums(even, odd, (sum_x,))
    low, high = swap(low, 2), swap(high, 4)
    input_grad, gain_one_grad = input_back(dp, projected_back, qkv_blocks, tokens, gains, wide_back, (sum_x,))
    gain_grads = jnp.stack([gain_one_grad[0], gain_two_grad[0]])
    gain_grads = gain_grads + swap(gain_grads, 1)
    sum_x, sum_y = second_sums(sum_x, sum_y, low, high, (input_grad,))
    qkv_terms = (qkv_terms, swap(sum_x, 2), swap(sum_y, 4))
    out_mine = total((behind(out_terms[0], sum_x),) + out_terms[1:]).astype(BF16)
    out_mine = behind(out_mine, up_grad, gate_grad, down_shard)
    out_sum = lax.psum_scatter(out_mine, "fsdp", scatter_dimension=0, tiled=True)
    out_shard = out_sum.astype(F32)

    gain_grads = behind(gain_grads, out_mine)
    gain_grads = gain_grads + swap(gain_grads, 2) + swap(gain_grads, 4) + swap(gain_grads, 6)
    gain_mine = lax.dynamic_slice(gain_grads, (0, dp_index * (D // 8)), (2, D // 8)).reshape(2, nf, d_rows)
    gain_mine = gain_mine.transpose(1, 0, 2).reshape(nf, 1, 2 * d_rows).astype(BF16)
    gain_mine = jnp.pad(gain_mine, ((0, 0), (0, d_rows - 1), (0, 128 - 2 * d_rows))).reshape(D // 8, 128)
    qkv_mine = jnp.concatenate([total(qkv_terms).astype(BF16), gain_mine], axis=1)
    qkv_grads = lax.psum_scatter(qkv_mine, "fsdp", scatter_dimension=0, tiled=True)
    attention_state = adam_attention(qkv_grads, w_qkv, m_qkv, v_qkv, norm_gains, m_gains, v_gains)

    down_state = adam_step(
        w_down, m_down, v_down, behind(down_shard, qkv_mine).astype(F32), RATE_MATRIX, DECAY_MATRIX
    )

    gate_grad, up_grad = (behind(grad, qkv_mine, out_sum) for grad in (gate_grad, up_grad))
    gate_up_shard = jnp.zeros((d_rows, 2 * FF), BF16)
    for k in range(4):
        there = chip ^ k
        piece = jnp.concatenate(
            [lax.dynamic_slice(grad, (there, 0, 0), (1, d_rows, width))[0] for grad in (gate_grad, up_grad)], axis=1
        )
        if k:
            piece = swap(piece, 2 * k)
        for h in range(2):
            gate_up_shard = lax.dynamic_update_slice(
                gate_up_shard, piece[:, h * width : (h + 1) * width], (0, (h * 4 + there) * width)
            )

    output = (middle + total((behind(out_own_rows, piece), out_x, out_y, out_d))).astype(BF16)
    gate_up_state = adam_step(
        w_gate_up, m_gate_up, v_gate_up, gate_up_shard.astype(F32), RATE_MATRIX, DECAY_MATRIX
    )

    return (
        output,
        input_grad,
        *attention_state[:3],
        *adam_step(w_out, m_out, v_out, out_shard, RATE_MATRIX, DECAY_MATRIX),
        *gate_up_state,
        *down_state,
        *attention_state[3:],
    )


def solution(mesh):
    body, axes = any_mesh, ("dp", "fsdp")
    if (mesh.shape["dp"], mesh.shape["fsdp"]) == (8, 4):
        body, axes = cube, ("tp", "core", "fsdp")
        mesh = jax.sharding.Mesh(mesh.devices.reshape(4, 2, 4), axes)
    rows, cols = P(axes, None), P(None, axes)
    in_specs = (rows,) * 15 + (cols,) * 3
    out_specs = (rows,) * 14 + (cols,) * 3
    return jax.shard_map(body, mesh=mesh, in_specs=in_specs, out_specs=out_specs, check_vma=False)
```

```python
import jax
import jax.numpy as jnp
from jax import lax
from jax.experimental import pallas as pl
from jax.experimental.pallas import tpu as pltpu
from jax.sharding import PartitionSpec as P

D = 2048
FF = 5632
HEADS = 32
KV_HEADS = 4
HEAD_DIM = 64
STEP = 10
QKV_W = (HEADS + 2 * KV_HEADS) * HEAD_DIM
PAD = 128


EPS_NORM = 1e-05
BETA_ONE = 0.9
BETA_TWO = 0.999
EPS_ADAM = 1e-08
RATE_MATRIX = 0.02
RATE_GAIN = 0.2
DECAY_MATRIX = 0.1
THETA = 10000.0

BF16 = jnp.bfloat16
F32 = jnp.float32


def layout(lengths, count):
    seq_ends = jnp.cumsum(lengths)
    row_ids = jnp.arange(count, dtype=jnp.int32)
    passed = row_ids[:, None] >= seq_ends[None, :]
    segment = jnp.sum(passed.astype(jnp.int32), axis=1)
    start = jnp.max(jnp.where(passed, seq_ends[None, :], 0), axis=1)
    return (segment, row_ids - start, row_ids < seq_ends[-1])


def adam_step(weight, first_moment, second_moment, gradient, step_rate, weight_decay):
    first_new = BETA_ONE * first_moment + (1.0 - BETA_ONE) * gradient
    second_new = BETA_TWO * second_moment + (1.0 - BETA_TWO) * gradient * gradient
    first_hat = first_new / (1.0 - BETA_ONE**STEP)
    second_hat = second_new / (1.0 - BETA_TWO**STEP)
    updated = weight - step_rate * (
        first_hat / (jnp.sqrt(second_hat) + EPS_ADAM) + weight_decay * weight
    )
    return (first_new, second_new, updated)


VMEM = pltpu.VMEM
ANY = pl.BlockSpec(memory_space=pl.ANY)
WHOLE = pl.BlockSpec(memory_space=pltpu.VMEM)
SCALAR = pl.BlockSpec(memory_space=pltpu.SMEM)
DMA = pltpu.SemaphoreType.DMA
HBM = pl.BlockSpec(memory_space=pltpu.HBM)


def run(
    kernel, name, us, args, in_specs, out_shape, out_specs, scratch=(), after=(), aliases=None, prefetch=0, grid=None, vmem=52
):
    count, ordered = len(args), len(after)

    def body(*refs):
        kernel(*refs[:count], *refs[count + ordered :])

    specs = dict(
        in_specs=list(in_specs) + [ANY] * ordered,
        out_specs=out_specs,
        scratch_shapes=list(scratch),
    )
    if grid and not prefetch:
        specs["grid"] = grid
    if prefetch:
        specs = dict(grid_spec=pltpu.PrefetchScalarGridSpec(num_scalar_prefetch=prefetch, grid=grid, **specs))
    return pl.pallas_call(
        body,
        out_shape=out_shape,
        input_output_aliases=aliases or {},
        compiler_params=pltpu.CompilerParams(vmem_limit_bytes=vmem << 20),
        cost_estimate=pl.CostEstimate(flops=int(us * COST), bytes_accessed=int(us * 1.0e5), transcendentals=0),
        name=name,
        **specs,
    )(*args, *after)


COST = 0.1e9


def low_like(rows, cols):
    return jax.ShapeDtypeStruct((rows, cols), BF16)


def wide_like(rows, cols):
    return jax.ShapeDtypeStruct((rows, cols), F32)


def behind(x, *deps, vmem=52):
    return run(
        lambda x_ref, o_ref: None,
        "behind",
        0.1,
        (x,),
        [HBM],
        jax.ShapeDtypeStruct(x.shape, x.dtype),
        HBM,
        after=deps,
        aliases={0: 0},
        vmem=vmem,
    )


def lowered(x, *deps):
    def kernel(x_ref, o_ref):
        o_ref[...] = x_ref[...].astype(BF16)

    return run(kernel, "lowered", 1, (x,), [WHOLE], low_like(*x.shape), WHOLE, after=deps)


def half_of(x, which, *deps):
    rows = x.shape[0] // 2

    def kernel(x_ref, o_ref, sem):
        copy = pltpu.make_async_copy(x_ref.at[pl.ds(which * rows, rows), :], o_ref, sem)
        copy.start()
        copy.wait()

    return run(kernel, "half_of", 1, (x,), [ANY], low_like(rows, x.shape[1]), WHOLE, [DMA], deps)


def halves(first, second, *deps):
    rows = first.shape[0] // 2

    def kernel(first_ref, second_ref, upper_ref, lower_ref, sems):
        copies = [
            pltpu.make_async_copy(ref.at[pl.ds(i * rows, rows), :], out_ref, sems.at[i])
            for i, (ref, out_ref) in enumerate(((first_ref, upper_ref), (second_ref, lower_ref)))
        ]
        for copy in copies:
            copy.start()
        for copy in copies:
            copy.wait()

    return run(
        kernel, "halves", 1, (first, second), [ANY] * 2, (low_like(rows, first.shape[1]),) * 2, (WHOLE,) * 2,
        [DMA((2,))], deps,
    )


def stacked(slots, pieces, *deps):
    count = len(pieces)

    def kernel(slots_ref, *refs):
        copies = [
            pltpu.make_async_copy(ref, refs[count].at[slots_ref[i]], refs[count + 1].at[i])
            for i, ref in enumerate(refs[:count])
        ]
        for copy in copies:
            copy.start()
        for copy in copies:
            copy.wait()

    return run(
        kernel, "stacked", 1, (slots, *pieces), [SCALAR] + [ANY] * count,
        jax.ShapeDtypeStruct((count, *pieces[0].shape), BF16), WHOLE, [DMA((count,))], deps,
    )


def tiles(width, step=256):
    return [(at, min(step, width - at)) for at in range(0, width, step)]


NT = (((1,), (1,)), ((), ()))
TN = (((0,), (0,)), ((), ()))


def dot(a, b, dims=(((1,), (0,)), ((), ()))):
    return lax.dot_general(a, b, dims, preferred_element_type=F32)


def flat(blocks):
    pieces, places = [], []
    for i, block in enumerate(blocks):
        row = 0
        for piece in block if isinstance(block, tuple) else (block,):
            pieces.append(piece)
            places.append((i, row))
            row += piece.shape[0]
    return pieces, places


def fetch(piece_refs, places, held, sems, width):
    copies = {}
    for j, (ref, (i, row)) in enumerate(zip(piece_refs, places)):
        to = held.at[i, pl.ds(row, ref.shape[0]), :]
        copies.setdefault(i, []).append(pltpu.make_async_copy(ref.at[:, pl.ds(0, width)], to, sems.at[j]))
        copies[i][-1].start()
    return copies


def wait(copies):
    for copy in copies:
        copy.wait()


def row_scale(values):
    return lax.rsqrt(jnp.mean(values * values, axis=-1, keepdims=True) + EPS_NORM)


def project_blocks(dp, ks, x_ref, scale, held, copies, a_ref, g_ref, add):
    _, depth, cols = held.shape
    wide = cols - 128
    first = lax.broadcasted_iota(jnp.int32, (8, 128), 1) < 64
    for i, k in enumerate(ks):
        wait(copies[i])
        base = (dp ^ k) * depth
        for t in range(depth // 128):
            pair = [
                jnp.broadcast_to(held[i, 64 * z : 64 * z + 16, wide:].astype(F32)[:1], (8, 128))
                for z in (2 * t, 2 * t + 1)
            ]
            turned = [pltpu.roll(row, 64, 1) for row in pair]
            at = pl.ds(pl.multiple_of(base + 128 * t, 128), 128)
            g_ref[:8, at] = jnp.where(first, pair[0], turned[1])
            g_ref[8:, at] = jnp.where(first, turned[0], pair[1])
        at = pl.ds(pl.multiple_of(base, depth), depth)
        normed = (x_ref[:, at].astype(F32) * scale * g_ref[:1, at]).astype(BF16)
        a_ref[:, at] = normed
        for c, w in tiles(wide, 512):
            add(i, c, w, dot(normed, held[i, :, c : c + w]))


def project(dp, ks, tokens, blocks, before):
    rows, model = tokens.shape
    pieces, places = flat(blocks)
    depth, cols = model // 8, pieces[0].shape[1]
    count, ahead = len(pieces), len(before)
    wide = cols - 128

    def kernel(dp_ref, x_ref, *refs):
        before_refs, block_refs = refs[:ahead], refs[ahead : ahead + count]
        p_ref, a_ref, g_ref, held, sems = refs[ahead + count :]
        copies = fetch(block_refs, places, held, sems, cols)
        if ahead:
            a_ref[...] = before_refs[1][...]
            g_ref[...] = before_refs[2][...]
        else:
            a_ref[...] = jnp.zeros_like(a_ref)
            g_ref[...] = jnp.zeros_like(g_ref)

        def add(i, c, w, term):
            if i:
                p_ref[:, c : c + w] += term
            elif ahead:
                p_ref[:, c : c + w] = before_refs[0][:, c : c + w] + term
            else:
                p_ref[:, c : c + w] = term

        project_blocks(dp_ref[0], ks, x_ref, row_scale(x_ref[...].astype(F32)), held, copies, a_ref, g_ref, add)

    return run(
        kernel, "project", 5 if ahead else 9, (dp, tokens, *before, *pieces), [SCALAR] + [WHOLE] * (1 + ahead) + [ANY] * count,
        (wide_like(rows, wide), low_like(rows, model), wide_like(16, model)), (WHOLE,) * 3,
        [VMEM((len(blocks), depth, cols), BF16), DMA((count,))],
    )


def out_part(dp, ks, attended, blocks, base, deps):
    rows, model = base.shape
    pieces, places = flat(blocks)
    depth, count = model // 8, len(pieces)

    def kernel(dp_ref, o_ref, x_ref, *refs):
        block_refs, (m_ref, held, sems) = refs[:count], refs[count:]
        copies = fetch(block_refs, places, held, sems, model)
        add_blocks(dp_ref[0], ks, o_ref, x_ref, held, copies, m_ref)

    return run(
        kernel, "out_part", 8, (dp, attended, base, *pieces), [SCALAR] + [WHOLE] * 2 + [ANY] * count,
        wide_like(rows, model), WHOLE, [VMEM((len(blocks), depth, model), BF16), DMA((count,))], deps,
    )


def add_blocks(dp, ks, o_ref, x_ref, held, copies, m_ref):
    _, depth, model = held.shape
    for i, k in enumerate(ks):
        wait(copies[i])
        at = pl.ds(pl.multiple_of((dp ^ k) * depth, depth), depth)
        part = o_ref[:, at]
        for c, w in tiles(model, 512):
            term = dot(part, held[i, :, c : c + w])
            if i == 0:
                m_ref[:, c : c + w] = x_ref[:, c : c + w].astype(F32) + term
            else:
                m_ref[:, c : c + w] += term


def out_norm(dp, ks, attended, blocks, base, gains, deps):
    rows, model = base.shape
    pieces, places = flat(blocks)
    depth, count = model // 8, len(pieces)

    def kernel(dp_ref, o_ref, x_ref, g_ref, *refs):
        block_refs, (m_ref, a_ref, held, sems) = refs[:count], refs[count:]
        copies = fetch(block_refs, places, held, sems, model)
        add_blocks(dp_ref[0], ks, o_ref, x_ref, held, copies, m_ref)
        scale = row_scale(m_ref[...])
        for c, w in tiles(model):
            a_ref[:, c : c + w] = (m_ref[:, c : c + w] * scale * g_ref[8:9, c : c + w]).astype(BF16)

    return run(
        kernel, "out_norm", 6, (dp, attended, base, gains, *pieces), [SCALAR] + [WHOLE] * 3 + [ANY] * count,
        (wide_like(rows, model), low_like(rows, model)), (WHOLE,) * 2,
        [VMEM((len(blocks), depth, model), BF16), DMA((count,))], deps,
    )


def norm_back(values, scale, gain, grads, gain_grad_ref, sums):
    model = gain_grad_ref.shape[1]
    inner = 0.0
    for c, w in tiles(model):
        normed, grad = values(c, w) * scale, grads(c, w)
        gain_grad_ref[:, c : c + w] = jnp.broadcast_to(jnp.sum(grad * normed, axis=0, keepdims=True), (8, w))
        inner = inner + jnp.sum(grad * gain(c, w) * normed, axis=-1, keepdims=True)
    inner = inner / model
    for c, w in tiles(model):
        normed = values(c, w) * scale
        sums(c, w, scale * (grads(c, w) * gain(c, w) - normed * inner))


def middle_back(terms, middle, cotangent, live, gains, deps):
    rows, model = middle.shape
    count = len(terms)

    def kernel(m_ref, c_ref, l_ref, g_ref, *refs):
        term_refs, (wide_ref, low_ref, gain_ref, held) = refs[:count], refs[count:]
        for c, w in tiles(model):
            held[:, c : c + w] = sum(ref[:, c : c + w].astype(F32) for ref in term_refs)
        scale = row_scale(m_ref[...])
        alive = l_ref[:, :1]

        def keep(c, w, grad):
            total = c_ref[:, c : c + w].astype(F32) * alive + grad
            wide_ref[:, c : c + w] = total
            low_ref[:, c : c + w] = total.astype(BF16)

        norm_back(
            lambda c, w: m_ref[:, c : c + w], scale, lambda c, w: g_ref[8:9, c : c + w],
            lambda c, w: held[:, c : c + w], gain_ref, keep,
        )

    return run(
        kernel, "middle_back", 6, (middle, cotangent, live, gains, *terms), [WHOLE] * (4 + count),
        (wide_like(rows, model), low_like(rows, model), wide_like(8, model)), (WHOLE,) * 3,
        [VMEM((rows, model), F32)], deps,
    )


def attended_grad(dp, branch, blocks, deps):
    rows, model = branch.shape
    pieces, places = flat(blocks)
    depth, count = model // 8, len(pieces)

    def kernel(dp_ref, y_ref, *refs):
        block_refs, (out_ref, held, sems) = refs[:count], refs[count:]
        copies = fetch(block_refs, places, held, sems, model)
        for k in range(len(blocks)):
            wait(copies[k])
            at = pl.ds(pl.multiple_of((dp_ref[0] ^ k) * depth, depth), depth)
            out_ref[:, at] = dot(y_ref[...], held[k], NT).astype(BF16)

    return run(
        kernel, "attended_grad", 11, (dp, branch, *pieces), [SCALAR, WHOLE] + [ANY] * count,
        low_like(rows, model), WHOLE, [VMEM((len(blocks), depth, model), BF16), DMA((count,))], deps,
    )


def input_back(dp, grad, blocks, tokens, gains, residual, deps):
    rows, model = tokens.shape
    pieces, places = flat(blocks)
    depth, wide, count = model // 8, grad.shape[1], len(pieces)

    def kernel(dp_ref, y_ref, x_ref, g_ref, r_ref, *refs):
        block_refs, (out_ref, gain_ref, held, total, sems) = refs[:count], refs[count:]
        copies = fetch(block_refs, places, held, sems, wide)
        for k in range(len(blocks)):
            wait(copies[k])
            at = pl.ds(pl.multiple_of((dp_ref[0] ^ k) * depth, depth), depth)
            total[:, at] = dot(y_ref[...], held[k], NT)
        scale = row_scale(x_ref[...].astype(F32))

        def keep(c, w, back):
            out_ref[:, c : c + w] = (r_ref[:, c : c + w] + back).astype(BF16)

        norm_back(
            lambda c, w: x_ref[:, c : c + w].astype(F32), scale, lambda c, w: g_ref[:1, c : c + w],
            lambda c, w: total[:, c : c + w], gain_ref, keep,
        )

    return run(
        kernel, "input_back", 18, (dp, grad, tokens, gains, residual, *pieces), [SCALAR] + [WHOLE] * 4 + [ANY] * count,
        (low_like(rows, model), wide_like(8, model)), (WHOLE,) * 2,
        [VMEM((len(blocks), depth, wide), BF16), VMEM((rows, model), F32), DMA((count,))], deps,
    )


def blocks_outer(dp, ks, counts, x, y, deps):
    rows, cols = y.shape
    depth = x.shape[1] // 8
    lows = [sum(counts[:i]) for i in range(len(counts))]

    def kernel(dp_ref, x_ref, y_ref, *out_refs):
        step = pl.program_id(0)
        term = dot(x_ref[...], y_ref[...], TN).astype(BF16)[None]
        for ref, low, n in zip(out_refs, lows, counts):

            @pl.when((step >= low) & (step < low + n))
            def _():
                ref[...] = term

    def block(i, dp_ref):
        k = ks[-1]
        for j in range(len(ks) - 1):
            k = jnp.where(i == j, ks[j], k)
        return dp_ref[0] ^ k

    return run(
        kernel, "blocks_outer", 10, (dp, x, y),
        [
            pl.BlockSpec((rows, depth), lambda i, dp_ref: (0, block(i, dp_ref))),
            pl.BlockSpec((rows, cols), lambda i, dp_ref: (0, 0)),
        ],
        tuple(jax.ShapeDtypeStruct((n, depth, cols), BF16) for n in counts),
        tuple(
            pl.BlockSpec((1, depth, cols), lambda i, dp_ref, low=low, n=n: (jnp.clip(i - low, 0, n - 1), 0, 0))
            for low, n in zip(lows, counts)
        ),
        after=deps, prefetch=1, grid=(len(ks),),
    )


def outer_swapped(dp, x, y, deps):
    odd = blocks_outer(dp, (7, 3, 5, 1), (2, 2), x, y, deps)
    (even,) = blocks_outer(dp, (6, 2, 4, 0), (4,), x, y, (odd[0],))
    return [swap(part, 1) for part in odd], even


def first_sums(even, others, deps):
    _, depth, cols = even.shape
    half = depth // 2

    def kernel(even_ref, first_ref, second_ref, low_ref, high_ref, *refs):
        other = lambda i, at: (first_ref if i < 2 else second_ref)[i % 2, at].astype(F32)
        add = lambda i, at: (even_ref[i, at].astype(F32) + other(i, at)).astype(BF16)
        low_ref[...] = add(0, slice(0, half))
        high_ref[...] = add(0, slice(half, depth))
        for i, ref in enumerate(refs):
            ref[...] = add(i + 1, slice(0, depth))

    return run(
        kernel, "first_sums", 5, (even, *others), [WHOLE] * 3,
        (low_like(half, cols),) * 2 + (low_like(depth, cols),) * 3, (WHOLE,) * 5, after=deps,
    )


def second_sums(x_block, y_block, low, high, deps):
    half, cols = low.shape

    def kernel(x_ref, y_ref, low_ref, high_ref, x_out, y_out):
        add = lambda a, b: (a.astype(F32) + b.astype(F32)).astype(BF16)
        x_out[:half], x_out[half:] = x_ref[:half], add(x_ref[half:], high_ref[...])
        y_out[:half], y_out[half:] = add(y_ref[:half], low_ref[...]), y_ref[half:]

    return run(
        kernel, "second_sums", 2, (x_block, y_block, low, high), [WHOLE] * 4, (low_like(2 * half, cols),) * 2,
        (WHOLE,) * 2, after=deps,
    )


def folded(keep, others, parts, deps):
    rows, cols = keep.shape
    share, count = cols // parts, len(others)

    def kernel(keep_ref, *refs):
        row = 0
        for other_ref in refs[:count]:
            down = slice(row, row + other_ref.shape[0])
            row += other_ref.shape[0]
            for i, ref in enumerate(refs[count:]):
                here = slice(share * i, share * (i + 1))
                ref[down] = (keep_ref[down, here].astype(F32) + other_ref[:, here].astype(F32)).astype(BF16)

    return run(
        kernel, "folded", 2 if parts > 1 else 1, (keep, *others), [WHOLE] * (1 + count), (low_like(rows, share),) * parts,
        (WHOLE,) * parts, after=deps,
    )


def gate_rows(a2, weight, deps):
    pieces, _ = flat(a2)
    count = len(pieces)
    rows = sum(piece.shape[0] for piece in pieces)
    model, both = weight.shape
    width = both // 2
    parts = tiles(width)

    def kernel(w_hbm, *refs):
        a_hbms, (gu_hbm, hid_ref, held, a_ref, stage, sems, a_sems, out_sems) = refs[:count], refs[count:]
        row, rows_in, arriving = 0, [], []
        for i, ref in enumerate(a_hbms):
            rows_in.append(pltpu.make_async_copy(ref, a_ref.at[pl.ds(row, ref.shape[0]), :], a_sems.at[i]))
            row += ref.shape[0]
        for i, (at, w) in enumerate(parts):
            arriving.append([])
            for h, col in enumerate((at, width + at)):
                here = (slice(None), pl.ds(col, w))
                arriving[-1].append(pltpu.make_async_copy(w_hbm.at[here], held.at[here], sems.at[2 * i + h]))
        for copy in rows_in + sum(arriving, []):
            copy.start()
        wait(rows_in)
        leaving = []
        for i, (at, w) in enumerate(parts):
            wait(arriving[i])
            slot = i % 2
            if i > 1:
                wait(leaving[i - 2])
            gate = dot(a_ref[...], held[:, at : at + w])
            stage[slot, 0, :, :w] = gate
            upper = dot(a_ref[...], held[:, width + at : width + at + w])
            stage[slot, 1, :, :w] = upper
            hid_ref[:, at : at + w] = (gate * jax.nn.sigmoid(gate) * upper).astype(BF16)
            leaving.append(
                [
                    pltpu.make_async_copy(
                        stage.at[slot, h, :, pl.ds(0, w)], gu_hbm.at[:, pl.ds(h * width + at, w)], out_sems.at[slot, h]
                    )
                    for h in range(2)
                ]
            )
            for copy in leaving[-1]:
                copy.start()
        for copies in leaving[-2:]:
            wait(copies)

    return run(
        kernel, "gate_rows", 2 + 7 * rows // 384, (weight, *pieces), [ANY] * (1 + count),
        (wide_like(rows, both), low_like(rows, width)), (ANY, WHOLE),
        [
            VMEM((model, both), BF16), VMEM((rows, model), BF16), VMEM((2, 2, rows, 256), F32),
            DMA((2 * len(parts),)), DMA((count,)), DMA((2, 2)),
        ],
        deps,
    )


def gate_back(gate_up, at_rows, eb, down, weight, split, deps):
    pieces, _ = flat(eb)
    count = len(pieces)
    rows = sum(piece.shape[0] for piece in pieces) // 2
    model, both = weight.shape
    width = both // 2
    shares = [rows // 2] * 2 + [rows] if split else [rows] * 2

    def kernel(*refs):
        gu_hbms, (down_hbm, w_hbm), e_hbms = refs[:2], refs[2:4], refs[4 : 4 + count]
        dgu_ref, back_refs, (down_ref, held, gu_ref, e_ref, sems) = refs[4 + count], refs[5 + count : -5], refs[-5:]
        first, row = [pltpu.make_async_copy(down_hbm, down_ref, sems.at[0])], 0
        for j, ref in enumerate(e_hbms):
            first.append(pltpu.make_async_copy(ref, e_ref.at[pl.ds(row, ref.shape[0]), :], sems.at[4 + j]))
            row += ref.shape[0]
        for i in range(2):
            to = gu_ref.at[pl.ds(rows * i, rows), :]
            first.append(pltpu.make_async_copy(gu_hbms[i].at[pl.ds(at_rows[i], rows), :], to, sems.at[2 + i]))
        second = [pltpu.make_async_copy(w_hbm, held, sems.at[1])]
        for copy in first + second:
            copy.start()
        wait(first)
        for at, w in tiles(width):
            back = dot(e_ref[...], down_ref[at : at + w, :], NT)
            gate, upper = gu_ref[:, at : at + w], gu_ref[:, width + at : width + at + w]
            sigma = jax.nn.sigmoid(gate)
            dgu_ref[:, at : at + w] = (back * upper * sigma * (1.0 + gate * (1.0 - sigma))).astype(BF16)
            dgu_ref[:, width + at : width + at + w] = (back * gate * sigma).astype(BF16)
        wait(second)
        for at, w in tiles(model):
            part = dot(dgu_ref[...], held[at : at + w, :], NT).astype(BF16)
            row = 0
            for share, ref in zip(shares, back_refs):
                ref[:, at : at + w] = part[row : row + share]
                row += share

    return run(
        kernel, "gate_back", 22, (*gate_up, down, weight, *pieces), [ANY] * (4 + count),
        (low_like(2 * rows, both),) + tuple(low_like(share, model) for share in shares), (WHOLE,) * (1 + len(shares)),
        [
            VMEM((width, model), BF16), VMEM((model, both), BF16), VMEM((2 * rows, both), F32),
            VMEM((2 * rows, model), BF16), DMA((4 + count,)),
        ],
        deps,
    )


def down_rows(hidden, rows, down, deps):
    width, model = down.shape
    count = len(hidden)
    blocks = [(i, at) for i, h in enumerate(hidden) for at in range(0, h.shape[0], rows)]

    def kernel(down_ref, *refs):
        hid_refs, out_refs = refs[:count], refs[count:]
        for (i, at_row), out_ref in zip(blocks, out_refs):
            for at, w in tiles(model):
                out_ref[:, at : at + w] = dot(hid_refs[i][at_row : at_row + rows], down_ref[:, at : at + w]).astype(BF16)

    return run(
        kernel, "down_rows", 13, (down, *hidden), [WHOLE] * (1 + count),
        (low_like(rows, model),) * len(blocks), (WHOLE,) * len(blocks), after=deps,
    )


def outer_sum(starts, sizes, xs, ys, deps):
    xs, ys = flat(xs)[0], flat(ys)[0]
    height, cols = xs[0].shape[1], ys[0].shape[1]
    rows = sum(x.shape[0] for x in xs)
    half = height // 2
    count, pieces = len(xs), len(sizes)

    def kernel(starts_ref, *refs):
        x_refs, y_refs = refs[:count], refs[count : count + len(ys)]
        keep_ref, piece_refs, (turned, tile) = refs[count + len(ys)], refs[count + len(ys) + 1 : -2], refs[-2:]

        @pl.when(pl.program_id(0) == 0)
        def _():
            base = 0
            for ref in x_refs:
                for at in range(0, height, 128):
                    turned[at : at + 128, base : base + ref.shape[0]] = ref[:, at : at + 128].T
                base += ref.shape[0]

        base = 0
        for ref in y_refs:
            tile[base : base + ref.shape[0], :] = ref[...]
            base += ref.shape[0]
        row, into = 0, []
        for size in sizes:
            into.append(keep_ref.at[pl.ds(row, size), :])
            row += size
        for i, ref in enumerate((*into, *piece_refs)):
            at = pl.multiple_of(starts_ref[i], 16)
            ref[...] = dot(turned[pl.ds(at, sizes[i % pieces]), :], tile[...]).astype(BF16)

    fixed = lambda i, s: (0, 0)
    column = lambda i, s: (0, i)
    return run(
        kernel, "outer_sum", 8 if cols > D else 5, (starts, *xs, *ys),
        [pl.BlockSpec(x.shape, fixed) for x in xs] + [pl.BlockSpec((y.shape[0], 256), column) for y in ys],
        (low_like(half, cols),) + tuple(low_like(size, cols) for size in sizes),
        (pl.BlockSpec((half, 256), column),) + tuple(pl.BlockSpec((size, 256), column) for size in sizes),
        [VMEM((height, rows), BF16), VMEM((rows, 256), BF16)],
        deps, prefetch=1, grid=(cols // 256,), vmem=60,
    )


def adam_attention(grads, weight, first_moment, second_moment, gains, first_gains, second_gains):
    rows, wide = weight.shape
    share = gains.shape[1]

    def kernel(g_ref, w_ref, m_ref, v_ref, gain_ref, gain_m_ref, gain_v_ref, *out_refs):
        for c, w in tiles(wide, 512):
            here = (slice(None), slice(c, c + w))
            state = adam_step(w_ref[here], m_ref[here], v_ref[here], g_ref[here].astype(F32), RATE_MATRIX, DECAY_MATRIX)
            for ref, value in zip(out_refs[:3], state):
                ref[here] = value
        row = g_ref[:16, wide:].astype(F32)
        grad = jnp.concatenate([row[:1], pltpu.roll(row, share, 1)[:1]], axis=0)[:, :share]
        state = adam_step(gain_ref[...], gain_m_ref[...], gain_v_ref[...], grad, RATE_GAIN, 0.0)
        for ref, value in zip(out_refs[3:], state):
            ref[...] = value

    state = (wide_like(rows, wide),) * 3 + (wide_like(2, share),) * 3
    return run(
        kernel, "adam_attention", 3,
        (grads, weight, first_moment, second_moment, gains, first_gains, second_gains), [WHOLE] * 7, state, (WHOLE,) * 6,
    )


def turn(x, cosine, sine):
    lane = lax.broadcasted_iota(jnp.int32, cosine.shape, 1)
    lower = (lane & (HEAD_DIM - 1)) < HEAD_DIM // 2
    out = []
    for j in range(x.shape[1] // 128):
        tile = x[:, 128 * j : 128 * (j + 1)]
        other = jnp.where(lower, pltpu.roll(tile, 96, 1), pltpu.roll(tile, 32, 1))
        out.append(tile * cosine + other * sine)
    return out


def both_halves(tile, which):
    lane = lax.broadcasted_iota(jnp.int32, tile.shape, 1)
    other = pltpu.roll(tile, HEAD_DIM, 1)
    low, high = (tile, other) if which == 0 else (other, tile)
    zero = jnp.zeros_like(tile)
    return jnp.where(lane < HEAD_DIM, low, zero), jnp.where(lane >= HEAD_DIM, high, zero)


PAIRS = HEADS // KV_HEADS // 2
STEP_ROWS = 128


def masked_scores(q, k, seg_q, seg_k, first):
    scores = lax.dot_general(q, k, (((1,), (1,)), ((), ())), preferred_element_type=F32) * HEAD_DIM ** (-0.5)
    pairs, keys = q.shape[0] // STEP_ROWS, k.shape[0]
    rows = lax.broadcasted_iota(jnp.int32, (STEP_ROWS, keys), 0) + first
    cols = lax.broadcasted_iota(jnp.int32, (STEP_ROWS, keys), 1)
    allowed = (seg_q == seg_k) & (cols <= rows)
    scores = jnp.where(allowed[None], scores.reshape(pairs, STEP_ROWS, keys), -1e30)
    raised = jnp.exp(scores - jnp.max(scores, axis=-1, keepdims=True))
    return (raised / jnp.sum(raised, axis=-1, keepdims=True)).reshape(pairs * STEP_ROWS, keys)


def attend(projected, cosine, sine, segment):
    rows = projected.shape[0]
    kv = KV_HEADS * HEAD_DIM

    def kernel(p_ref, cos_ref, sin_ref, segq_ref, segk_ref, q_ref, k_ref, v_ref, o_ref):
        cosine, sine = cos_ref[...], sin_ref[...]
        for j, tile in enumerate(turn(p_ref[:, :D], cosine, sine)):
            q_ref[:, 128 * j : 128 * (j + 1)] = tile.astype(BF16)
        for j, tile in enumerate(turn(p_ref[:, D : D + kv], cosine, sine)):
            k_ref[:, 128 * j : 128 * (j + 1)] = tile.astype(BF16)
        v_ref[...] = p_ref[:, D + kv : D + 2 * kv].astype(BF16)
        for g in range(KV_HEADS):
            tile = slice(128 * (g // 2), 128 * (g // 2 + 1))
            k_low, k_high = both_halves(k_ref[:, tile].astype(F32), g % 2)
            v_low, v_high = both_halves(v_ref[:, tile].astype(F32), g % 2)
            k_low, k_high, v_low, v_high = (x.astype(BF16) for x in (k_low, k_high, v_low, v_high))
            for first in range(0, rows, STEP_ROWS):
                keys = first + STEP_ROWS
                at = lambda j: slice(128 * (g * PAIRS + j), 128 * (g * PAIRS + j + 1))
                q = jnp.concatenate([q_ref[first:keys, at(j)] for j in range(PAIRS)], axis=0)
                seg_q, seg_k = segq_ref[first:keys, :1], segk_ref[:1, :keys]
                low = masked_scores(q, k_low[:keys], seg_q, seg_k, first).astype(BF16)
                high = masked_scores(q, k_high[:keys], seg_q, seg_k, first).astype(BF16)
                out = jnp.dot(low, v_low[:keys], preferred_element_type=F32)
                out = out + jnp.dot(high, v_high[:keys], preferred_element_type=F32)
                for j in range(PAIRS):
                    o_ref[first:keys, at(j)] = out[STEP_ROWS * j : STEP_ROWS * (j + 1)].astype(BF16)

    return run(
        kernel, "attend", 15,
        (projected, cosine, sine, jnp.broadcast_to(segment[:, None], (rows, 128)), jnp.broadcast_to(segment[None], (8, rows))),
        [WHOLE] * 5, (low_like(rows, D), low_like(rows, kv), low_like(rows, kv), low_like(rows, D)), (WHOLE,) * 4,
    )


def attend_back(queries, key_rows, value_rows, attended_back, cosine, sine, segment, deps):
    rows = queries.shape[0]
    kv = KV_HEADS * HEAD_DIM
    factor = HEAD_DIM ** (-0.5)

    def kernel(q_ref, k_ref, v_ref, b_ref, cos_ref, sin_ref, segq_ref, segk_ref, dp_ref, dk_ref, dv_ref):
        cosine, sine = cos_ref[...], -sin_ref[...]
        lane = lax.broadcasted_iota(jnp.int32, (STEP_ROWS, 128), 1)
        contract = lambda a, b: lax.dot_general(a, b, (((0,), (0,)), ((), ())), preferred_element_type=F32)
        for g in range(KV_HEADS):
            tile = slice(128 * (g // 2), 128 * (g // 2 + 1))
            k_low, k_high = both_halves(k_ref[:, tile].astype(F32), g % 2)
            v_low, v_high = both_halves(v_ref[:, tile].astype(F32), g % 2)
            k_low, k_high, v_low, v_high = (x.astype(BF16) for x in (k_low, k_high, v_low, v_high))
            dk_ref[...] = jnp.zeros_like(dk_ref)
            dv_ref[...] = jnp.zeros_like(dv_ref)
            for first in range(0, rows, STEP_ROWS):
                keys = first + STEP_ROWS
                at = lambda j: slice(128 * (g * PAIRS + j), 128 * (g * PAIRS + j + 1))
                q = jnp.concatenate([q_ref[first:keys, at(j)] for j in range(PAIRS)], axis=0)
                b = jnp.concatenate([b_ref[first:keys, at(j)] for j in range(PAIRS)], axis=0)
                seg_q, seg_k = segq_ref[first:keys, :1], segk_ref[:1, :keys]
                dq, dk, dv = None, [], []
                for k_half, v_half in ((k_low, v_low), (k_high, v_high)):
                    probs = masked_scores(q, k_half[:keys], seg_q, seg_k, first)
                    back = lax.dot_general(b, v_half[:keys], (((1,), (1,)), ((), ())), preferred_element_type=F32)
                    inner = jnp.sum(back * probs, axis=-1, keepdims=True)
                    ds = (probs * (back - inner)).astype(BF16)
                    dv.append(contract(probs.astype(BF16), b))
                    dk.append(contract(ds, q))
                    term = jnp.dot(ds, k_half[:keys], preferred_element_type=F32)
                    dq = term if dq is None else dq + term
                low = lax.broadcasted_iota(jnp.int32, (keys, 128), 1) < HEAD_DIM
                dk_ref[:keys] += jnp.where(low, dk[0], dk[1])
                dv_ref[:keys] += jnp.where(low, dv[0], dv[1])
                for j in range(PAIRS):
                    (turned,) = turn(
                        dq[STEP_ROWS * j : STEP_ROWS * (j + 1)] * factor, cosine[first:keys], sine[first:keys]
                    )
                    dp_ref[first:keys, at(j)] = turned.astype(BF16)
            total_k = dk_ref[...] + pltpu.roll(dk_ref[...], HEAD_DIM, 1)
            total_v = dv_ref[...] + pltpu.roll(dv_ref[...], HEAD_DIM, 1)
            (total_k,) = turn(total_k * factor, cosine, sine)
            mine = lax.broadcasted_iota(jnp.int32, (rows, 128), 1) // HEAD_DIM == g % 2
            for base, total in ((D, total_k), (D + kv, total_v)):
                here = slice(base + 128 * (g // 2), base + 128 * (g // 2 + 1))
                if g % 2 == 0:
                    dp_ref[:, here] = total.astype(BF16)
                else:
                    dp_ref[:, here] = jnp.where(mine, total, dp_ref[:, here].astype(F32)).astype(BF16)

    return run(
        kernel, "attend_back", 24,
        (
            queries, key_rows, value_rows, attended_back, cosine, sine,
            jnp.broadcast_to(segment[:, None], (rows, 128)), jnp.broadcast_to(segment[None], (8, rows)),
        ),
        [WHOLE] * 8, low_like(rows, QKV_W), WHOLE, [VMEM((rows, 128), F32)] * 2, deps, vmem=28,
    )


def turning(position):
    frequency = THETA ** (-(jnp.arange(HEAD_DIM // 2, dtype=F32) * 2.0 / HEAD_DIM))
    phases = position.astype(F32)[:, None] * frequency[None, :]
    cosine, sine = jnp.cos(phases), jnp.sin(phases)
    return jnp.concatenate([cosine] * 4, axis=1), jnp.concatenate([-sine, sine] * 2, axis=1)


def rotary(vectors, cosine, sine_part):
    half_dim = HEAD_DIM // 2
    lower_half = vectors[..., :half_dim]
    upper_half = vectors[..., half_dim:]
    return jnp.concatenate(
        [
            lower_half * cosine - upper_half * sine_part,
            upper_half * cosine + lower_half * sine_part,
        ],
        axis=-1,
    )


def any_mesh(
    tokens, cotangent, seq_table, w_qkv, m_qkv, v_qkv, w_out, m_out, v_out, w_gate_up, m_gate_up, v_gate_up,
    w_down, m_down, v_down, norm_gains, m_gains, v_gains,
):
    everyone = ("dp", "fsdp")
    nd = lax.axis_size("dp")
    rows_here = tokens.shape[0]
    kv_width = KV_HEADS * HEAD_DIM
    group_size = HEADS // KV_HEADS
    factor = HEAD_DIM ** (-0.5)
    width = FF // nd
    d_rows = w_gate_up.shape[0]
    einsum = lambda how, a, b: jnp.einsum(how, a, b, preferred_element_type=F32)
    scatter = lambda x, axes, dim: lax.psum_scatter(x.astype(BF16), axes, scatter_dimension=dim, tiled=True)

    segment, position, live_rows = layout(seq_table[0], rows_here)
    row_ids = jnp.arange(rows_here)
    allowed = (segment[:, None] == segment[None, :]) & (row_ids[None, :] <= row_ids[:, None])
    frequency = THETA ** (-(jnp.arange(HEAD_DIM // 2, dtype=F32) * 2.0 / HEAD_DIM))
    phases = position.astype(F32)[:, None] * frequency[None, :]
    cosine, sine = jnp.cos(phases)[:, None, :], jnp.sin(phases)[:, None, :]

    qkv_full = lax.all_gather(w_qkv.astype(BF16), everyone, axis=0, tiled=True)
    out_full = lax.all_gather(w_out.astype(BF16), everyone, axis=0, tiled=True)
    gains_full = lax.all_gather(norm_gains.astype(BF16), everyone, axis=1, tiled=True).astype(F32)
    pieces = w_gate_up.astype(BF16).reshape(d_rows, 2, nd, width).transpose(2, 0, 1, 3).reshape(nd, d_rows, 2 * width)
    gate_up_here = lax.all_to_all(pieces, "dp", 0, 0, tiled=True)
    gate_up_here = lax.all_gather(gate_up_here, "fsdp", axis=1, tiled=True).reshape(D, 2 * width)
    down_here = lax.all_gather(w_down.astype(BF16), "fsdp", axis=0, tiled=True)

    inputs = tokens.astype(F32)
    scale_one = lax.rsqrt(jnp.mean(inputs * inputs, axis=-1, keepdims=True) + EPS_NORM)
    normed_one = inputs * scale_one
    low_one = (normed_one * gains_full[0]).astype(BF16)
    projected = einsum("td,de->te", low_one, qkv_full)
    queries = rotary(projected[:, :D].reshape(rows_here, HEADS, HEAD_DIM), cosine, sine)
    queries = queries.astype(BF16).reshape(rows_here, KV_HEADS, group_size, HEAD_DIM)
    key_rows = rotary(projected[:, D : D + kv_width].reshape(rows_here, KV_HEADS, HEAD_DIM), cosine, sine).astype(BF16)
    value_rows = projected[:, D + kv_width :].reshape(rows_here, KV_HEADS, HEAD_DIM).astype(BF16)
    scores = jnp.where(allowed, einsum("qhgd,khd->hgqk", queries, key_rows) * factor, -1e30)
    raised = jnp.exp(scores - jnp.max(scores, axis=-1, keepdims=True))
    attention = raised / jnp.sum(raised, axis=-1, keepdims=True)
    attention_low = attention.astype(BF16)
    attended = einsum("hgqk,khd->qhgd", attention_low, value_rows).reshape(rows_here, D).astype(BF16)
    middle = inputs + einsum("td,de->te", attended, out_full)
    scale_two = lax.rsqrt(jnp.mean(middle * middle, axis=-1, keepdims=True) + EPS_NORM)
    normed_two = middle * scale_two
    low_two = lax.all_gather((normed_two * gains_full[1]).astype(BF16), "dp", axis=0, tiled=True)

    back_rows = cotangent.astype(F32) * live_rows[:, None].astype(F32)
    down_back = lax.all_gather(back_rows.astype(BF16), "dp", axis=0, tiled=True)
    gate_up = einsum("td,df->tf", low_two, gate_up_here)
    gate, upper = gate_up[:, :width], gate_up[:, width:]
    sigma = jax.nn.sigmoid(gate)
    hidden = (gate * sigma * upper).astype(BF16)
    output = (middle + scatter(einsum("tf,fd->td", hidden, down_here), "dp", 0).astype(F32)).astype(BF16)
    hidden_back = einsum("td,fd->tf", down_back, down_here)
    gate_back = hidden_back * upper * sigma * (1.0 + gate * (1.0 - sigma))
    gate_up_back = jnp.concatenate([gate_back, hidden_back * gate * sigma], axis=1).astype(BF16)
    normed_two_back = scatter(einsum("tf,df->td", gate_up_back, gate_up_here), "dp", 0).astype(F32)
    down_shard = scatter(einsum("tf,td->fd", hidden, down_back), "fsdp", 0).astype(F32)
    gate_up_grad = einsum("td,tf->df", low_two, gate_up_back).reshape(nd, D // nd, 2 * width)
    gate_up_grad = lax.all_to_all(scatter(gate_up_grad, "fsdp", 1), "dp", 0, 0, tiled=True)
    gate_up_shard = gate_up_grad.reshape(nd, d_rows, 2, width).transpose(1, 2, 0, 3).reshape(d_rows, 2 * FF).astype(F32)

    def norm_grad(normed, scale, gain, grad):
        inner = grad * gain
        grad_in = scale * (inner - normed * jnp.mean(inner * normed, axis=-1, keepdims=True))
        return grad_in, jnp.sum(grad * normed, axis=0)

    middle_grad, gain_two_grad = norm_grad(normed_two, scale_two, gains_full[1], normed_two_back)
    middle_grad = back_rows + middle_grad
    branch_back = middle_grad.astype(BF16)
    out_shard = scatter(scatter(einsum("tr,tf->rf", attended, branch_back), "dp", 0), "fsdp", 0).astype(F32)
    attended_back = einsum("te,de->td", branch_back, out_full).astype(BF16)
    attended_back = attended_back.reshape(rows_here, KV_HEADS, group_size, HEAD_DIM)
    prob_back = einsum("qhgd,khd->hgqk", attended_back, value_rows)
    value_back = einsum("hgqk,qhgd->khd", attention_low, attended_back)
    score_back = attention * (prob_back - jnp.sum(prob_back * attention, axis=-1, keepdims=True))
    score_back = score_back.astype(BF16)
    query_back = einsum("hgqk,khd->qhgd", score_back, key_rows) * factor
    key_back = einsum("hgqk,qhgd->khd", score_back, queries) * factor
    query_back = rotary(query_back.reshape(rows_here, HEADS, HEAD_DIM), cosine, -sine).reshape(rows_here, D)
    key_back = rotary(key_back, cosine, -sine).reshape(rows_here, kv_width)
    projected_back = jnp.concatenate([query_back, key_back, value_back.reshape(rows_here, kv_width)], axis=1).astype(BF16)
    qkv_shard = scatter(scatter(einsum("tr,tf->rf", low_one, projected_back), "dp", 0), "fsdp", 0).astype(F32)
    normed_one_back = einsum("te,de->td", projected_back, qkv_full)
    input_norm_back, gain_one_grad = norm_grad(normed_one, scale_one, gains_full[0], normed_one_back)
    input_grad = (middle_grad + input_norm_back).astype(BF16)
    gain_grads = jnp.stack([gain_one_grad, gain_two_grad], axis=1)
    gain_shard = lax.psum_scatter(gain_grads, everyone, scatter_dimension=0, tiled=True).T

    return (
        output,
        input_grad,
        *adam_step(w_qkv, m_qkv, v_qkv, qkv_shard, RATE_MATRIX, DECAY_MATRIX),
        *adam_step(w_out, m_out, v_out, out_shard, RATE_MATRIX, DECAY_MATRIX),
        *adam_step(w_gate_up, m_gate_up, v_gate_up, gate_up_shard, RATE_MATRIX, DECAY_MATRIX),
        *adam_step(w_down, m_down, v_down, down_shard, RATE_MATRIX, DECAY_MATRIX),
        *adam_step(norm_gains, m_gains, v_gains, gain_shard, RATE_GAIN, 0.0),
    )


PLANE = ("tp", "core")


def swap(x, k):
    return lax.ppermute(x, PLANE, [(d, d ^ k) for d in range(8)])


NEAR, FAR = (0, 1, 2, 4, 3, 5), (6, 7)


def gather_plane(own, deps, with_near):
    b = {0: own}
    b[2] = swap(own, 2)
    b[4] = swap(own, 4)
    b[1] = swap(own, 1)
    if deps:
        b[2], b[4] = behind(b[2], *deps), behind(b[4], *deps)
    low, high = halves(b[4], b[2])
    low, high = swap(low, 2), swap(high, 4)
    for k in (2, 4):
        b[k + 1] = swap(b[k], 1)
    near = with_near([b[k] for k in NEAR])
    first = jax.tree.leaves(near)[0]
    b[6] = (behind(low, first), behind(high, first))
    b[7] = (swap(b[6][0], 1), swap(b[6][1], 1))
    return [b[k] for k in range(8)], near


def total(terms):
    return sum(term.astype(F32) for term in terms)


def cube(
    tokens, cotangent, seq_table, w_qkv, m_qkv, v_qkv, w_out, m_out, v_out, w_gate_up, m_gate_up, v_gate_up,
    w_down, m_down, v_down, norm_gains, m_gains, v_gains,
):
    nf = lax.axis_size("fsdp")
    dp_index = lax.axis_index(PLANE)
    dp = dp_index[None]
    core, chip = dp & 1, dp_index >> 1
    rows_here = tokens.shape[0]
    d_rows = w_qkv.shape[0]
    width = FF // 4

    gain_pad = jnp.pad(norm_gains.astype(BF16).reshape(1, 2 * d_rows), ((0, d_rows - 1), (0, 128 - 2 * d_rows)))
    qkv_low = jnp.concatenate([w_qkv.astype(BF16), gain_pad], axis=1)
    qkv_own = lax.all_gather(qkv_low, "fsdp", axis=0, tiled=True)

    segment, position, live_rows = layout(seq_table[0], rows_here)
    cosine, sine = turning(position)
    live = jnp.broadcast_to(live_rows[:, None].astype(F32), (rows_here, 128))
    eb = (cotangent.astype(F32) * live_rows[:, None].astype(F32)).astype(BF16)
    gu_low = lowered(w_gate_up, qkv_low)
    pieces = []
    for k in range(4):
        there = chip ^ k
        piece = jnp.concatenate(
            [lax.dynamic_slice(gu_low, (0, (h * 4 + there) * width), (d_rows, width)) for h in range(2)], axis=1
        )
        pieces.append(swap(piece, 2 * k) if k else piece)
    chips = jnp.stack([chip ^ k for k in range(4)])

    out_low = lowered(w_out, *pieces[1:])
    out_own = lax.all_gather(out_low, "fsdp", axis=0, tiled=True)
    gate_up_here = lax.all_gather(stacked(chips, pieces, out_low), ("core", "fsdp"), axis=1, tiled=True)
    gate_up_here = gate_up_here.reshape(D, 2 * width)

    qkv_blocks, near = gather_plane(qkv_own, (), lambda blocks: project(dp, NEAR, tokens, blocks, ()))
    down_here = lax.all_gather(lowered(w_down, qkv_blocks[2], qkv_blocks[4]), ("core", "fsdp"), axis=0, tiled=True)
    projected, low_one, gains = project(dp, FAR, tokens, qkv_blocks[6:], near)
    queries, key_rows, value_rows, attended = attend(projected, cosine, sine, segment)
    out_blocks, near = gather_plane(
        behind(out_own, *qkv_blocks[6]), (attended,),
        lambda blocks: out_part(dp, NEAR, attended, blocks, tokens, ()),
    )
    middle, a2 = out_norm(dp, FAR, attended, out_blocks[6:], near, gains, ())

    a2_x, a2_y = swap(a2, 2), swap(a2, 4)
    a2_low, a2_high = halves(a2_y, a2_x)
    cut = (a2_low, a2_high)
    a2_low, a2_high = swap(a2_low, 2), swap(a2_high, 4)
    gate_up_a, hidden_a = gate_rows((a2, a2_x, a2_y), gate_up_here, cut)
    eb = behind(eb, hidden_a, a2_low, a2_high)
    eb_x, eb_y = swap(eb, 2), swap(eb, 4)
    a2_d = (a2_low, a2_high)
    gate_up_b, hidden_b = gate_rows((a2_d,), gate_up_here, (hidden_a,))
    hidden = (hidden_a, hidden_b)
    half_ff = width // 2
    thirds = (240, 240, 224)
    thirds_at = jnp.concatenate([c * half_ff + at for c in (core, 1 - core) for at in (0, 240, 480)])
    out_own_rows, out_x, out_y, out_d = down_rows(hidden, rows_here, down_here, (hidden_b,))
    eb_low, eb_high = halves(eb_y, eb_x, out_own_rows)
    eb_low, eb_high = swap(eb_low, 2), swap(eb_high, 4)
    eb_d = (eb_low, eb_high)
    weights = (down_here, gate_up_here)
    back_gu_a, back_x, back_own = gate_back(
        (gate_up_a, gate_up_a), (rows_here, 0), (eb_x, eb), *weights, False, (out_own_rows,)
    )
    out_x, out_y = swap(behind(out_x, back_x), 2), swap(behind(out_y, back_x), 4)
    back_gu_b, back_low, back_high, back_y = gate_back(
        (gate_up_b, gate_up_a), (0, 2 * rows_here), (eb_d, eb_y), *weights, True, (back_x,)
    )
    back_low, back_high = swap(back_low, 2), swap(back_high, 4)
    keep, *send = outer_sum(
        thirds_at, thirds, hidden, (eb, eb_x, eb_y, eb_d), (back_y,)
    )
    back_x, back_y = second_sums(back_x, back_y, back_low, back_high, (keep, out_x, out_y))
    send = [swap(behind(piece, back_x), 1) for piece in send]
    (down_grad,) = folded(keep, send, 1, ())
    down_shard = lax.psum_scatter(down_grad, "fsdp", scatter_dimension=0, tiled=True)
    sent_x, sent_y = swap(back_x, 2), swap(back_y, 4)
    chunks_at = jnp.concatenate([2 * t + c for c in (core, 1 - core) for t in range(4)]) * (D // 8)
    keep, *send = outer_sum(chunks_at, (D // 8,) * 4, (a2_x, a2, a2_d, a2_y), (back_gu_a, back_gu_b), (down_grad,))
    wide_back, branch_back, gain_two_grad = middle_back(
        (back_own, sent_x, sent_y), middle, cotangent, live, gains, (keep,)
    )
    send = [swap(behind(piece, sent_x, sent_y, vmem=62), 1) for piece in send]
    (gu_grad,) = folded(keep, send, 1, (branch_back,))
    gu_sum = lax.psum_scatter(gu_grad.reshape(4, D // 8, 2 * width), "fsdp", scatter_dimension=1, tiled=True)

    out_d = swap(behind(out_d, branch_back), 6)
    odd, even = outer_swapped(dp, attended, branch_back, (gu_grad,))
    attended_back = attended_grad(dp, branch_back, out_blocks, (even,))
    low, high, sum_x, sum_y, out_terms = first_sums(even, odd, (attended_back,))
    low, high = swap(low, 2), swap(high, 4)
    projected_back = attend_back(queries, key_rows, value_rows, attended_back, cosine, sine, segment, (sum_x,))
    sum_x, sum_y = second_sums(sum_x, sum_y, low, high, (projected_back,))
    out_terms = (out_terms, swap(sum_x, 2), swap(sum_y, 4))
    odd, even = outer_swapped(dp, low_one, projected_back, (out_d, sum_x))
    low, high, sum_x, sum_y, qkv_terms = first_sums(even, odd, (sum_x,))
    low, high = swap(low, 2), swap(high, 4)
    input_grad, gain_one_grad = input_back(dp, projected_back, qkv_blocks, tokens, gains, wide_back, (sum_x,))
    gain_grads = jnp.stack([gain_one_grad[0], gain_two_grad[0]])
    gain_grads = gain_grads + swap(gain_grads, 1)
    out_mine = total((behind(out_terms[0], input_grad),) + out_terms[1:]).astype(BF16)
    sum_x, sum_y = second_sums(sum_x, sum_y, low, high, (input_grad, out_mine))
    qkv_terms = (qkv_terms, swap(sum_x, 2), swap(sum_y, 4))
    out_mine = behind(out_mine, gu_sum, down_shard, gain_grads, sum_x)
    out_sum = lax.psum_scatter(out_mine, "fsdp", scatter_dimension=0, tiled=True)
    out_shard = out_sum.astype(F32)

    gain_grads = behind(gain_grads, sum_x)
    gain_grads = gain_grads + swap(gain_grads, 2) + swap(gain_grads, 4) + swap(gain_grads, 6)
    gain_mine = lax.dynamic_slice(gain_grads, (0, dp_index * (D // 8)), (2, D // 8)).reshape(2, nf, d_rows)
    gain_mine = gain_mine.transpose(1, 0, 2).reshape(nf, 1, 2 * d_rows).astype(BF16)
    gain_mine = jnp.pad(gain_mine, ((0, 0), (0, d_rows - 1), (0, 128 - 2 * d_rows))).reshape(D // 8, 128)
    qkv_mine = jnp.concatenate([total(qkv_terms).astype(BF16), gain_mine], axis=1)
    qkv_grads = lax.psum_scatter(qkv_mine, "fsdp", scatter_dimension=0, tiled=True)
    attention_state = adam_attention(qkv_grads, w_qkv, m_qkv, v_qkv, norm_gains, m_gains, v_gains)

    down_state = adam_step(
        w_down, m_down, v_down, behind(down_shard, qkv_mine).astype(F32), RATE_MATRIX, DECAY_MATRIX
    )

    gu_sum = behind(gu_sum, qkv_mine, out_sum)
    gate_up_shard = jnp.zeros((d_rows, 2 * FF), BF16)
    for k in range(4):
        there = chip ^ k
        piece = lax.dynamic_slice(gu_sum, (there, 0, 0), (1, d_rows, 2 * width))[0]
        if k:
            piece = swap(piece, 2 * k)
        for h in range(2):
            gate_up_shard = lax.dynamic_update_slice(
                gate_up_shard, piece[:, h * width : (h + 1) * width], (0, (h * 4 + there) * width)
            )

    output = (middle + total((behind(out_own_rows, piece), out_x, out_y, out_d))).astype(BF16)
    gate_up_state = adam_step(
        w_gate_up, m_gate_up, v_gate_up, gate_up_shard.astype(F32), RATE_MATRIX, DECAY_MATRIX
    )

    return (
        output,
        input_grad,
        *attention_state[:3],
        *adam_step(w_out, m_out, v_out, out_shard, RATE_MATRIX, DECAY_MATRIX),
        *gate_up_state,
        *down_state,
        *attention_state[3:],
    )


def solution(mesh):
    body, axes = any_mesh, ("dp", "fsdp")
    if (mesh.shape["dp"], mesh.shape["fsdp"]) == (8, 4):
        body, axes = cube, ("tp", "core", "fsdp")
        mesh = jax.sharding.Mesh(mesh.devices.reshape(4, 2, 4), axes)
    rows, cols = P(axes, None), P(None, axes)
    in_specs = (rows,) * 15 + (cols,) * 3
    out_specs = (rows,) * 14 + (cols,) * 3
    return jax.shard_map(body, mesh=mesh, in_specs=in_specs, out_specs=out_specs, check_vma=False)
```
